32 devices in a mesh: dp: 8 (over z, x), tensor: 4 (over y, core).
Axes of the slice: x: 2, y: 2, z: 4, core: 2. Of those that a mesh axis runs over, the one named last changes fastest.
Arguments:
- tokens: bfloat16 [4096, 768], P('dp'), may hold values from -6 to 6
- segment_ids: int32 [8, 512], P('dp'), may hold values from 0 to 5, never falling along the last dimension, each value on 1 to 256 neighbouring positions
- cotangent: bfloat16 [4096, 768], P('dp'), may hold values from -6 to 6
- w_qkv: float32 [3, 768, 768], P(None, 'dp', 'tensor'), may hold values from -0.21875 to 0.21875
- w_out: float32 [768, 768], P('tensor', 'dp'), may hold values from -1.75 to 1.75
- w_in: float32 [2, 768, 1152], P(None, 'dp', 'tensor'), may hold values from -0.21875 to 0.21875
- w_down: float32 [1152, 768], P('tensor', 'dp'), may hold values from -0.1875 to 0.1875
- gains: float32 [2, 768], P(None, 'dp'), may hold values from 0.5 to 1.5
- first_qkv: float32 [3, 768, 768], P(None, 'dp', 'tensor'), may hold values from -23.04 to 23.04
- first_out: float32 [768, 768], P('tensor', 'dp'), may hold values from -3.84 to 3.84
- first_in: float32 [2, 768, 1152], P(None, 'dp', 'tensor'), may hold values from -23.04 to 23.04
- first_down: float32 [1152, 768], P('tensor', 'dp'), may hold values from -23.04 to 23.04
- first_gains: float32 [2, 768], P(None, 'dp'), may hold values from -23.04 to 23.04
- second_qkv: float32 [3, 768, 768], P(None, 'dp', 'tensor'), may hold values from 409.6 to 1638.4
- second_out: float32 [768, 768], P('tensor', 'dp'), may hold values from 20.48 to 81.92
- second_in: float32 [2, 768, 1152], P(None, 'dp', 'tensor'), may hold values from 81.92 to 327.68
- second_down: float32 [1152, 768], P('tensor', 'dp'), may hold values from 307.2 to 1228.8
- second_gains: float32 [2, 768], P(None, 'dp'), may hold values from 614.4 to 2457.6
Outputs:
- out_tokens: float32 [4096, 768], P('dp')
- grad_tokens: float32 [4096, 768], P('dp')
- grad_qkv: float32 [3, 768, 768], P(None, 'dp', 'tensor')
- grad_out: float32 [768, 768], P('tensor', 'dp')
- grad_in: float32 [2, 768, 1152], P(None, 'dp', 'tensor')
- grad_down: float32 [1152, 768], P('tensor', 'dp')
- grad_gains: float32 [2, 768], P(None, 'dp')
- delta_qkv: float32 [3, 768, 768], P(None, 'dp', 'tensor')
- delta_out: float32 [768, 768], P('tensor', 'dp')
- delta_in: float32 [2, 768, 1152], P(None, 'dp', 'tensor')
- delta_down: float32 [1152, 768], P('tensor', 'dp')
- delta_gains: float32 [2, 768], P(None, 'dp')
- new_first_qkv: float32 [3, 768, 768], P(None, 'dp', 'tensor')
- new_first_out: float32 [768, 768], P('tensor', 'dp')
- new_first_in: float32 [2, 768, 1152], P(None, 'dp', 'tensor')
- new_first_down: float32 [1152, 768], P('tensor', 'dp')
- new_first_gains: float32 [2, 768], P(None, 'dp')
- new_second_qkv: float32 [3, 768, 768], P(None, 'dp', 'tensor')
- new_second_out: float32 [768, 768], P('tensor', 'dp')
- new_second_in: float32 [2, 768, 1152], P(None, 'dp', 'tensor')
- new_second_down: float32 [1152, 768], P('tensor', 'dp')
- new_second_gains: float32 [2, 768], P(None, 'dp')
The draws below stay inside these ranges and needn't reach their ends.
Inputs may be any that keep to these rules, and one draw needn't show every extreme that they name: `segment_ids`: along each of the 8 sequences the ids never fall; each document holds 1 to 256 tokens, and one holds exactly 256.
All inputs are finite; a program needn't handle non-finite values.
Results may differ from the reference program's by a relative error of at most 0.018.
Values may be sent and summed in bfloat16 or wider, within the bound.
No kernel may reach another device: no remote copies, remote signals or barrier semaphores. Data moves between devices by JAX's collectives and lax.ppermute only.
A program may use at most 128 MiB of HBM per device.

```python
import math
import jax
import jax.numpy as jnp
import numpy as np
from jax import lax

D = 768
HEAD_DIM = 64
FF = 1152
LEN = 512
STEP = 3
SEQS = 8
TOKENS = 4096


def draw_tokens(key, part):
    noise_key = jax.random.fold_in(key, 11)
    values = jnp.clip(jax.random.normal(noise_key, (TOKENS, D), jnp.float32), -6.0, 6.0)
    return values.astype(jnp.bfloat16)


def shard_levels(rng, shape, cuts, low, top_value):
    def one(axis_at, blocks):
        steps = jax.random.uniform(jax.random.fold_in(jax.random.fold_in(rng, 6), axis_at), (blocks,), jnp.float32, low / len(cuts), top_value / len(cuts))
        return jnp.repeat(jnp.exp(steps), shape[axis_at] // blocks).reshape((-1,) + (1,) * (len(shape) - axis_at - 1))

    factor_of = one(*cuts[0])
    for cut in cuts[1:]:
        factor_of = factor_of * one(*cut)
    return factor_of


def profile(count, total, limit, skew):
    portions = [(1 << 20) // math.isqrt(standing ** skew) + 1 for standing in range(2, count + 1)]
    surplus, holding = total - limit - (count - 1), [1] * (count - 1)
    while surplus > 0:
        candidates = [i for i in range(count - 1) if holding[i] < limit]
        mass, budget = sum([portions[i] for i in candidates]), surplus
        for i in candidates:
            extra = min(limit - holding[i], max(1, budget * portions[i] // mass), surplus)
            holding[i] = holding[i] + extra
            surplus = surplus - extra
    return np.array([limit] + holding)


def uneven_parts(key, number_of, total, limit, lean):
    if number_of == 2:
        one = jax.random.randint(key, (), max(1, total - limit), min(limit, total - 1) + 1)
        return jnp.stack([one, total - one])
    tallies = jnp.asarray(profile(number_of, total, limit, lean), jnp.int32)
    pairs = (number_of - 1) // 2
    source_of, receiver = tallies[1:1 + 2 * pairs:2], tallies[2:2 + 2 * pairs:2]
    room = jnp.minimum(source_of - 1, limit - receiver)
    shifted = jax.random.randint(jax.random.fold_in(key, 1), (pairs,), 0, 1 << 20) % (room + 1)
    tallies = tallies.at[1:1 + 2 * pairs:2].set(source_of - shifted).at[2:2 + 2 * pairs:2].set(receiver + shifted)
    return tallies[jax.random.permutation(jax.random.fold_in(key, 2), number_of)]


def bell_draw(own_key, shape, spread, most, shards=(), kind=jnp.bfloat16):
    array = spread * jax.random.normal(own_key, shape, jnp.float32)
    if shards:
        array = array * shard_levels(own_key, shape, shards, -0.22, 0.18)
    return jnp.clip(array, -most, most).astype(kind)


def setup_inputs(seed: int = 0) -> dict:
    key_of = jax.random.split(jax.random.key(seed), 19)
    tokens = draw_tokens(jax.random.fold_in(key_of[18], 71), 0)
    segment_ids = jax.vmap(lambda own: jnp.searchsorted(jnp.cumsum(uneven_parts(own, 6, LEN, LEN // 2, 0)), jnp.arange(LEN), side="right"))(jax.random.split(key_of[1], SEQS)).reshape((SEQS, LEN)).astype(jnp.int32)
    cotangent = bell_draw(key_of[2], (TOKENS, D), 1.0, 6.0, ((0, 8),))
    w_qkv = bell_draw(key_of[3], (3, D, D), D ** -0.5, 0.21875, ((1, 8), (2, 4)), jnp.float32)
    w_out = bell_draw(key_of[4], (D, D), (D // 64) ** -0.5, 1.75, ((0, 4), (1, 8)), jnp.float32)
    w_in = bell_draw(key_of[5], (2, D, FF), D ** -0.5, 0.21875, ((1, 8), (2, 4)), jnp.float32)
    w_down = bell_draw(key_of[6], (FF, D), FF ** -0.5, 0.1875, ((0, 4), (1, 8)), jnp.float32)
    gains = jnp.clip(1.0 + 0.1 * jax.random.normal(key_of[7], (2, D), jnp.float32), 0.5, 1.5)
    first_qkv = bell_draw(key_of[8], (3, D, D), (0.06 * TOKENS ** 0.5), 23.04, ((1, 8), (2, 4)), jnp.float32)
    first_out = bell_draw(key_of[9], (D, D), (0.01 * TOKENS ** 0.5), 3.84, ((0, 4), (1, 8)), jnp.float32)
    first_in = bell_draw(key_of[10], (2, D, FF), (0.06 * TOKENS ** 0.5), 23.04, ((1, 8), (2, 4)), jnp.float32)
    first_down = bell_draw(key_of[11], (FF, D), (0.06 * TOKENS ** 0.5), 23.04, ((0, 4), (1, 8)), jnp.float32)
    first_gains = bell_draw(key_of[12], (2, D), (0.06 * TOKENS ** 0.5), 23.04, ((1, 8),), jnp.float32)
    second_qkv = jnp.clip(jnp.exp(math.log(1638.4) - 1.3862944 * jax.random.uniform(key_of[13], (3, D, D), jnp.float32) ** shard_levels(key_of[13], (3, D, D), ((1, 8), (2, 4)), -0.2, 0.2)), 409.6, 1638.4)
    second_out = jnp.clip(jnp.exp(math.log(81.92) - 1.3862944 * jax.random.uniform(key_of[14], (D, D), jnp.float32) ** shard_levels(key_of[14], (D, D), ((0, 4), (1, 8)), -0.2, 0.2)), 20.48, 81.92)
    second_in = jnp.clip(jnp.exp(math.log(327.68) - 1.3862944 * jax.random.uniform(key_of[15], (2, D, FF), jnp.float32) ** shard_levels(key_of[15], (2, D, FF), ((1, 8), (2, 4)), -0.2, 0.2)), 81.92, 327.68)
    second_down = jnp.clip(jnp.exp(math.log(1228.8) - 1.3862944 * jax.random.uniform(key_of[16], (FF, D), jnp.float32) ** shard_levels(key_of[16], (FF, D), ((0, 4), (1, 8)), -0.2, 0.2)), 307.2, 1228.8)
    second_gains = jnp.clip(jnp.exp(math.log(2457.6) - 1.3862944 * jax.random.uniform(key_of[17], (2, D), jnp.float32) ** shard_levels(key_of[17], (2, D), ((1, 8),), -0.2, 0.2)), 614.4, 2457.6)
    return {"tokens": tokens, "segment_ids": segment_ids, "cotangent": cotangent, "w_qkv": w_qkv, "w_out": w_out, "w_in": w_in, "w_down": w_down, "gains": gains, "first_qkv": first_qkv, "first_out": first_out, "first_in": first_in, "first_down": first_down, "first_gains": first_gains, "second_qkv": second_qkv, "second_out": second_out, "second_in": second_in, "second_down": second_down, "second_gains": second_gains}


norm_eps = 1e-05
rope_base = 160000.0
learn_rate = 0.01
beta_one = 0.9
beta_two = 0.98
adam_eps = 1e-08
decay_rate = 0.01
big_negative = -1e+30

def rounded(values):
    return lax.optimization_barrier(values.astype(jnp.bfloat16)).astype(jnp.float32)

def rope_tables(count, head_width):
    half_dim = head_width // 2
    frequency = rope_base ** (-(jnp.arange(half_dim, dtype=jnp.float32) * 2.0 / head_width))
    angles = jnp.arange(count, dtype=jnp.float32)[:, None] * frequency[None, :]
    cosine_table = jnp.concatenate([jnp.cos(angles), jnp.cos(angles)], axis=1)
    sine_values = jnp.concatenate([jnp.sin(angles), jnp.sin(angles)], axis=1)
    return (cosine_table, sine_values)

def rotate_fwd(values, cosine_table, sine_values):
    half_dim = values.shape[-1] // 2
    turned = jnp.concatenate([-values[..., half_dim:], values[..., :half_dim]], axis=-1)
    return values * cosine_table + turned * sine_values

def inverse_rotation(gradient, cosine_table, sine_values):
    half_dim = gradient.shape[-1] // 2
    scaled = gradient * sine_values
    turned = jnp.concatenate([scaled[..., half_dim:], -scaled[..., :half_dim]], axis=-1)
    return gradient * cosine_table + turned

def gelu_parts(inputs):
    normal_cdf = 0.5 * (1.0 + lax.erf(inputs * 0.7071067811865476))
    density = jnp.exp(-0.5 * inputs * inputs) * 0.3989422804014327
    return (inputs * normal_cdf, normal_cdf + inputs * density)

def norm_fwd(values, gain_vec):
    center = values - lax.optimization_barrier(jnp.mean(values, axis=-1, keepdims=True))
    inverse = lax.rsqrt(lax.optimization_barrier(jnp.mean(center * center, axis=-1, keepdims=True)) + norm_eps)
    normed = center * inverse
    return (normed * gain_vec, normed, inverse)

def norm_back(grad_norm, gain_vec, normed, inverse):
    scaled = grad_norm * gain_vec
    grad_input = (scaled - lax.optimization_barrier(jnp.mean(scaled, axis=-1, keepdims=True)) - normed * lax.optimization_barrier(jnp.mean(scaled * normed, axis=-1, keepdims=True))) * inverse
    grad_gain = lax.optimization_barrier(jnp.sum(grad_norm * normed, axis=0))
    return (grad_input, grad_gain)

def sequence_pass(params, inputs):
    w_qkv, w_out, w_in, w_down, gain_one, gain_two = params
    tokens, segments, cotangent = inputs
    length = tokens.shape[0]
    head_count = w_qkv.shape[2] // HEAD_DIM
    logit_scale = HEAD_DIM ** (-0.5)
    cosine_table, sine_values = rope_tables(length, HEAD_DIM)
    stream = tokens.astype(jnp.float32)
    normed_one, hat_one, inv_one = norm_fwd(stream, gain_one)
    in_one = normed_one.astype(jnp.bfloat16)
    projected = jnp.einsum('ld,sde->sle', in_one.astype(jnp.float32), w_qkv.astype(jnp.float32))
    split_heads = projected.reshape(3, length, head_count, HEAD_DIM).transpose(0, 2, 1, 3)
    query_per_head = rotate_fwd(split_heads[0], cosine_table, sine_values).astype(jnp.bfloat16)
    key_per_head = rotate_fwd(split_heads[1], cosine_table, sine_values).astype(jnp.bfloat16)
    value_per_head = split_heads[2].astype(jnp.bfloat16)
    allowed = (segments[:, None] == segments[None, :])[None]
    attention_logits = jnp.einsum('sjr,szr->sjz', query_per_head.astype(jnp.float32), key_per_head.astype(jnp.float32)) * logit_scale
    attention_logits = jnp.where(allowed, attention_logits, big_negative)
    row_top = lax.optimization_barrier(jnp.max(attention_logits, axis=-1, keepdims=True))
    expd = jnp.exp(attention_logits - row_top)
    row_total = lax.optimization_barrier(jnp.sum(expd, axis=-1, keepdims=True))
    soft_weights = expd / row_total
    softmax_probs_narrow = soft_weights.astype(jnp.bfloat16)
    attended_values = jnp.einsum('sur,srk->suk', softmax_probs_narrow.astype(jnp.float32), value_per_head.astype(jnp.float32)).astype(jnp.bfloat16)
    merged = attended_values.transpose(1, 0, 2).reshape(length, head_count * HEAD_DIM)
    middle = stream + jnp.dot(merged, w_out, preferred_element_type=jnp.float32)
    normed_two, hat_two, inv_two = norm_fwd(middle, gain_two)
    in_two = normed_two.astype(jnp.bfloat16)
    lifted = jnp.einsum('ld,sdf->slf', in_two.astype(jnp.float32), w_in.astype(jnp.float32))
    gelu_val, gelu_slope = gelu_parts(lifted[0])
    hidden = (gelu_val * lifted[1]).astype(jnp.bfloat16)
    output = middle + jnp.dot(hidden, w_down, preferred_element_type=jnp.float32)
    grad_stream = cotangent.astype(jnp.float32)
    grad_down = jnp.einsum('lf,ld->fd', hidden.astype(jnp.float32), grad_stream)
    grad_hidden = jnp.einsum('ld,fd->lf', grad_stream, w_down.astype(jnp.float32))
    grad_up = jnp.stack([grad_hidden * lifted[1] * gelu_slope, grad_hidden * gelu_val]).astype(jnp.bfloat16)
    grad_in = jnp.einsum('ld,slf->sdf', in_two.astype(jnp.float32), grad_up.astype(jnp.float32))
    grad_two = jnp.einsum('slf,sdf->ld', grad_up.astype(jnp.float32), w_in.astype(jnp.float32))
    back_two, grad_gain_two = norm_back(grad_two, gain_two, hat_two, inv_two)
    grad_middle = grad_stream + back_two
    middle_low = grad_middle.astype(jnp.bfloat16)
    grad_out = jnp.einsum('le,ld->ed', merged.astype(jnp.float32), middle_low.astype(jnp.float32))
    grad_merged = jnp.einsum('ld,ed->le', middle_low.astype(jnp.float32), w_out.astype(jnp.float32)).astype(jnp.bfloat16)
    attended_gradient = grad_merged.reshape(length, head_count, HEAD_DIM).transpose(1, 0, 2).astype(jnp.float32)
    value_gradient = jnp.einsum('xuy,xup->xyp', softmax_probs_narrow.astype(jnp.float32), attended_gradient)
    softmax_gradient = jnp.einsum('sjr,szr->sjz', attended_gradient, value_per_head.astype(jnp.float32))
    delta_rows = lax.optimization_barrier(jnp.sum(attended_gradient * attended_values.astype(jnp.float32), axis=-1, keepdims=True))
    score_gradient = (soft_weights * (softmax_gradient - delta_rows) * logit_scale).astype(jnp.bfloat16).astype(jnp.float32)
    query_gradient = inverse_rotation(jnp.einsum('sur,srk->suk', score_gradient, key_per_head.astype(jnp.float32)), cosine_table, sine_values)
    key_gradient = inverse_rotation(jnp.einsum('xuy,xup->xyp', score_gradient, query_per_head.astype(jnp.float32)), cosine_table, sine_values)
    grad_proj = jnp.stack([query_gradient, key_gradient, value_gradient]).astype(jnp.bfloat16)
    grad_proj = grad_proj.transpose(0, 2, 1, 3).reshape(3, length, head_count * HEAD_DIM).astype(jnp.float32)
    grad_qkv = jnp.einsum('ld,sle->sde', in_one.astype(jnp.float32), grad_proj)
    grad_one = jnp.einsum('sle,sde->ld', grad_proj, w_qkv.astype(jnp.float32))
    back_one, grad_gain_one = norm_back(grad_one, gain_one, hat_one, inv_one)
    grad_tokens = grad_middle + back_one
    return ((output, grad_tokens), (grad_qkv, grad_out, grad_in, grad_down, grad_gain_one, grad_gain_two))

def adamw(weight, gradient, first_mom, second, decay_now):
    first_new = beta_one * first_mom + (1.0 - beta_one) * gradient
    second_new = beta_two * second + (1.0 - beta_two) * gradient * gradient
    corr_one = 1.0 - beta_one ** STEP
    corr_two = 1.0 - beta_two ** STEP
    update = first_new / corr_one / (jnp.sqrt(second_new / corr_two) + adam_eps) + decay_now * weight
    return (-learn_rate * update, first_new, second_new)

def reference(tokens, segment_ids, cotangent, w_qkv, w_out, w_in, w_down, gains, first_qkv, first_out, first_in, first_down, first_gains, second_qkv, second_out, second_in, second_down, second_gains):
    params = (w_qkv.astype(jnp.bfloat16), w_out.astype(jnp.bfloat16), w_in.astype(jnp.bfloat16), w_down.astype(jnp.bfloat16), rounded(gains[0]), rounded(gains[1]))
    seq_count = segment_ids.shape[0]
    length = segment_ids.shape[1]
    stacked = (tokens.reshape(seq_count, length, -1), segment_ids, cotangent.reshape(seq_count, length, -1))
    start = (jnp.zeros(w_qkv.shape, jnp.float32), jnp.zeros(w_out.shape, jnp.float32), jnp.zeros(w_in.shape, jnp.float32), jnp.zeros(w_down.shape, jnp.float32), jnp.zeros(gains.shape[1:], jnp.float32), jnp.zeros(gains.shape[1:], jnp.float32))

    def step_fn(running, inputs):
        results, gradients = sequence_pass(params, inputs)
        return (jax.tree.map(jnp.add, running, gradients), results)
    sums, (outputs, grad_rows) = lax.scan(step_fn, start, stacked)
    g_qkv, g_out, g_in, g_down, g_one, g_two = sums
    g_gains = jnp.stack([g_one, g_two])
    n_qkv, m_qkv, s_qkv = adamw(w_qkv, g_qkv, first_qkv, second_qkv, decay_rate)
    n_out, m_out, s_out = adamw(w_out, g_out, first_out, second_out, decay_rate)
    n_in, m_in, s_in = adamw(w_in, g_in, first_in, second_in, decay_rate)
    n_down, m_down, s_down = adamw(w_down, g_down, first_down, second_down, decay_rate)
    n_gains, m_gains, s_gains = adamw(gains, g_gains, first_gains, second_gains, 0.0)
    return (outputs.reshape(tokens.shape), grad_rows.reshape(tokens.shape), g_qkv, g_out, g_in, g_down, g_gains, n_qkv, n_out, n_in, n_down, n_gains, m_qkv, m_out, m_in, m_down, m_gains, s_qkv, s_out, s_in, s_down, s_gains)
```

```python
import jax
import jax.numpy as jnp
from jax import lax
from jax.sharding import PartitionSpec as P

HEAD_DIM = 64
STEP = 3


norm_eps = 1e-05
rope_base = 160000.0
learn_rate = 0.01
beta_one = 0.9
beta_two = 0.98
adam_eps = 1e-08
decay_rate = 0.01
big_negative = -1e30

BF = jnp.bfloat16
F32 = jnp.float32


def rope_tables(count, head_width):
    half_dim = head_width // 2
    frequency = rope_base ** (-(jnp.arange(half_dim, dtype=jnp.float32) * 2.0 / head_width))
    angles = jnp.arange(count, dtype=jnp.float32)[:, None] * frequency[None, :]
    cosine_table = jnp.concatenate([jnp.cos(angles), jnp.cos(angles)], axis=1)
    sine_values = jnp.concatenate([jnp.sin(angles), jnp.sin(angles)], axis=1)
    return (cosine_table, sine_values)


def rotate_fwd(values, cosine_table, sine_values):
    half_dim = values.shape[-1] // 2
    turned = jnp.concatenate([-values[..., half_dim:], values[..., :half_dim]], axis=-1)
    return values * cosine_table + turned * sine_values


def inverse_rotation(gradient, cosine_table, sine_values):
    half_dim = gradient.shape[-1] // 2
    scaled = gradient * sine_values
    turned = jnp.concatenate([scaled[..., half_dim:], -scaled[..., :half_dim]], axis=-1)
    return gradient * cosine_table + turned


def gelu_parts(inputs):
    normal_cdf = 0.5 * (1.0 + lax.erf(inputs * 0.7071067811865476))
    density = jnp.exp(-0.5 * inputs * inputs) * 0.3989422804014327
    return (inputs * normal_cdf, normal_cdf + inputs * density)


def norm_fwd(values, gain_vec):
    center = values - jnp.mean(values, axis=-1, keepdims=True)
    inverse = lax.rsqrt(jnp.mean(center * center, axis=-1, keepdims=True) + norm_eps)
    normed = center * inverse
    return (normed * gain_vec, normed, inverse)


def norm_back(grad_norm, gain_vec, normed, inverse):
    scaled = grad_norm * gain_vec
    return (
        scaled
        - jnp.mean(scaled, axis=-1, keepdims=True)
        - normed * jnp.mean(scaled * normed, axis=-1, keepdims=True)
    ) * inverse


def adamw(weight, gradient, first_mom, second, decay_now):
    first_new = beta_one * first_mom + (1.0 - beta_one) * gradient
    second_new = beta_two * second + (1.0 - beta_two) * gradient * gradient
    corr_one = 1.0 - beta_one**STEP
    corr_two = 1.0 - beta_two**STEP
    update = (
        first_new / corr_one / (jnp.sqrt(second_new / corr_two) + adam_eps) + decay_now * weight
    )
    return (-learn_rate * update, first_new, second_new)


def swap(values, axis, mask):
    count = lax.axis_size(axis)
    return lax.ppermute(values, axis, [(i, i ^ mask) for i in range(count)])


def place_blocks(pieces, masks, index):
    out = jnp.zeros((len(pieces),) + pieces[0].shape, pieces[0].dtype)
    for piece, mask in zip(pieces, masks):
        out = lax.dynamic_update_slice(out, piece[None], (index ^ mask, 0, 0))
    return out


def gather_direct(shard):
    count = lax.axis_size("dp")
    if count != 8:
        return lax.all_gather(shard, "dp", axis=0, tiled=True)
    index = lax.axis_index("dp")
    order = (1, 2, 4, 3, 6, 5, 7)
    pieces = [shard] + [swap(shard, "dp", m) for m in order]
    out = place_blocks(pieces, (0,) + order, index)
    return out.reshape(count * shard.shape[0], shard.shape[1])


def gather_two_level(shard):
    count = lax.axis_size("dp")
    if count != 8:
        return lax.all_gather(shard, "dp", axis=0, tiled=True)
    index = lax.axis_index("dp")
    order = (2, 4, 6)
    pieces = [shard] + [swap(shard, "dp", m) for m in order]
    column = place_blocks(pieces, (0, 1, 2, 3), index // 2)
    other = swap(column, "dp", 1)
    odd = index % 2
    low = jnp.where(odd == 0, column, other)
    high = jnp.where(odd == 0, other, column)
    return jnp.stack([low, high], axis=1).reshape(count * shard.shape[0], shard.shape[1])


def scatter_two_level(grad):
    count = lax.axis_size("dp")
    if count != 8:
        return lax.psum_scatter(grad.astype(F32), "dp", scatter_dimension=0, tiled=True)
    index = lax.axis_index("dp")
    odd, level = index % 2, index // 2
    rows = grad.shape[0] // count
    blocks = grad.reshape(count // 2, 2, rows, grad.shape[1])
    keep = lax.dynamic_index_in_dim(blocks, odd, 1, keepdims=False)
    send = lax.dynamic_index_in_dim(blocks, 1 - odd, 1, keepdims=False)
    pair = (keep.astype(F32) + swap(send, "dp", 1).astype(F32)).astype(BF)
    total = lax.dynamic_index_in_dim(pair, level, 0, keepdims=False).astype(F32)
    for m in (1, 2, 3):
        part = lax.dynamic_index_in_dim(pair, level ^ m, 0, keepdims=False)
        total = total + swap(part, "dp", 2 * m).astype(F32)
    return total


def reduce_tensor(part):
    count = lax.axis_size("tensor")
    if count != 4:
        return lax.psum(part.astype(F32), "tensor")
    half = part.shape[0] // 2
    core = lax.axis_index("tensor") % 2
    low = part.astype(BF)
    mine = lax.dynamic_slice_in_dim(low, core * half, half, 0)
    theirs = lax.dynamic_slice_in_dim(low, (1 - core) * half, half, 0)
    chip = (mine.astype(F32) + swap(theirs, "tensor", 1).astype(F32)).astype(BF)
    total = chip.astype(F32) + swap(chip, "tensor", 2).astype(F32)
    other = swap(total, "tensor", 1)
    return jnp.where(
        core == 0,
        jnp.concatenate([total, other], axis=0),
        jnp.concatenate([other, total], axis=0),
    )


def local(
    tokens,
    segment_ids,
    cotangent,
    w_qkv,
    w_out,
    w_in,
    w_down,
    gains,
    first_qkv,
    first_out,
    first_in,
    first_down,
    first_gains,
    second_qkv,
    second_out,
    second_in,
    second_down,
    second_gains,
):
    head_total = w_qkv.shape[2]
    hidden_total = w_in.shape[2]
    shard_a = jnp.concatenate(
        [w_qkv[0], w_qkv[1], w_qkv[2], gains[0][:, None]], axis=1
    ).astype(BF)
    shard_b = jnp.concatenate(
        [w_in[0], w_in[1], w_out.T, w_down.T, gains[1][:, None]], axis=1
    ).astype(BF)
    full_a = gather_direct(shard_a)
    full_b = gather_two_level(shard_b)
    wide = 3 * head_total
    full_qkv = full_a[:, :wide]
    gain_one = full_a[:, wide].astype(F32)
    full_in = full_b[:, : 2 * hidden_total]
    at = 2 * hidden_total
    full_out = full_b[:, at : at + head_total]
    at = at + head_total
    full_down = full_b[:, at : at + hidden_total]
    at = at + hidden_total
    gain_two = full_b[:, at].astype(F32)

    segments = segment_ids[0]
    length = tokens.shape[0]
    head_count = head_total // HEAD_DIM
    logit_scale = HEAD_DIM ** (-0.5)
    cosine_table, sine_values = rope_tables(length, HEAD_DIM)
    allowed = (segments[:, None] == segments[None, :])[None]
    stream = tokens.astype(F32)
    normed_one, hat_one, inv_one = norm_fwd(stream, gain_one)
    in_one = normed_one.astype(BF)
    projected = jnp.dot(in_one, full_qkv, preferred_element_type=F32)
    split_heads = projected.reshape(length, 3, head_count, HEAD_DIM).transpose(1, 2, 0, 3)
    query_per_head = rotate_fwd(split_heads[0], cosine_table, sine_values).astype(BF)
    key_per_head = rotate_fwd(split_heads[1], cosine_table, sine_values).astype(BF)
    value_per_head = split_heads[2].astype(BF)
    attention_logits = (
        jnp.einsum("sjr,szr->sjz", query_per_head, key_per_head, preferred_element_type=F32)
        * logit_scale
    )
    attention_logits = jnp.where(allowed, attention_logits, big_negative)
    row_top = jnp.max(attention_logits, axis=-1, keepdims=True)
    expd = jnp.exp(attention_logits - row_top)
    row_total = jnp.sum(expd, axis=-1, keepdims=True)
    log_total = row_top + jnp.log(row_total)
    softmax_probs_narrow = (expd / row_total).astype(BF)
    attended_values = jnp.einsum(
        "sur,srk->suk", softmax_probs_narrow, value_per_head, preferred_element_type=F32
    ).astype(BF)
    merged = attended_values.transpose(1, 0, 2).reshape(length, head_total)
    attn_part = jnp.einsum("le,de->ld", merged, full_out, preferred_element_type=F32)
    middle = stream + reduce_tensor(attn_part)
    normed_two, hat_two, inv_two = norm_fwd(middle, gain_two)
    in_two = normed_two.astype(BF)
    lifted = jnp.dot(in_two, full_in, preferred_element_type=F32)
    lift_up, lift_gate = lifted[:, :hidden_total], lifted[:, hidden_total:]
    gelu_val, gelu_slope = gelu_parts(lift_up)
    hidden = (gelu_val * lift_gate).astype(BF)
    grad_hidden = jnp.dot(cotangent, full_down, preferred_element_type=F32)
    grad_up = jnp.concatenate(
        [grad_hidden * lift_gate * gelu_slope, grad_hidden * gelu_val], axis=1
    ).astype(BF)
    two_part = jnp.einsum("lf,df->ld", grad_up, full_in, preferred_element_type=F32)
    grad_two = reduce_tensor(two_part)
    mlp_part = jnp.einsum("lf,df->ld", hidden, full_down, preferred_element_type=F32)
    output = middle + reduce_tensor(mlp_part)
    grad_ffn = jnp.concatenate(
        [
            jnp.einsum("ld,lf->df", in_two, grad_up, preferred_element_type=F32),
            jnp.einsum("ld,lf->df", cotangent, hidden, preferred_element_type=F32),
            jnp.sum(two_part * hat_two, axis=0)[:, None],
        ],
        axis=1,
    ).astype(BF)
    share_ffn = scatter_two_level(grad_ffn)

    grad_middle = cotangent.astype(F32) + norm_back(grad_two, gain_two, hat_two, inv_two)
    middle_low = grad_middle.astype(BF)
    grad_out = jnp.einsum("ld,le->de", middle_low, merged, preferred_element_type=F32)
    grad_merged = jnp.dot(middle_low, full_out, preferred_element_type=F32).astype(BF)
    attended_gradient = grad_merged.reshape(length, head_count, HEAD_DIM).transpose(1, 0, 2)
    again = (
        jnp.einsum("sjr,szr->sjz", query_per_head, key_per_head, preferred_element_type=F32)
        * logit_scale
    )
    again = jnp.where(allowed, again, big_negative)
    soft_again = jnp.exp(again - log_total)
    value_gradient = jnp.einsum(
        "xuy,xup->xyp", softmax_probs_narrow, attended_gradient, preferred_element_type=F32
    )
    softmax_gradient = jnp.einsum(
        "sjr,szr->sjz", attended_gradient, value_per_head, preferred_element_type=F32
    )
    delta_rows = jnp.sum(
        attended_gradient.astype(F32) * attended_values.astype(F32),
        axis=-1,
        keepdims=True,
    )
    score_gradient = (soft_again * (softmax_gradient - delta_rows) * logit_scale).astype(BF)
    query_gradient = inverse_rotation(
        jnp.einsum("sur,srk->suk", score_gradient, key_per_head, preferred_element_type=F32),
        cosine_table,
        sine_values,
    )
    key_gradient = inverse_rotation(
        jnp.einsum("xuy,xup->xyp", score_gradient, query_per_head, preferred_element_type=F32),
        cosine_table,
        sine_values,
    )
    grad_proj = jnp.stack([query_gradient, key_gradient, value_gradient]).astype(BF)
    grad_proj = grad_proj.transpose(2, 0, 1, 3).reshape(length, wide)
    one_part = jnp.einsum("le,de->ld", grad_proj, full_qkv, preferred_element_type=F32)
    grad_attn = jnp.concatenate(
        [
            jnp.einsum("ld,le->de", in_one, grad_proj, preferred_element_type=F32),
            grad_out,
            jnp.sum(one_part * hat_one, axis=0)[:, None],
        ],
        axis=1,
    ).astype(BF)
    share_attn = scatter_two_level(grad_attn)
    grad_one = reduce_tensor(one_part)
    grad_tokens = grad_middle + norm_back(grad_one, gain_one, hat_one, inv_one)

    share_qkv = jnp.stack([share_attn[:, i * head_total : (i + 1) * head_total] for i in range(3)])
    share_out = share_attn[:, wide : wide + head_total].T
    share_in = jnp.stack([share_ffn[:, i * hidden_total : (i + 1) * hidden_total] for i in range(2)])
    share_down = share_ffn[:, 2 * hidden_total : 3 * hidden_total].T
    share_gains = jnp.stack([share_attn[:, wide + head_total], share_ffn[:, 3 * hidden_total]])
    if lax.axis_size("tensor") == 4:
        share_gains = share_gains + swap(share_gains, "tensor", 1)
        share_gains = share_gains + swap(share_gains, "tensor", 2)
    else:
        share_gains = lax.psum(share_gains, "tensor")
    n_qkv, m_qkv, s_qkv = adamw(w_qkv, share_qkv, first_qkv, second_qkv, decay_rate)
    n_out, m_out, s_out = adamw(w_out, share_out, first_out, second_out, decay_rate)
    n_in, m_in, s_in = adamw(w_in, share_in, first_in, second_in, decay_rate)
    n_down, m_down, s_down = adamw(w_down, share_down, first_down, second_down, decay_rate)
    n_gains, m_gains, s_gains = adamw(gains, share_gains, first_gains, second_gains, 0.0)
    return (
        output,
        grad_tokens,
        share_qkv,
        share_out,
        share_in,
        share_down,
        share_gains,
        n_qkv,
        n_out,
        n_in,
        n_down,
        n_gains,
        m_qkv,
        m_out,
        m_in,
        m_down,
        m_gains,
        s_qkv,
        s_out,
        s_in,
        s_down,
        s_gains,
    )


def solution(mesh):
    placed = (
        P("dp", None),
        P("dp", None),
        P("dp", None),
        P(None, "dp", "tensor"),
        P("tensor", "dp"),
        P(None, "dp", "tensor"),
        P("tensor", "dp"),
        P(None, "dp"),
        P(None, "dp", "tensor"),
        P("tensor", "dp"),
        P(None, "dp", "tensor"),
        P("tensor", "dp"),
        P(None, "dp"),
        P(None, "dp", "tensor"),
        P("tensor", "dp"),
        P(None, "dp", "tensor"),
        P("tensor", "dp"),
        P(None, "dp"),
    )
    return jax.shard_map(
        local,
        mesh=mesh,
        in_specs=placed,
        out_specs=(
            P("dp", None),
            P("dp", None),
            P(None, "dp", "tensor"),
            P("tensor", "dp"),
            P(None, "dp", "tensor"),
            P("tensor", "dp"),
            P(None, "dp"),
            P(None, "dp", "tensor"),
            P("tensor", "dp"),
            P(None, "dp", "tensor"),
            P("tensor", "dp"),
            P(None, "dp"),
            P(None, "dp", "tensor"),
            P("tensor", "dp"),
            P(None, "dp", "tensor"),
            P("tensor", "dp"),
            P(None, "dp"),
            P(None, "dp", "tensor"),
            P("tensor", "dp"),
            P(None, "dp", "tensor"),
            P("tensor", "dp"),
            P(None, "dp"),
        ),
        check_vma=False,
    )
```

```python
import jax
import jax.numpy as jnp
from jax import lax
from jax.experimental import pallas as pl
from jax.experimental.pallas import tpu as pltpu
from jax.sharding import PartitionSpec as P

HEAD_DIM = 64
STEP = 3


norm_eps = 1e-05
rope_base = 160000.0
learn_rate = 0.01
beta_one = 0.9
beta_two = 0.98
adam_eps = 1e-08
decay_rate = 0.01
big_negative = -1e30

BF = jnp.bfloat16
F32 = jnp.float32


def rope_tables(count, width, deps):
    half_dim = HEAD_DIM // 2
    spot = (jnp.arange(width) % half_dim).astype(jnp.float32)
    frequency = rope_base ** (-(spot * 2.0 / HEAD_DIM))
    place = gate(jnp.arange(count, dtype=jnp.float32)[:, None], deps)
    angles = place * frequency[None, :]
    return (jnp.cos(angles), jnp.sin(angles))


def gelu_parts(inputs):
    normal_cdf = 0.5 * (1.0 + lax.erf(inputs * 0.7071067811865476))
    density = jnp.exp(-0.5 * inputs * inputs) * 0.3989422804014327
    return (inputs * normal_cdf, normal_cdf + inputs * density)


def adamw(weight, gradient, first_mom, second, decay_now):
    first_new = beta_one * first_mom + (1.0 - beta_one) * gradient
    second_new = beta_two * second + (1.0 - beta_two) * gradient * gradient
    corr_one = 1.0 - beta_one**STEP
    corr_two = 1.0 - beta_two**STEP
    update = (
        first_new / corr_one / (jnp.sqrt(second_new / corr_two) + adam_eps) + decay_now * weight
    )
    return (-learn_rate * update, first_new, second_new)


def swap(values, axis, mask):
    count = lax.axis_size(axis)
    return lax.ppermute(values, axis, [(i, i ^ mask) for i in range(count)])


def pack(first, second, gains, row, deps=()):
    rows = first.shape[1]
    used = first.shape[0] * first.shape[2] + second.shape[0] + 1
    width = -(-used // 128) * 128
    return stream(
        lambda *refs: pack_kernel(row, *refs), [((rows, width), BF)], [first, second, gains], smem=0, deps=deps, vmem=16
    )[0]


def gather_pieces(pack_a, pack_b):
    if lax.axis_size("dp") != 8:
        full_a = lax.all_gather(pack_a(()), "dp", axis=0, tiled=True)
        full_b = lax.all_gather(pack_b(()), "dp", axis=0, tiled=True)
        return [full_a], None, [full_b], None, []
    order = (4, 6, 2)
    shard_a, shard_b = pack_a(()), pack_b(())
    far_one, far_two, near = [swap(shard_a, "dp", m) for m in order]
    sides = [swap(piece, "dp", 1) for piece in (shard_a, near, far_one)]
    sides.append(swap(gate(far_two, sides[1:]), "dp", 1))
    pieces_a = [shard_a, near, far_one, far_two] + sides
    masks_a = [[m] for m in (0, 2, 4, 6, 1, 3, 5, 7)]
    shard_b = gate(shard_b, [far_one, far_two])
    column = [swap(shard_b, "dp", m) for m in order]
    side = swap(shard_b, "dp", 1)
    stacked = stack(column)
    pieces_b = [shard_b, stacked, side, swap(stacked, "dp", 1)]
    return pieces_a, masks_a, pieces_b, [[0], [4, 6, 2], [1], [5, 7, 3]], column + [side]


def pair_kernel(where_ref, keep_ref, got_ref, own_ref, *far_refs):
    level = where_ref[0] >> 1
    for m, ref in enumerate((own_ref,) + far_refs):
        at = level ^ m
        ref[...] = (keep_ref[at].astype(F32) + got_ref[at].astype(F32)).astype(BF)


def scatter_start(where, grads, deps=()):
    if len(grads) == 1:
        return [lax.psum_scatter(grads[0].astype(F32), "dp", scatter_dimension=0, tiled=True)], []
    keep, send = grads
    got = swap(gate(send, deps) if deps else send, "dp", 1)
    parts = call(pair_kernel, [(keep.shape[1:], BF)] * keep.shape[0], [where, keep, got])
    return [parts[0]] + [swap(parts[m], "dp", 2 * m) for m in range(1, len(parts))], [got]


def grad_outs(depth, width):
    count = lax.axis_size("dp")
    if count != 8:
        return [((depth, width), BF)]
    return [((count // 2, depth // count, width), BF)] * 2


def emit_grad(where_ref, grad_scr, refs):
    if len(refs) == 1:
        refs[0][...] = grad_scr[...]
        return
    keep_ref, send_ref = refs
    levels, rows, _width = keep_ref.shape
    odd = where_ref[0] & 1
    for level in range(levels):
        at = pl.multiple_of((2 * level + odd) * rows, rows)
        keep_ref[level] = grad_scr[pl.ds(at, rows), :]
        at = pl.multiple_of((2 * level + 1 - odd) * rows, rows)
        send_ref[level] = grad_scr[pl.ds(at, rows), :]


def add_kernel(a_ref, b_ref, out_ref):
    out_ref[...] = (a_ref[...].astype(F32) + b_ref[...].astype(F32)).astype(BF)


def reduce_start(mine, theirs, deps=()):
    got = swap(theirs, "tensor", 1)
    return call(add_kernel, [(mine.shape, BF)], [mine, got], smem=0, deps=deps)[0]


def reduce_finish(chip, deps=()):
    got = swap(chip, "tensor", 2)
    if deps:
        got = gate(got, deps)
    return chip, got, swap(chip, "tensor", 1), swap(got, "tensor", 1)


def dot(a, b):
    return jnp.dot(a, b, preferred_element_type=F32)


def dot_nt(a, b):
    return lax.dot_general(a, b, (((1,), (1,)), ((), ())), preferred_element_type=F32)


def dot_tn(a, b):
    return lax.dot_general(a, b, (((0,), (0,)), ((), ())), preferred_element_type=F32)


def head_mask(rows, width, head):
    lane = lax.broadcasted_iota(jnp.int32, (rows, width), 1)
    return (lane >= head * HEAD_DIM) & (lane < (head + 1) * HEAD_DIM)


def only_head(values, head):
    return jnp.where(head_mask(values.shape[0], values.shape[1], head), values, jnp.zeros_like(values))


def turn_matrix(width):
    half = HEAD_DIM // 2
    source = lax.broadcasted_iota(jnp.int32, (width, width), 0)
    target = lax.broadcasted_iota(jnp.int32, (width, width), 1)
    low = (target & (HEAD_DIM - 1)) < half
    value = jnp.where(low & (source == target + half), -1.0, 0.0)
    return (value + jnp.where((~low) & (source == target - half), 1.0, 0.0)).astype(BF)


def column_as_row(block, lane):
    pick = (lax.broadcasted_iota(jnp.int32, (16, block.shape[1]), 1) == lane).astype(F32).astype(BF)
    return dot_nt(pick, block)[0:1]


def normalize(values):
    center = values - jnp.mean(values, axis=-1, keepdims=True)
    inverse = lax.rsqrt(jnp.mean(center * center, axis=-1, keepdims=True) + norm_eps)
    return center * inverse, inverse


def norm_back(grad_norm, gain_row, normed, inverse):
    scaled = grad_norm * gain_row
    return (
        scaled
        - jnp.mean(scaled, axis=-1, keepdims=True)
        - normed * jnp.mean(scaled * normed, axis=-1, keepdims=True)
    ) * inverse


def place_pieces(where_ref, pieces, masks, out_ref):
    if masks is None:
        out_ref[...] = pieces[0][...]
        return
    for piece, own in zip(pieces, masks):
        rows = piece.shape[-2]
        for i, mask in enumerate(own):
            at = pl.multiple_of((where_ref[0] ^ mask) * rows, rows)
            out_ref[pl.ds(at, rows), :] = piece[i] if len(piece.shape) == 3 else piece[...]


def call(kernel, outs, operands, scratch=(), smem=1, deps=(), vmem=8):
    count = len(operands)

    def body(*refs):
        kernel(*refs[:count], *refs[count + len(deps) :])

    return pl.pallas_call(
        body,
        out_shape=[jax.ShapeDtypeStruct(s, d) for s, d in outs],
        in_specs=[pl.BlockSpec(memory_space=pltpu.SMEM)] * smem
        + [pl.BlockSpec()] * (count - smem)
        + [pl.BlockSpec(memory_space=pl.ANY)] * len(deps),
        out_specs=[pl.BlockSpec()] * len(outs),
        scratch_shapes=list(scratch),
        compiler_params=pltpu.CompilerParams(vmem_limit_bytes=vmem * 1024 * 1024),
    )(*operands, *deps)


def stream(kernel, outs, operands, scratch=(), smem=1, deps=(), vmem=58):
    count, total = len(operands), len(outs)
    late = count - smem
    room = [pltpu.VMEM(x.shape, x.dtype) for x in operands[smem:]] + [pltpu.VMEM(x, d) for x, d in outs]

    def body(*refs):
        given, results = refs[smem:count], refs[count + len(deps) : count + len(deps) + total]
        own = refs[count + len(deps) + total :]
        flags, own = own[-1], own[:-1]
        own, held, made = own[: -late - total], own[-late - total : -total], own[-total:]
        copies = [pltpu.make_async_copy(given[i], held[i], flags.at[i]) for i in range(late)]
        for copy in copies:
            copy.start()
        waiting = {id(ref): copy for ref, copy in zip(held, copies)}
        place = {id(ref): i for i, ref in enumerate(made)}
        sent = []
        shipped = {}

        def ready(*wanted):
            for ref in wanted:
                copy = waiting.pop(id(ref), None)
                if copy is not None:
                    copy.wait()

        def ship(ref, rows=None):
            i = place[id(ref)]
            part = shipped.get(i, 0)
            shipped[i] = part + 1
            source, target = (ref, results[i]) if rows is None else (ref.at[rows], results[i].at[rows])
            copy = pltpu.make_async_copy(source, target, flags.at[late + 2 * i + part])
            copy.start()
            sent.append(copy)

        kernel(ready, ship, *refs[:smem], *held, *made, *own)
        ready(*held)
        for i, ref in enumerate(made):
            if i not in shipped:
                ship(ref)
        for copy in sent:
            copy.wait()

    anywhere = pl.BlockSpec(memory_space=pl.ANY)
    return pl.pallas_call(
        body,
        out_shape=[jax.ShapeDtypeStruct(s, d) for s, d in outs],
        in_specs=[pl.BlockSpec(memory_space=pltpu.SMEM)] * smem + [anywhere] * (late + len(deps)),
        out_specs=[anywhere] * total,
        scratch_shapes=list(scratch) + room + [pltpu.SemaphoreType.DMA((late + 2 * total,))],
        compiler_params=pltpu.CompilerParams(vmem_limit_bytes=vmem * 1024 * 1024),
    )(*operands, *deps)


def gate(value, deps):
    return pl.pallas_call(
        lambda *refs: None,
        out_shape=jax.ShapeDtypeStruct(value.shape, value.dtype),
        in_specs=[pl.BlockSpec(memory_space=pl.ANY)] * (1 + len(deps)),
        out_specs=pl.BlockSpec(memory_space=pl.ANY),
        input_output_aliases={0: 0},
        compiler_params=pltpu.CompilerParams(vmem_limit_bytes=1024 * 1024),
    )(value, *deps)


def pack_kernel(row, ready, ship, first_ref, second_ref, gain_ref, out_ref):
    width = out_ref.shape[1]
    ready(first_ref, second_ref, gain_ref)
    gain = jnp.broadcast_to(gain_ref[row : row + 1, :], (8, gain_ref.shape[1])).T
    parts = [first_ref[i] for i in range(first_ref.shape[0])] + [second_ref[...].T, gain[:, 0:1]]
    used = sum(part.shape[1] for part in parts)
    parts.append(jnp.zeros((out_ref.shape[0], width - used), F32))
    out_ref[...] = jnp.concatenate(parts, axis=1).astype(BF)


def stack(pieces):
    def body(*refs):
        flags = refs[-1]
        copies = [pltpu.make_async_copy(ref, refs[-2].at[i], flags.at[i]) for i, ref in enumerate(refs[:-2])]
        for copy in copies:
            copy.start()
        for copy in copies:
            copy.wait()

    anywhere = pl.BlockSpec(memory_space=pl.ANY)
    return pl.pallas_call(
        body,
        out_shape=jax.ShapeDtypeStruct((len(pieces),) + pieces[0].shape, pieces[0].dtype),
        in_specs=[anywhere] * len(pieces),
        out_specs=anywhere,
        scratch_shapes=[pltpu.SemaphoreType.DMA((len(pieces),))],
        compiler_params=pltpu.CompilerParams(vmem_limit_bytes=1024 * 1024),
    )(*pieces)


CHUNK = 128


def halves(core, length):
    half = length // 2
    return ((False, (1 - core) * half), (True, core * half))


def attention_kernel(masks, count, width, ready, ship, where_ref, tok_ref, segc_ref, segr_ref, cos_ref, sin_ref, *rest):
    pieces = rest[:count]
    n1_ref, q_ref, k_ref, v_ref, o_ref, ab_ref, gain_ref, mine_ref, theirs_ref, full_ref, w_scr, vm_scr = rest[count:]
    length = tok_ref.shape[0]
    heads = width // HEAD_DIM
    ready(*pieces)
    place_pieces(where_ref, pieces, masks, full_ref)
    ship(full_ref)
    gain = column_as_row(full_ref[:, 4 * width :], 0)
    gain_ref[...] = jnp.broadcast_to(gain, gain_ref.shape)
    turn = turn_matrix(width)
    for s in range(3):
        w_scr[s] = full_ref[:, s * width : (s + 1) * width]
    for s in range(2):
        w_scr[3 + s] = dot(w_scr[s], turn).astype(BF)
    w_scr[5] = full_ref[:, 3 * width : 4 * width]
    ready(tok_ref, cos_ref, sin_ref, segc_ref, segr_ref)

    def project(i, _):
        rows = pl.ds(pl.multiple_of(i * CHUNK, CHUNK), CHUNK)
        hat, _unused = normalize(tok_ref[rows, :].astype(F32))
        normed = (hat * gain).astype(BF)
        n1_ref[rows, :] = normed
        cosine, sine = cos_ref[rows, :], sin_ref[rows, :]
        q_ref[rows, :] = (dot(normed, w_scr[0]) * cosine + dot(normed, w_scr[3]) * sine).astype(BF)
        k_ref[rows, :] = (dot(normed, w_scr[1]) * cosine + dot(normed, w_scr[4]) * sine).astype(BF)
        v_ref[rows, :] = dot(normed, w_scr[2]).astype(BF)
        return 0

    lax.fori_loop(0, length // CHUNK, project, 0)
    for ref in (n1_ref, q_ref, k_ref, v_ref):
        ship(ref)
    for h in range(heads):
        vm_scr[h] = only_head(v_ref[...], h)
    core = where_ref[1] & 1
    for is_mine, first in halves(core, length):
        def attend(i, _):
            at = pl.multiple_of(i * CHUNK, CHUNK)
            rows = pl.ds(pl.multiple_of(first + at, CHUNK), CHUNK)
            allowed = segc_ref[rows, :] == segr_ref[...]
            query, keys = q_ref[rows, :], k_ref[...]
            total = jnp.zeros((CHUNK, width), F32)
            for h in range(heads):
                logits = dot_nt(only_head(query, h), keys) * HEAD_DIM ** (-0.5)
                logits = jnp.where(allowed, logits, big_negative)
                expd = jnp.exp(logits - jnp.max(logits, axis=-1, keepdims=True))
                probs = (expd / jnp.sum(expd, axis=-1, keepdims=True)).astype(BF)
                ab_ref[h, rows, :] = probs
                total = total + dot(probs, vm_scr[h])
            attended = total.astype(BF)
            o_ref[rows, :] = attended
            part = dot_nt(attended, w_scr[5]).astype(BF)
            if is_mine:
                mine_ref[pl.ds(at, CHUNK), :] = part
            else:
                theirs_ref[pl.ds(at, CHUNK), :] = part
            return 0

        lax.fori_loop(0, length // 2 // CHUNK, attend, 0)
        ship(mine_ref if is_mine else theirs_ref)


def feed_kernel(masks, count, width, ready, ship, where_ref, tok_ref, cot_ref, a_ref, b_ref, c_ref, d_ref, *rest):
    pieces = rest[:count]
    (h_ref, n2_ref, z_ref, du_ref, dv_ref, gain_ref, mine_ref, theirs_ref, full_ref, w_scr) = rest[count:]
    length = tok_ref.shape[0]
    core = where_ref[1] & 1
    ready(*pieces)
    place_pieces(where_ref, pieces, masks, full_ref)
    ship(full_ref)
    last = 3 * width // 128 * 128
    gain = column_as_row(full_ref[:, last:], 3 * width - last)
    gain_ref[...] = jnp.broadcast_to(gain, gain_ref.shape)
    for s in range(3):
        w_scr[s] = full_ref[:, s * width : (s + 1) * width]
    ready(tok_ref, cot_ref, a_ref, b_ref, c_ref, d_ref)
    for is_mine, first in halves(core, length):
        low, high = (a_ref, b_ref) if is_mine else (c_ref, d_ref)

        def step(i, _):
            at = pl.multiple_of(i * CHUNK, CHUNK)
            rows = pl.ds(pl.multiple_of(first + at, CHUNK), CHUNK)
            here = pl.ds(at, CHUNK)
            middle = tok_ref[rows, :].astype(F32) + (low[here, :].astype(F32) + high[here, :].astype(F32))
            h_ref[rows, :] = middle
            hat, _unused = normalize(middle)
            normed = (hat * gain).astype(BF)
            n2_ref[rows, :] = normed
            up, gate = dot(normed, w_scr[0]), dot(normed, w_scr[1])
            value, slope = gelu_parts(up)
            z_ref[rows, :] = (value * gate).astype(BF)
            back = dot(cot_ref[rows, :], w_scr[2])
            du, dv = (back * gate * slope).astype(BF), (back * value).astype(BF)
            du_ref[rows, :] = du
            dv_ref[rows, :] = dv
            part = dot_nt(du, w_scr[0]) + dot_nt(dv, w_scr[1])
            part = part.astype(BF)
            if is_mine:
                mine_ref[here, :] = part
            else:
                theirs_ref[here, :] = part
            return 0

        lax.fori_loop(0, length // 2 // CHUNK, step, 0)
        rows = pl.ds(pl.multiple_of(first, length // 2), length // 2)
        for ref in (h_ref, n2_ref, z_ref, du_ref, dv_ref):
            ship(ref, rows)
        ship(mine_ref if is_mine else theirs_ref)


def feed_grad_kernel(width, ready, ship, where_ref, n2_ref, cot_ref, z_ref, du_ref, dv_ref, full_ref, mine_ref, theirs_ref, *rest):
    grad_ref, w_scr = rest[-2:]
    ready(n2_ref, du_ref)
    grad_ref[:, 0:width] = dot_tn(n2_ref[...], du_ref[...]).astype(BF)
    ready(dv_ref)
    grad_ref[:, width : 2 * width] = dot_tn(n2_ref[...], dv_ref[...]).astype(BF)
    ready(cot_ref, z_ref)
    grad_ref[:, 2 * width : 3 * width] = dot_tn(cot_ref[...], z_ref[...]).astype(BF)
    emit_grad(where_ref, grad_ref, rest[:-2])
    for ref in rest[:-2]:
        ship(ref)
    ready(full_ref)
    w_scr[...] = full_ref[:, 2 * width : 3 * width]
    length = z_ref.shape[0]
    core = where_ref[1] & 1
    for is_mine, first in halves(core, length):
        rows = pl.ds(pl.multiple_of(first, length // 2), length // 2)
        part = dot_nt(z_ref[rows, :], w_scr[...]).astype(BF)
        if is_mine:
            mine_ref[...] = part
        else:
            theirs_ref[...] = part


SPAN = 256


def back_kernel(width, ready, ship, where_ref, a_ref, b_ref, c_ref, d_ref, h_ref, cot_ref, gain_ref, full_ref, q_ref, k_ref, v_ref, o_ref, ab_ref,
                n1_ref, cos_ref, sin_ref, om_ref, ot_ref, dh_ref, mine_ref, theirs_ref, *rest):
    grad_ref, low_scr, do_scr, w_scr, km_scr, qm_scr, dk_scr, dv_scr, dp_scr = rest[-9:]
    length = h_ref.shape[0]
    half = length // 2
    heads = width // HEAD_DIM
    core = where_ref[1] & 1
    ready(gain_ref, full_ref, a_ref, b_ref, c_ref, d_ref, h_ref, cot_ref)
    gain = gain_ref[0:1, :]
    for s in range(4):
        w_scr[s] = full_ref[:, s * width : (s + 1) * width]
    for is_mine, first in halves(core, length):
        low, high = (a_ref, b_ref) if is_mine else (c_ref, d_ref)

        def step(i, _):
            at = pl.multiple_of(i * CHUNK, CHUNK)
            rows = pl.ds(pl.multiple_of(first + at, CHUNK), CHUNK)
            here = pl.ds(at, CHUNK)
            grad = low[here, :].astype(F32) + high[here, :].astype(F32)
            hat, inverse = normalize(h_ref[rows, :])
            total = cot_ref[rows, :].astype(F32) + norm_back(grad, gain, hat, inverse)
            dh_ref[rows, :] = total
            narrow = total.astype(BF)
            low_scr[rows, :] = narrow
            do_scr[rows, :] = dot(narrow, w_scr[3]).astype(BF)
            return 0

        lax.fori_loop(0, half // CHUNK, step, 0)
    ship(dh_ref)
    turn = turn_matrix(width)
    ready(q_ref, k_ref, v_ref, o_ref, ab_ref)
    kt = (-dot(k_ref[...], turn)).astype(BF)
    qt = (-dot(q_ref[...], turn)).astype(BF)
    for h in range(heads):
        km_scr[h, :, 0:width] = only_head(k_ref[...], h)
        km_scr[h, :, 256 : 256 + width] = only_head(kt, h)
        qm_scr[h, :, 0:width] = only_head(q_ref[...], h)
        qm_scr[h, :, 256 : 256 + width] = only_head(qt, h)

    ready(cos_ref, sin_ref)
    for i in range(length // SPAN):
        rows = pl.ds(i * SPAN, SPAN)
        grad_o = do_scr[rows, :]
        product = grad_o.astype(F32) * o_ref[rows, :].astype(F32)
        dq = None
        dk = None
        dv = None
        for h in range(heads):
            own = only_head(grad_o, h)
            delta = jnp.sum(only_head(product, h), axis=-1, keepdims=True)
            da = dot_nt(own, v_ref[...])
            probs = ab_ref[h, rows, :]
            term = dot_tn(probs, own)
            dv = term if dv is None else dv + term
            ds = (probs.astype(F32) * (da - delta) * HEAD_DIM ** (-0.5)).astype(BF)
            term = dot(ds, km_scr[h])
            dq = term if dq is None else dq + term
            term = dot_tn(ds, qm_scr[h, rows, :])
            dk = term if dk is None else dk + term
        dp_scr[0, rows, :] = (dq[:, :width] * cos_ref[rows, :] + dq[:, 256 : 256 + width] * sin_ref[rows, :]).astype(BF)
        if i == 0:
            dk_scr[...] = dk
            dv_scr[...] = dv
        else:
            dk_scr[...] += dk
            dv_scr[...] += dv
    dp_scr[1] = (dk_scr[:, :width] * cos_ref[...] + dk_scr[:, 256 : 256 + width] * sin_ref[...]).astype(BF)
    dp_scr[2] = dv_scr[...].astype(BF)
    ready(n1_ref)
    for s in range(3):
        grad_ref[:, s * width : (s + 1) * width] = dot_tn(n1_ref[...], dp_scr[s]).astype(BF)
    grad_ref[:, 3 * width :] = dot_tn(low_scr[...], o_ref[...]).astype(BF)
    emit_grad(where_ref, grad_ref, rest[:-9])
    for ref in rest[:-9]:
        ship(ref)
    ready(om_ref, ot_ref)
    for is_mine, first in halves(core, length):
        out, other = (mine_ref, om_ref) if is_mine else (theirs_ref, ot_ref)
        rows = pl.ds(pl.multiple_of(first, half), half)
        part = dot_nt(dp_scr[0, rows, :], w_scr[0]) + dot_nt(dp_scr[1, rows, :], w_scr[1]) + dot_nt(dp_scr[2, rows, :], w_scr[2])
        out[0] = part.astype(BF)
        out[1] = other[...]
        ship(out)


def output_kernel(ready, ship, where_ref, h_ref, tok_ref, dh_ref, gain_ref, a_ref, b_ref, c_ref, d_ref, out_ref, grad_ref):
    length = h_ref.shape[0]
    core = where_ref[1] & 1
    ready(h_ref, tok_ref, dh_ref, gain_ref, a_ref, b_ref, c_ref, d_ref)
    gain = gain_ref[0:1, :]
    for is_mine, first in halves(core, length):
        low, high = (a_ref, b_ref) if is_mine else (c_ref, d_ref)

        def step(i, _):
            at = pl.multiple_of(i * CHUNK, CHUNK)
            rows = pl.ds(pl.multiple_of(first + at, CHUNK), CHUNK)
            here = pl.ds(at, CHUNK)
            out_ref[rows, :] = h_ref[rows, :] + (low[1, here, :].astype(F32) + high[1, here, :].astype(F32))
            grad = low[0, here, :].astype(F32) + high[0, here, :].astype(F32)
            hat, inverse = normalize(tok_ref[rows, :].astype(F32))
            grad_ref[rows, :] = dh_ref[rows, :] + norm_back(grad, gain, hat, inverse)
            return 0

        lax.fori_loop(0, length // 2 // CHUNK, step, 0)
        rows = pl.ds(pl.multiple_of(first, length // 2), length // 2)
        ship(out_ref, rows)
        ship(grad_ref, rows)


def total_of(refs):
    total = refs[0][...].astype(F32)
    for ref in refs[1:]:
        total = total + ref[...].astype(F32)
    return total


def step_kernel(groups, plan, *refs):
    at = 0
    shards = []
    for count in groups:
        shards.append(total_of(refs[at : at + count]))
        at += count
    outs = refs[at + 3 * len(plan) :]
    for leaf, (transposed, slices) in enumerate(plan):
        w_ref, f_ref, s_ref = refs[at : at + 3]
        at += 3
        g_out, d_out, f_out, s_out = outs[4 * leaf : 4 * leaf + 4]
        for i, (group, first, columns) in enumerate(slices):
            grad = shards[group][:, first : first + columns]
            if transposed:
                grad = grad.T
            where = (i,) if len(w_ref.shape) == 3 else Ellipsis
            delta, first_new, second_new = adamw(w_ref[where], grad, f_ref[where], s_ref[where], decay_rate)
            g_out[where] = grad
            d_out[where] = delta
            f_out[where] = first_new
            s_out[where] = second_new


def gain_kernel(columns, gain_row, w_ref, gains_ref, *refs):
    shard = total_of(refs[:-1])
    total = jnp.zeros((shard.shape[0], 1), F32)
    for i, first in enumerate(columns):
        width = w_ref.shape[2]
        narrow = w_ref[i].astype(BF).astype(F32)
        total = total + jnp.sum(narrow * shard[:, first : first + width], axis=-1, keepdims=True)
    wide = jnp.broadcast_to(total, (shard.shape[0], 128)).T
    gain = gains_ref[gain_row : gain_row + 1, :].astype(BF).astype(F32)
    refs[-1][...] = wide[0:8, :] / gain


def gain_call(columns, gain_row, weight, gains, pieces, deps=()):
    return call(
        lambda *refs: gain_kernel(columns, gain_row, *refs),
        [((8, gains.shape[1]), F32)],
        [weight, gains, *pieces],
        smem=0,
        deps=deps,
    )[0]


def sum_small(values):
    if lax.axis_size("tensor") != 4:
        return lax.psum(values, "tensor")
    return (values + swap(values, "tensor", 1)) + (swap(values, "tensor", 2) + swap(values, "tensor", 3))


def step_call(groups, plan, leaves):
    operands = [piece for group in groups for piece in group]
    for leaf in leaves:
        operands += list(leaf)
    outs = [(leaf[0].shape, F32) for leaf in leaves for _ in range(4)]

    def kernel(*refs):
        step_kernel([len(g) for g in groups], plan, *refs)

    flat = call(kernel, outs, operands, smem=0)
    return [flat[4 * i : 4 * i + 4] for i in range(len(leaves))]


def local(
    tokens,
    segment_ids,
    cotangent,
    w_qkv,
    w_out,
    w_in,
    w_down,
    gains,
    first_qkv,
    first_out,
    first_in,
    first_down,
    first_gains,
    second_qkv,
    second_out,
    second_in,
    second_down,
    second_gains,
):
    heads = w_qkv.shape[2]
    hidden = w_in.shape[2]
    length, depth = tokens.shape
    half = length // 2
    where = jnp.stack([lax.axis_index("dp"), lax.axis_index("tensor")]).astype(jnp.int32)
    pieces_a, masks_a, pieces_b, masks_b, early = gather_pieces(
        lambda deps: pack(w_qkv, w_out, gains, 0, deps), lambda deps: pack(w_in, w_down, gains, 1, deps)
    )
    wide_a, wide_b = pieces_a[0].shape[-1], pieces_b[0].shape[-1]
    repeat = heads // HEAD_DIM
    cosine_table, sine_values = rope_tables(length, heads, pieces_a[1:2])
    segments = segment_ids.astype(jnp.int32)

    n1, q, k, v, o, ab, gain_one, mine, theirs, full_a = stream(
        lambda *refs: attention_kernel(masks_a, len(pieces_a), heads, *refs),
        [
            ((length, depth), BF),
            ((length, heads), BF),
            ((length, heads), BF),
            ((length, heads), BF),
            ((length, heads), BF),
            ((repeat, length, length), BF),
            ((8, depth), F32),
            ((half, depth), BF),
            ((half, depth), BF),
            ((depth, wide_a), BF),
        ],
        [where, tokens, segments.reshape(length, 1), segments, cosine_table, sine_values, *pieces_a],
        [pltpu.VMEM((6, depth, heads), BF), pltpu.VMEM((repeat, length, heads), BF)],
    )
    terms = reduce_finish(reduce_start(mine, gate(theirs, early) if early else theirs))
    middle, n2, z, du, dv2, gain_two, mine, theirs, full_b = stream(
        lambda *refs: feed_kernel(masks_b, len(pieces_b), hidden, *refs),
        [
            ((length, depth), F32),
            ((length, depth), BF),
            ((length, hidden), BF),
            ((length, hidden), BF),
            ((length, hidden), BF),
            ((8, depth), F32),
            ((half, depth), BF),
            ((half, depth), BF),
            ((depth, wide_b), BF),
        ],
        [where, tokens, cotangent, *terms, *pieces_b],
        [pltpu.VMEM((3, depth, hidden), BF)],
    )
    chip = reduce_start(mine, theirs)
    width = 3 * hidden
    out_mine, out_theirs, *grad_feed = stream(
        lambda *refs: feed_grad_kernel(hidden, *refs),
        [((half, depth), BF), ((half, depth), BF)] + grad_outs(depth, width),
        [where, n2, cotangent, z, du, dv2, full_b],
        [pltpu.VMEM((depth, width), BF), pltpu.VMEM((depth, hidden), BF)],
        deps=[chip],
    )
    terms = reduce_finish(chip, [out_mine])
    feed_pieces, feed_got = scatter_start(where, grad_feed)
    width = 4 * heads
    dh, mine, theirs, *grad_attn = stream(
        lambda *refs: back_kernel(heads, *refs),
        [((length, depth), F32), ((2, half, depth), BF), ((2, half, depth), BF)] + grad_outs(depth, width),
        [where, *terms, middle, cotangent, gain_two, full_a, q, k, v, o, ab, n1, cosine_table, sine_values, out_mine, out_theirs],
        [
            pltpu.VMEM((depth, width), BF),
            pltpu.VMEM((length, depth), BF),
            pltpu.VMEM((length, heads), BF),
            pltpu.VMEM((4, depth, heads), BF),
            pltpu.VMEM((repeat, length, 512), BF),
            pltpu.VMEM((repeat, length, 512), BF),
            pltpu.VMEM((length, 512), F32),
            pltpu.VMEM((length, heads), F32),
            pltpu.VMEM((3, length, heads), BF),
        ],
    )
    attn_pieces, attn_got = scatter_start(where, grad_attn)
    terms = reduce_finish(reduce_start(mine, gate(theirs, feed_got) if feed_got else theirs), feed_pieces[1:] + attn_got)
    output, grad_tokens = stream(
        output_kernel,
        [((length, depth), F32), ((length, depth), F32)],
        [where, middle, tokens, dh, gain_one, *terms],
    )

    gain_sum_two = gain_call([0, hidden], 1, w_in, gains, feed_pieces)
    leaf_in, leaf_down = step_call(
        [feed_pieces],
        [(False, [(0, 0, hidden), (0, hidden, hidden)]), (True, [(0, 2 * hidden, hidden)])],
        [(w_in, first_in, second_in), (w_down, first_down, second_down)],
    )
    gain_sum_one = gain_call([0, heads, 2 * heads], 0, w_qkv, gains, attn_pieces, [grad_tokens, leaf_in[0]])
    share_gains = sum_small(jnp.concatenate([gain_sum_one[0:1], gain_sum_two[0:1]], axis=0))
    leaf_qkv, leaf_out = step_call(
        [attn_pieces],
        [(False, [(0, 0, heads), (0, heads, heads), (0, 2 * heads, heads)]), (True, [(0, 3 * heads, heads)])],
        [(w_qkv, first_qkv, second_qkv), (w_out, first_out, second_out)],
    )
    n_gains, m_gains, s_gains = adamw(gains, share_gains, first_gains, second_gains, 0.0)
    by_kind = list(zip(leaf_qkv, leaf_out, leaf_in, leaf_down, (share_gains, n_gains, m_gains, s_gains)))
    return (output, grad_tokens, *by_kind[0], *by_kind[1], *by_kind[2], *by_kind[3])


def solution(mesh):
    placed = (
        P("dp", None),
        P("dp", None),
        P("dp", None),
        P(None, "dp", "tensor"),
        P("tensor", "dp"),
        P(None, "dp", "tensor"),
        P("tensor", "dp"),
        P(None, "dp"),
        P(None, "dp", "tensor"),
        P("tensor", "dp"),
        P(None, "dp", "tensor"),
        P("tensor", "dp"),
        P(None, "dp"),
        P(None, "dp", "tensor"),
        P("tensor", "dp"),
        P(None, "dp", "tensor"),
        P("tensor", "dp"),
        P(None, "dp"),
    )
    return jax.shard_map(
        local,
        mesh=mesh,
        in_specs=placed,
        out_specs=(
            P("dp", None),
            P("dp", None),
            P(None, "dp", "tensor"),
            P("tensor", "dp"),
            P(None, "dp", "tensor"),
            P("tensor", "dp"),
            P(None, "dp"),
            P(None, "dp", "tensor"),
            P("tensor", "dp"),
            P(None, "dp", "tensor"),
            P("tensor", "dp"),
            P(None, "dp"),
            P(None, "dp", "tensor"),
            P("tensor", "dp"),
            P(None, "dp", "tensor"),
            P("tensor", "dp"),
            P(None, "dp"),
            P(None, "dp", "tensor"),
            P("tensor", "dp"),
            P(None, "dp", "tensor"),
            P("tensor", "dp"),
            P(None, "dp"),
        ),
        check_vma=False,
    )
```

```python
import jax
import jax.numpy as jnp
from jax import lax
from jax.experimental import pallas as pl
from jax.experimental.pallas import tpu as pltpu
from jax.sharding import PartitionSpec as P

HEAD_DIM = 64
STEP = 3


norm_eps = 1e-05
rope_base = 160000.0
learn_rate = 0.01
beta_one = 0.9
beta_two = 0.98
adam_eps = 1e-08
decay_rate = 0.01
big_negative = -1e30

BF = jnp.bfloat16
F32 = jnp.float32


def rope_tables(count, width):
    half_dim = HEAD_DIM // 2
    spot = (jnp.arange(width) % half_dim).astype(jnp.float32)
    frequency = rope_base ** (-(spot * 2.0 / HEAD_DIM))
    angles = jnp.arange(count, dtype=jnp.float32)[:, None] * frequency[None, :]
    return (jnp.cos(angles), jnp.sin(angles))


def gelu_parts(inputs):
    normal_cdf = 0.5 * (1.0 + lax.erf(inputs * 0.7071067811865476))
    density = jnp.exp(-0.5 * inputs * inputs) * 0.3989422804014327
    return (inputs * normal_cdf, normal_cdf + inputs * density)


def adamw(weight, gradient, first_mom, second, decay_now):
    first_new = beta_one * first_mom + (1.0 - beta_one) * gradient
    second_new = beta_two * second + (1.0 - beta_two) * gradient * gradient
    corr_one = 1.0 - beta_one**STEP
    corr_two = 1.0 - beta_two**STEP
    update = (
        first_new / corr_one / (jnp.sqrt(second_new / corr_two) + adam_eps) + decay_now * weight
    )
    return (-learn_rate * update, first_new, second_new)


def swap(values, axis, mask):
    count = lax.axis_size(axis)
    return lax.ppermute(values, axis, [(i, i ^ mask) for i in range(count)])


def pack(first, second, gains, row, deps=()):
    rows = first.shape[1]
    used = first.shape[0] * first.shape[2] + second.shape[0] + 1
    width = -(-used // 128) * 128
    return stream(
        lambda *refs: pack_kernel(row, *refs), [((rows, width), BF)], [first, second, gains], smem=0, deps=deps, vmem=16, near=(0,), far=(0, 1, 2)
    )[0]


def gather_pieces(beside, pack_a, pack_b):
    if lax.axis_size("dp") != 8:
        full_a = lax.all_gather(pack_a(()), "dp", axis=0, tiled=True)
        full_b = lax.all_gather(pack_b(()), "dp", axis=0, tiled=True)
        return [full_a], None, [full_b], None, [], []
    order = (4, 6, 2)
    shard_a, shard_b = pack_a(()), pack_b(())
    far_one, far_two, near = [swap(shard_a, "dp", m) for m in order]
    side = swap(shard_a, "dp", 1)
    sides = [side, swap(gate(side, beside), "dp", 2), swap(far_one, "dp", 1), swap(far_two, "dp", 1)]
    pieces_a = [shard_a, near, far_one, far_two] + sides
    masks_a = [[m] for m in (0, 2, 4, 6, 1, 3, 5, 7)]
    shard_b = gate(shard_b, [far_one, far_two, sides[1]])
    column = [swap(shard_b, "dp", m) for m in order]
    side = swap(shard_b, "dp", 1)
    stacked = stack(column)
    pieces_b = [shard_b, stacked, side, swap(stacked, "dp", 1)]
    return pieces_a, masks_a, pieces_b, [[0], [4, 6, 2], [1], [5, 7, 3]], column + [side], [stacked]


def pair_kernel(where_ref, keep_ref, got_ref, own_ref, *far_refs):
    level = where_ref[0] >> 1
    for m, ref in enumerate((own_ref,) + far_refs):
        at = level ^ m
        ref[...] = (keep_ref[at].astype(F32) + got_ref[at].astype(F32)).astype(BF)


def scatter_start(where, grads, deps=()):
    if len(grads) == 1:
        return [lax.psum_scatter(grads[0].astype(F32), "dp", scatter_dimension=0, tiled=True)], [], []
    keep, send = grads
    got = swap(send, "dp", 1)
    parts = call(pair_kernel, [(keep.shape[1:], BF)] * keep.shape[0], [where, keep, got], deps=deps)
    return [parts[0]] + [swap(parts[m], "dp", 2 * m) for m in range(1, len(parts))], [got], [parts[0]]


def far_kernel(where_ref, *refs):
    terms, (own_ref, send_ref) = refs[:-2], refs[-2:]
    rows = own_ref.shape[0]
    odd = where_ref[0] & 1
    for ref, at in ((own_ref, odd), (send_ref, 1 - odd)):
        span = pl.ds(pl.multiple_of(at * rows, rows), rows)
        total = terms[0][span, :].astype(F32)
        for term in terms[1:]:
            total = total + term[span, :].astype(F32)
        ref[...] = total.astype(BF)


def scatter_far_first(where, grads):
    if len(grads) == 1:
        pieces, got, _unused = scatter_start(where, grads)
        return lambda deps: pieces, got
    got = [swap(grads[m], "dp", 2 * m) for m in range(1, len(grads))]
    rows, width = grads[0].shape

    def finish(deps):
        own, send = call(far_kernel, [((rows // 2, width), BF)] * 2, [where, grads[0], *got], deps=deps)
        return [own, swap(send, "dp", 1)]

    return finish, got


def far_outs(depth, width):
    count = lax.axis_size("dp")
    if count != 8:
        return [((depth, width), BF)]
    return [((2 * depth // count, width), BF)] * (count // 2)


def emit_far(where_ref, grad_scr, refs):
    level = where_ref[0] >> 1
    for m, ref in enumerate(refs):
        if len(refs) == 1:
            ref[...] = grad_scr[...]
        else:
            at = pl.multiple_of((level ^ m) * ref.shape[0], ref.shape[0])
            ref[...] = grad_scr[pl.ds(at, ref.shape[0]), :]


def grad_outs(depth, width):
    count = lax.axis_size("dp")
    if count != 8:
        return [((depth, width), BF)]
    return [((count // 2, depth // count, width), BF)] * 2


def emit_grad(where_ref, grad_scr, refs):
    if len(refs) == 1:
        refs[0][...] = grad_scr[...]
        return
    keep_ref, send_ref = refs
    levels, rows, _width = keep_ref.shape
    odd = where_ref[0] & 1
    for level in range(levels):
        at = pl.multiple_of((2 * level + odd) * rows, rows)
        keep_ref[level] = grad_scr[pl.ds(at, rows), :]
        at = pl.multiple_of((2 * level + 1 - odd) * rows, rows)
        send_ref[level] = grad_scr[pl.ds(at, rows), :]


def add_kernel(a_ref, b_ref, out_ref):
    out_ref[...] = (a_ref[...].astype(F32) + b_ref[...].astype(F32)).astype(BF)


def reduce_start(mine, theirs, deps=()):
    got = swap(theirs, "tensor", 1)
    return call(add_kernel, [(mine.shape, BF)], [mine, got], smem=0, deps=deps)[0]


def reduce_finish(chip, deps=()):
    got = swap(chip, "tensor", 2)
    if deps:
        got = gate(got, deps)
    return [chip, got, swap(chip, "tensor", 1), swap(got, "tensor", 1)]


def dot(a, b):
    return jnp.dot(a, b, preferred_element_type=F32)


def dot_nt(a, b):
    return lax.dot_general(a, b, (((1,), (1,)), ((), ())), preferred_element_type=F32)


def dot_tn(a, b):
    return lax.dot_general(a, b, (((0,), (0,)), ((), ())), preferred_element_type=F32)


def head_mask(rows, width, head):
    lane = lax.broadcasted_iota(jnp.int32, (rows, width), 1)
    return (lane >= head * HEAD_DIM) & (lane < (head + 1) * HEAD_DIM)


def only_head(values, head):
    return jnp.where(head_mask(values.shape[0], values.shape[1], head), values, jnp.zeros_like(values))


def turn_matrix(width):
    half = HEAD_DIM // 2
    source = lax.broadcasted_iota(jnp.int32, (width, width), 0)
    target = lax.broadcasted_iota(jnp.int32, (width, width), 1)
    low = (target & (HEAD_DIM - 1)) < half
    value = jnp.where(low & (source == target + half), -1.0, 0.0)
    return (value + jnp.where((~low) & (source == target - half), 1.0, 0.0)).astype(BF)


def column_as_row(block, lane):
    pick = (lax.broadcasted_iota(jnp.int32, (16, block.shape[1]), 1) == lane).astype(F32).astype(BF)
    return dot_nt(pick, block)[0:1]


def normalize(values):
    center = values - jnp.mean(values, axis=-1, keepdims=True)
    inverse = lax.rsqrt(jnp.mean(center * center, axis=-1, keepdims=True) + norm_eps)
    return center * inverse, inverse


def norm_back(grad_norm, gain_row, normed, inverse):
    scaled = grad_norm * gain_row
    return (
        scaled
        - jnp.mean(scaled, axis=-1, keepdims=True)
        - normed * jnp.mean(scaled * normed, axis=-1, keepdims=True)
    ) * inverse


def place_pieces(where_ref, pieces, masks, out_ref):
    if masks is None:
        out_ref[...] = pieces[0][...]
        return
    for piece, own in zip(pieces, masks):
        rows = piece.shape[-2]
        for i, mask in enumerate(own):
            at = pl.multiple_of((where_ref[0] ^ mask) * rows, rows)
            out_ref[pl.ds(at, rows), :] = piece[i] if len(piece.shape) == 3 else piece[...]


def call(kernel, outs, operands, scratch=(), smem=1, deps=(), vmem=8):
    count = len(operands)

    def body(*refs):
        kernel(*refs[:count], *refs[count + len(deps) :])

    return pl.pallas_call(
        body,
        out_shape=[jax.ShapeDtypeStruct(s, d) for s, d in outs],
        in_specs=[pl.BlockSpec(memory_space=pltpu.SMEM)] * smem
        + [pl.BlockSpec()] * (count - smem)
        + [pl.BlockSpec(memory_space=pl.ANY)] * len(deps),
        out_specs=[pl.BlockSpec()] * len(outs),
        scratch_shapes=list(scratch),
        compiler_params=pltpu.CompilerParams(vmem_limit_bytes=vmem * 1024 * 1024),
    )(*operands, *deps)


def stream(kernel, outs, operands, scratch=(), smem=1, deps=(), vmem=40, near=(), far=()):
    count, total = len(operands), len(outs)
    late = count - smem
    room = [pltpu.VMEM(x.shape, x.dtype) for x in operands[smem:]]
    room += [pltpu.VMEM(*out) for i, out in enumerate(outs) if i not in near]
    gone = total - len(near)

    def body(*refs):
        given, results = refs[smem:count], refs[count + len(deps) : count + len(deps) + total]
        own = refs[count + len(deps) + total :]
        flags, own = own[-1], own[:-1]
        own, held, made = own[: -late - gone], own[-late - gone : -gone or None], list(own[len(own) - gone :])
        for i in sorted(near):
            made.insert(i, results[i])
        copies = [pltpu.make_async_copy(given[i], held[i], flags.at[i]) for i in range(late)]
        for copy in copies:
            copy.start()
        waiting = {id(ref): copy for ref, copy in zip(held, copies)}
        place = {id(ref): i for i, ref in enumerate(made) if i not in near}
        sent = []
        shipped = {}

        def ready(*wanted):
            for ref in wanted:
                copy = waiting.pop(id(ref), None)
                if copy is not None:
                    copy.wait()

        def ship(ref, rows=None):
            i = place.get(id(ref))
            if i is None:
                return
            part = shipped.get(i, 0)
            shipped[i] = part + 1
            source, target = (ref, results[i]) if rows is None else (ref.at[rows], results[i].at[rows])
            copy = pltpu.make_async_copy(source, target, flags.at[late + 2 * i + part])
            copy.start()
            sent.append(copy)

        kernel(ready, ship, *refs[:smem], *held, *made, *own)
        ready(*held)
        for i, ref in enumerate(made):
            if i not in shipped:
                ship(ref)
        for copy in sent:
            copy.wait()

    anywhere = pl.BlockSpec(memory_space=pl.ANY)
    pinned = [pltpu.with_memory_space_constraint(x, pltpu.HBM) if i in far else x for i, x in enumerate(operands)]
    return pl.pallas_call(
        body,
        out_shape=[jax.ShapeDtypeStruct(*out) if i in near else pltpu.HBM(*out) for i, out in enumerate(outs)],
        in_specs=[pl.BlockSpec(memory_space=pltpu.SMEM)] * smem + [anywhere] * (late + len(deps)),
        out_specs=[pl.BlockSpec() if i in near else anywhere for i in range(total)],
        scratch_shapes=list(scratch) + room + [pltpu.SemaphoreType.DMA((late + 2 * total,))],
        compiler_params=pltpu.CompilerParams(vmem_limit_bytes=vmem * 1024 * 1024),
    )(*pinned, *deps)


def gate(value, deps):
    if not deps:
        return value
    return pl.pallas_call(
        lambda *refs: None,
        out_shape=jax.ShapeDtypeStruct(value.shape, value.dtype),
        in_specs=[pl.BlockSpec(memory_space=pl.ANY)] * (1 + len(deps)),
        out_specs=pl.BlockSpec(memory_space=pl.ANY),
        input_output_aliases={0: 0},
        compiler_params=pltpu.CompilerParams(vmem_limit_bytes=1024 * 1024),
    )(value, *deps)


def pack_kernel(row, ready, ship, first_ref, second_ref, gain_ref, out_ref):
    width = out_ref.shape[1]
    ready(first_ref, second_ref, gain_ref)
    gain = jnp.broadcast_to(gain_ref[row : row + 1, :], (8, gain_ref.shape[1])).T
    parts = [first_ref[i] for i in range(first_ref.shape[0])] + [second_ref[...].T, gain[:, 0:1]]
    used = sum(part.shape[1] for part in parts)
    parts.append(jnp.zeros((out_ref.shape[0], width - used), F32))
    out_ref[...] = jnp.concatenate(parts, axis=1).astype(BF)


def stack(pieces):
    def body(*refs):
        flags = refs[-1]
        copies = [pltpu.make_async_copy(ref, refs[-2].at[i], flags.at[i]) for i, ref in enumerate(refs[:-2])]
        for copy in copies:
            copy.start()
        for copy in copies:
            copy.wait()

    anywhere = pl.BlockSpec(memory_space=pl.ANY)
    return pl.pallas_call(
        body,
        out_shape=jax.ShapeDtypeStruct((len(pieces),) + pieces[0].shape, pieces[0].dtype),
        in_specs=[anywhere] * len(pieces),
        out_specs=anywhere,
        scratch_shapes=[pltpu.SemaphoreType.DMA((len(pieces),))],
        compiler_params=pltpu.CompilerParams(vmem_limit_bytes=1024 * 1024),
    )(*pieces)


CHUNK = 128


def halves(core, length):
    half = length // 2
    return ((False, (1 - core) * half), (True, core * half))


def attention_kernel(masks, count, width, ready, ship, where_ref, tok_ref, segc_ref, segr_ref, cos_ref, sin_ref, *rest):
    pieces = rest[:count]
    n1_ref, q_ref, k_ref, v_ref, o_ref, ab_ref, gain_ref, mine_ref, theirs_ref, full_ref, w_scr, vm_scr = rest[count:]
    length = tok_ref.shape[0]
    heads = width // HEAD_DIM
    ready(*pieces)
    place_pieces(where_ref, pieces, masks, full_ref)
    ship(full_ref)
    gain = column_as_row(full_ref[:, 4 * width :], 0)
    gain_ref[...] = jnp.broadcast_to(gain, gain_ref.shape)
    turn = turn_matrix(width)
    for s in range(3):
        w_scr[s] = full_ref[:, s * width : (s + 1) * width]
    for s in range(2):
        w_scr[3 + s] = dot(w_scr[s], turn).astype(BF)
    w_scr[5] = full_ref[:, 3 * width : 4 * width]
    ready(tok_ref, cos_ref, sin_ref, segc_ref, segr_ref)

    def project(i, _):
        rows = pl.ds(pl.multiple_of(i * CHUNK, CHUNK), CHUNK)
        hat, _unused = normalize(tok_ref[rows, :].astype(F32))
        normed = (hat * gain).astype(BF)
        n1_ref[rows, :] = normed
        cosine, sine = cos_ref[rows, :], sin_ref[rows, :]
        q_ref[rows, :] = (dot(normed, w_scr[0]) * cosine + dot(normed, w_scr[3]) * sine).astype(BF)
        k_ref[rows, :] = (dot(normed, w_scr[1]) * cosine + dot(normed, w_scr[4]) * sine).astype(BF)
        v_ref[rows, :] = dot(normed, w_scr[2]).astype(BF)
        return 0

    lax.fori_loop(0, length // CHUNK, project, 0)
    for ref in (n1_ref, q_ref, k_ref, v_ref):
        ship(ref)
    for h in range(heads):
        vm_scr[h] = only_head(v_ref[...], h)
    core = where_ref[1] & 1
    for is_mine, first in halves(core, length):
        def attend(i, _):
            at = pl.multiple_of(i * CHUNK, CHUNK)
            rows = pl.ds(pl.multiple_of(first + at, CHUNK), CHUNK)
            allowed = segc_ref[rows, :] == segr_ref[...]
            query, keys = q_ref[rows, :], k_ref[...]
            total = jnp.zeros((CHUNK, width), F32)
            for h in range(heads):
                logits = dot_nt(only_head(query, h), keys) * HEAD_DIM ** (-0.5)
                logits = jnp.where(allowed, logits, big_negative)
                expd = jnp.exp(logits - jnp.max(logits, axis=-1, keepdims=True))
                probs = (expd / jnp.sum(expd, axis=-1, keepdims=True)).astype(BF)
                ab_ref[h, rows, :] = probs
                total = total + dot(probs, vm_scr[h])
            attended = total.astype(BF)
            o_ref[rows, :] = attended
            part = dot_nt(attended, w_scr[5]).astype(BF)
            if is_mine:
                mine_ref[pl.ds(at, CHUNK), :] = part
            else:
                theirs_ref[pl.ds(at, CHUNK), :] = part
            return 0

        lax.fori_loop(0, length // 2 // CHUNK, attend, 0)
        ship(mine_ref if is_mine else theirs_ref)
        ship(ab_ref, (slice(None), pl.ds(pl.multiple_of(first, length // 2), length // 2)))


def feed_kernel(masks, count, width, ready, ship, where_ref, tok_ref, cot_ref, a_ref, b_ref, c_ref, d_ref, *rest):
    pieces = rest[:count]
    (h_ref, n2_ref, z_ref, du_ref, dv_ref, gain_ref, mine_ref, theirs_ref, full_ref, w_scr) = rest[count:]
    length = tok_ref.shape[0]
    core = where_ref[1] & 1
    ready(*pieces)
    place_pieces(where_ref, pieces, masks, full_ref)
    ship(full_ref)
    last = 3 * width // 128 * 128
    gain = column_as_row(full_ref[:, last:], 3 * width - last)
    gain_ref[...] = jnp.broadcast_to(gain, gain_ref.shape)
    for s in range(3):
        w_scr[s] = full_ref[:, s * width : (s + 1) * width]
    ready(tok_ref, cot_ref, a_ref, b_ref, c_ref, d_ref)
    for is_mine, first in halves(core, length):
        low, high = (a_ref, b_ref) if is_mine else (c_ref, d_ref)

        def step(i, _):
            at = pl.multiple_of(i * CHUNK, CHUNK)
            rows = pl.ds(pl.multiple_of(first + at, CHUNK), CHUNK)
            here = pl.ds(at, CHUNK)
            middle = tok_ref[rows, :].astype(F32) + (low[here, :].astype(F32) + high[here, :].astype(F32))
            h_ref[rows, :] = middle
            hat, _unused = normalize(middle)
            normed = (hat * gain).astype(BF)
            n2_ref[rows, :] = normed
            up, gate = dot(normed, w_scr[0]), dot(normed, w_scr[1])
            value, slope = gelu_parts(up)
            z_ref[rows, :] = (value * gate).astype(BF)
            back = dot(cot_ref[rows, :], w_scr[2])
            du, dv = (back * gate * slope).astype(BF), (back * value).astype(BF)
            du_ref[rows, :] = du
            dv_ref[rows, :] = dv
            part = dot_nt(du, w_scr[0]) + dot_nt(dv, w_scr[1])
            part = part.astype(BF)
            if is_mine:
                mine_ref[here, :] = part
            else:
                theirs_ref[here, :] = part
            return 0

        lax.fori_loop(0, length // 2 // CHUNK, step, 0)
        rows = pl.ds(pl.multiple_of(first, length // 2), length // 2)
        for ref in (h_ref, n2_ref, z_ref, du_ref, dv_ref):
            ship(ref, rows)
        ship(mine_ref if is_mine else theirs_ref)


def feed_grad_kernel(width, split, ready, ship, where_ref, n2_ref, du_ref, dv_ref, cot_ref, z_ref, full_ref, mine_ref, theirs_ref, *rest):
    grad_ref, down_ref, w_scr = rest[-3:]
    ready(n2_ref, du_ref)
    grad_ref[:, 0:width] = dot_tn(n2_ref[...], du_ref[...]).astype(BF)
    ready(dv_ref)
    grad_ref[:, width : 2 * width] = dot_tn(n2_ref[...], dv_ref[...]).astype(BF)
    emit_grad(where_ref, grad_ref, rest[:split])
    for ref in rest[:split]:
        ship(ref)
    ready(cot_ref, z_ref)
    down_ref[...] = dot_tn(cot_ref[...], z_ref[...]).astype(BF)
    emit_far(where_ref, down_ref, rest[split:-3])
    for ref in rest[split:-3]:
        ship(ref)
    ready(full_ref)
    w_scr[...] = full_ref[:, 2 * width : 3 * width]
    length = z_ref.shape[0]
    core = where_ref[1] & 1
    for is_mine, first in halves(core, length):
        rows = pl.ds(pl.multiple_of(first, length // 2), length // 2)
        part = dot_nt(z_ref[rows, :], w_scr[...]).astype(BF)
        if is_mine:
            mine_ref[...] = part
        else:
            theirs_ref[...] = part


SPAN = 256


def back_kernel(width, ready, ship, where_ref, a_ref, b_ref, c_ref, d_ref, h_ref, cot_ref, gain_ref, full_ref, q_ref, k_ref, v_ref, o_ref, ab_ref,
                n1_ref, cos_ref, sin_ref, dh_ref, mine_ref, theirs_ref, *rest):
    grad_ref, low_scr, do_scr, w_scr, km_scr, qm_scr, dk_scr, dv_scr, dp_scr = rest[-9:]
    length = h_ref.shape[0]
    half = length // 2
    heads = width // HEAD_DIM
    core = where_ref[1] & 1
    ready(gain_ref, full_ref, a_ref, b_ref, c_ref, d_ref, h_ref, cot_ref)
    gain = gain_ref[0:1, :]
    for s in range(4):
        w_scr[s] = full_ref[:, s * width : (s + 1) * width]
    for is_mine, first in halves(core, length):
        low, high = (a_ref, b_ref) if is_mine else (c_ref, d_ref)

        def step(i, _):
            at = pl.multiple_of(i * CHUNK, CHUNK)
            rows = pl.ds(pl.multiple_of(first + at, CHUNK), CHUNK)
            here = pl.ds(at, CHUNK)
            grad = low[here, :].astype(F32) + high[here, :].astype(F32)
            hat, inverse = normalize(h_ref[rows, :])
            total = cot_ref[rows, :].astype(F32) + norm_back(grad, gain, hat, inverse)
            dh_ref[rows, :] = total
            narrow = total.astype(BF)
            low_scr[rows, :] = narrow
            do_scr[rows, :] = dot(narrow, w_scr[3]).astype(BF)
            return 0

        lax.fori_loop(0, half // CHUNK, step, 0)
    ship(dh_ref)
    turn = turn_matrix(width)
    ready(q_ref, k_ref, v_ref, o_ref, ab_ref)
    kt = (-dot(k_ref[...], turn)).astype(BF)
    qt = (-dot(q_ref[...], turn)).astype(BF)
    for h in range(heads):
        km_scr[h, :, 0:width] = only_head(k_ref[...], h)
        km_scr[h, :, 256 : 256 + width] = only_head(kt, h)
        qm_scr[h, :, 0:width] = only_head(q_ref[...], h)
        qm_scr[h, :, 256 : 256 + width] = only_head(qt, h)

    ready(cos_ref, sin_ref)
    for i in range(length // SPAN):
        rows = pl.ds(i * SPAN, SPAN)
        grad_o = do_scr[rows, :]
        product = grad_o.astype(F32) * o_ref[rows, :].astype(F32)
        dq = None
        dk = None
        dv = None
        for h in range(heads):
            own = only_head(grad_o, h)
            delta = jnp.sum(only_head(product, h), axis=-1, keepdims=True)
            da = dot_nt(own, v_ref[...])
            probs = ab_ref[h, rows, :]
            term = dot_tn(probs, own)
            dv = term if dv is None else dv + term
            ds = (probs.astype(F32) * (da - delta) * HEAD_DIM ** (-0.5)).astype(BF)
            term = dot(ds, km_scr[h])
            dq = term if dq is None else dq + term
            term = dot_tn(ds, qm_scr[h, rows, :])
            dk = term if dk is None else dk + term
        dp_scr[0, rows, :] = (dq[:, :width] * cos_ref[rows, :] + dq[:, 256 : 256 + width] * sin_ref[rows, :]).astype(BF)
        if i == 0:
            dk_scr[...] = dk
            dv_scr[...] = dv
        else:
            dk_scr[...] += dk
            dv_scr[...] += dv
    dp_scr[1] = (dk_scr[:, :width] * cos_ref[...] + dk_scr[:, 256 : 256 + width] * sin_ref[...]).astype(BF)
    dp_scr[2] = dv_scr[...].astype(BF)
    ready(n1_ref)
    for s in range(3):
        grad_ref[:, s * width : (s + 1) * width] = dot_tn(n1_ref[...], dp_scr[s]).astype(BF)
    grad_ref[:, 3 * width :] = dot_tn(low_scr[...], o_ref[...]).astype(BF)
    emit_grad(where_ref, grad_ref, rest[:-9])
    for ref in rest[:-9]:
        ship(ref)
    for is_mine, first in halves(core, length):
        out = mine_ref if is_mine else theirs_ref
        rows = pl.ds(pl.multiple_of(first, half), half)
        part = dot_nt(dp_scr[0, rows, :], w_scr[0]) + dot_nt(dp_scr[1, rows, :], w_scr[1]) + dot_nt(dp_scr[2, rows, :], w_scr[2])
        out[...] = part.astype(BF)
        ship(out)


def output_kernel(ready, ship, where_ref, h_ref, a_ref, b_ref, c_ref, d_ref, out_ref, sign_ref):
    sign_ref[...] = jnp.zeros_like(sign_ref)
    half = h_ref.shape[0] // 2
    core = where_ref[1] & 1
    ready(h_ref, a_ref, b_ref, c_ref, d_ref)
    for is_mine, first in halves(core, 2 * half):
        low, high = (a_ref, b_ref) if is_mine else (c_ref, d_ref)
        rows = pl.ds(pl.multiple_of(first, half), half)
        out_ref[rows, :] = h_ref[rows, :] + (low[...].astype(F32) + high[...].astype(F32))
        ship(out_ref, rows)


def input_grad_kernel(ready, ship, where_ref, tok_ref, dh_ref, gain_ref, a_ref, b_ref, c_ref, d_ref, grad_ref, sign_ref):
    sign_ref[...] = jnp.zeros_like(sign_ref)
    half = dh_ref.shape[0] // 2
    core = where_ref[1] & 1
    ready(dh_ref, tok_ref, gain_ref, a_ref, b_ref, c_ref, d_ref)
    gain = gain_ref[0:1, :]
    for is_mine, first in halves(core, 2 * half):
        low, high = (a_ref, b_ref) if is_mine else (c_ref, d_ref)

        def step(i, _):
            at = pl.multiple_of(i * CHUNK, CHUNK)
            rows = pl.ds(pl.multiple_of(first + at, CHUNK), CHUNK)
            here = pl.ds(at, CHUNK)
            grad = low[here, :].astype(F32) + high[here, :].astype(F32)
            hat, inverse = normalize(tok_ref[rows, :].astype(F32))
            grad_ref[rows, :] = dh_ref[rows, :] + norm_back(grad, gain, hat, inverse)
            return 0

        lax.fori_loop(0, half // CHUNK, step, 0)
        ship(grad_ref, pl.ds(pl.multiple_of(first, half), half))


def total_of(refs):
    total = refs[0][...].astype(F32)
    for ref in refs[1:]:
        total = total + ref[...].astype(F32)
    return total


def step_kernel(groups, plan, *refs):
    at = 0
    shards = []
    for count in groups:
        shards.append(total_of(refs[at : at + count]))
        at += count
    outs = refs[at + 3 * len(plan) :]
    for leaf, (transposed, slices) in enumerate(plan):
        w_ref, f_ref, s_ref = refs[at : at + 3]
        at += 3
        g_out, d_out, f_out, s_out = outs[4 * leaf : 4 * leaf + 4]
        for i, (group, first, columns) in enumerate(slices):
            grad = shards[group][:, first : first + columns]
            if transposed:
                grad = grad.T
            where = (i,) if len(w_ref.shape) == 3 else Ellipsis
            delta, first_new, second_new = adamw(w_ref[where], grad, f_ref[where], s_ref[where], decay_rate)
            g_out[where] = grad
            d_out[where] = delta
            f_out[where] = first_new
            s_out[where] = second_new


def gain_kernel(columns, gain_row, w_ref, gains_ref, *refs):
    shard = total_of(refs[:-1])
    total = jnp.zeros((shard.shape[0], 1), F32)
    for i, first in enumerate(columns):
        width = w_ref.shape[2]
        narrow = w_ref[i].astype(BF).astype(F32)
        total = total + jnp.sum(narrow * shard[:, first : first + width], axis=-1, keepdims=True)
    wide = jnp.broadcast_to(total, (shard.shape[0], 128)).T
    gain = gains_ref[gain_row : gain_row + 1, :].astype(BF).astype(F32)
    refs[-1][...] = wide[0:8, :] / gain


def gain_call(columns, gain_row, weight, gains, pieces, deps=()):
    return call(
        lambda *refs: gain_kernel(columns, gain_row, *refs),
        [((8, gains.shape[1]), F32)],
        [weight, gains, *pieces],
        smem=0,
        deps=deps,
    )[0]


def sum_small(values):
    if lax.axis_size("tensor") != 4:
        return lax.psum(values, "tensor")
    return (values + swap(values, "tensor", 1)) + (swap(values, "tensor", 2) + swap(values, "tensor", 3))


def step_call(groups, plan, leaves):
    operands = [piece for group in groups for piece in group]
    for leaf in leaves:
        operands += list(leaf)
    outs = [(leaf[0].shape, F32) for leaf in leaves for _ in range(4)] + [((8, 128), F32)]

    def kernel(*refs):
        step_kernel([len(g) for g in groups], plan, *refs[:-1])
        refs[-1][...] = jnp.zeros_like(refs[-1])

    flat = call(kernel, outs, operands, smem=0)
    return [flat[4 * i : 4 * i + 4] for i in range(len(leaves))], flat[-1]


def local(
    tokens,
    segment_ids,
    cotangent,
    w_qkv,
    w_out,
    w_in,
    w_down,
    gains,
    first_qkv,
    first_out,
    first_in,
    first_down,
    first_gains,
    second_qkv,
    second_out,
    second_in,
    second_down,
    second_gains,
):
    heads = w_qkv.shape[2]
    hidden = w_in.shape[2]
    length, depth = tokens.shape
    half = length // 2
    where = jnp.stack([lax.axis_index("dp"), lax.axis_index("tensor")]).astype(jnp.int32)
    cosine_table, sine_values = rope_tables(length, heads)
    pieces_a, masks_a, pieces_b, masks_b, early, later = gather_pieces(
        [cosine_table, sine_values],
        lambda deps: pack(w_qkv, w_out, gains, 0, deps), lambda deps: pack(w_in, w_down, gains, 1, deps)
    )
    wide_a, wide_b = pieces_a[0].shape[-1], pieces_b[0].shape[-1]
    repeat = heads // HEAD_DIM
    segments = segment_ids.astype(jnp.int32)

    n1, q, k, v, o, ab, gain_one, mine, theirs, full_a = stream(
        lambda *refs: attention_kernel(masks_a, len(pieces_a), heads, *refs),
        [
            ((length, depth), BF),
            ((length, heads), BF),
            ((length, heads), BF),
            ((length, heads), BF),
            ((length, heads), BF),
            ((repeat, length, length), BF),
            ((8, depth), F32),
            ((half, depth), BF),
            ((half, depth), BF),
            ((depth, wide_a), BF),
        ],
        [where, tokens, segments.reshape(length, 1), segments, cosine_table, sine_values, *pieces_a],
        [pltpu.VMEM((6, depth, heads), BF), pltpu.VMEM((repeat, length, heads), BF)],
        near=(7, 8),
        far=(1,),
    )
    terms = reduce_finish(reduce_start(mine, gate(theirs, early) if early else theirs, later))
    middle, n2, z, du, dv2, gain_two, mine, theirs, full_b = stream(
        lambda *refs: feed_kernel(masks_b, len(pieces_b), hidden, *refs),
        [
            ((length, depth), F32),
            ((length, depth), BF),
            ((length, hidden), BF),
            ((length, hidden), BF),
            ((length, hidden), BF),
            ((8, depth), F32),
            ((half, depth), BF),
            ((half, depth), BF),
            ((depth, wide_b), BF),
        ],
        [where, tokens, cotangent, *terms, *pieces_b],
        [pltpu.VMEM((3, depth, hidden), BF)],
        near=(6, 7),
        far=(1, 2),
    )
    chip = reduce_start(mine, theirs)
    in_outs, down_outs = grad_outs(depth, 2 * hidden), far_outs(depth, hidden)
    split = len(in_outs)
    out_mine, out_theirs, *grads = stream(
        lambda *refs: feed_grad_kernel(hidden, split, *refs),
        [((half, depth), BF), ((half, depth), BF)] + in_outs + down_outs,
        [where, n2, du, dv2, cotangent, z, full_b],
        [pltpu.VMEM((depth, 2 * hidden), BF), pltpu.VMEM((depth, hidden), BF), pltpu.VMEM((depth, hidden), BF)],
        deps=[chip],
        near=range(2 + split + len(down_outs)),
        far=range(1, 7),
    )
    out_chip = reduce_start(out_mine, out_theirs)
    terms = reduce_finish(chip, [out_mine])
    in_pieces, in_got, _unused = scatter_start(where, grads[:split])
    down_finish, down_got = scatter_far_first(where, grads[split:])
    out_chip = gate(out_chip, terms[1:2])
    out_got = swap(out_chip, "tensor", 2)
    small = ((8, 128), F32)
    whole = ((length, depth), F32)
    width = 4 * heads
    attn_outs = grad_outs(depth, width)
    dh, mine, theirs, *grad_attn = stream(
        lambda *refs: back_kernel(heads, *refs),
        [((length, depth), F32), ((half, depth), BF), ((half, depth), BF)] + attn_outs,
        [where, *terms, middle, cotangent, gain_two, full_a, q, k, v, o, ab, n1, cosine_table, sine_values],
        [
            pltpu.VMEM((depth, width), BF),
            pltpu.VMEM((length, depth), BF),
            pltpu.VMEM((length, heads), BF),
            pltpu.VMEM((4, depth, heads), BF),
            pltpu.VMEM((repeat, length, 512), BF),
            pltpu.VMEM((repeat, length, 512), BF),
            pltpu.VMEM((length, 512), F32),
            pltpu.VMEM((length, heads), F32),
            pltpu.VMEM((3, length, heads), BF),
        ],
        near=range(1, 3 + len(attn_outs)),
        far=range(5, 17),
        vmem=44,
    )
    theirs = gate(theirs, [out_got] + in_got + down_got)
    out_terms = [out_chip, out_got, swap(out_chip, "tensor", 1), swap(out_got, "tensor", 1)]
    attn_pieces, _unused, attn_pair = scatter_start(where, grad_attn, in_pieces[1:])
    down_pieces = down_finish(attn_pair)
    output, sign = stream(
        output_kernel, [whole, small], [where, middle, *out_terms], near=(1,), far=(1,), vmem=10, deps=attn_pair
    )
    signs = [sign]
    terms = reduce_finish(reduce_start(mine, theirs, out_terms[2:]), in_pieces[1:])
    grad_tokens, sign = stream(
        input_grad_kernel, [whole, small], [where, tokens, dh, gain_one, *terms], near=(1,), far=(1, 2), vmem=10
    )
    signs.append(sign)

    gain_sum_two = gain_call([0, hidden], 1, w_in, gains, in_pieces)
    (leaf_in, leaf_down), sign = step_call(
        [in_pieces, down_pieces],
        [(False, [(0, 0, hidden), (0, hidden, hidden)]), (True, [(1, 0, hidden)])],
        [(w_in, first_in, second_in), (w_down, first_down, second_down)],
    )
    gain_sum_one = gain_call([0, heads, 2 * heads], 0, w_qkv, gains, attn_pieces, signs + [sign])
    share_gains = sum_small(jnp.concatenate([gain_sum_one[0:1], gain_sum_two[0:1]], axis=0))
    (leaf_qkv, leaf_out), _unused = step_call(
        [attn_pieces],
        [(False, [(0, 0, heads), (0, heads, heads), (0, 2 * heads, heads)]), (True, [(0, 3 * heads, heads)])],
        [(w_qkv, first_qkv, second_qkv), (w_out, first_out, second_out)],
    )
    n_gains, m_gains, s_gains = adamw(gains, share_gains, first_gains, second_gains, 0.0)
    by_kind = list(zip(leaf_qkv, leaf_out, leaf_in, leaf_down, (share_gains, n_gains, m_gains, s_gains)))
    return (output, grad_tokens, *by_kind[0], *by_kind[1], *by_kind[2], *by_kind[3])


def solution(mesh):
    placed = (
        P("dp", None),
        P("dp", None),
        P("dp", None),
        P(None, "dp", "tensor"),
        P("tensor", "dp"),
        P(None, "dp", "tensor"),
        P("tensor", "dp"),
        P(None, "dp"),
        P(None, "dp", "tensor"),
        P("tensor", "dp"),
        P(None, "dp", "tensor"),
        P("tensor", "dp"),
        P(None, "dp"),
        P(None, "dp", "tensor"),
        P("tensor", "dp"),
        P(None, "dp", "tensor"),
        P("tensor", "dp"),
        P(None, "dp"),
    )
    return jax.shard_map(
        local,
        mesh=mesh,
        in_specs=placed,
        out_specs=(
            P("dp", None),
            P("dp", None),
            P(None, "dp", "tensor"),
            P("tensor", "dp"),
            P(None, "dp", "tensor"),
            P("tensor", "dp"),
            P(None, "dp"),
            P(None, "dp", "tensor"),
            P("tensor", "dp"),
            P(None, "dp", "tensor"),
            P("tensor", "dp"),
            P(None, "dp"),
            P(None, "dp", "tensor"),
            P("tensor", "dp"),
            P(None, "dp", "tensor"),
            P("tensor", "dp"),
            P(None, "dp"),
            P(None, "dp", "tensor"),
            P("tensor", "dp"),
            P(None, "dp", "tensor"),
            P("tensor", "dp"),
            P(None, "dp"),
        ),
        check_vma=False,
    )
```

```python
import jax
import jax.numpy as jnp
from jax import lax
from jax.experimental import pallas as pl
from jax.experimental.pallas import tpu as pltpu
from jax.sharding import PartitionSpec as P

HEAD_DIM = 64
STEP = 3


norm_eps = 1e-05
rope_base = 160000.0
learn_rate = 0.01
beta_one = 0.9
beta_two = 0.98
adam_eps = 1e-08
decay_rate = 0.01
big_negative = -1e30

BF = jnp.bfloat16
F32 = jnp.float32


def rope_tables(count):
    half_dim = HEAD_DIM // 2
    lane = jnp.arange(2 * HEAD_DIM)
    frequency = rope_base ** (-((lane % half_dim).astype(jnp.float32) * 2.0 / HEAD_DIM))
    angles = jnp.arange(count, dtype=jnp.float32)[:, None] * frequency[None, :]
    return jnp.where(lane[None, :] < HEAD_DIM, jnp.cos(angles), jnp.sin(angles))


def gelu_parts(inputs):
    normal_cdf = 0.5 * (1.0 + lax.erf(inputs * 0.7071067811865476))
    density = jnp.exp(-0.5 * inputs * inputs) * 0.3989422804014327
    return (inputs * normal_cdf, normal_cdf + inputs * density)


def adamw(weight, gradient, first_mom, second, decay_now):
    first_new = beta_one * first_mom + (1.0 - beta_one) * gradient
    second_new = beta_two * second + (1.0 - beta_two) * gradient * gradient
    corr_one = 1.0 - beta_one**STEP
    corr_two = 1.0 - beta_two**STEP
    update = (
        first_new / corr_one / (jnp.sqrt(second_new / corr_two) + adam_eps) + decay_now * weight
    )
    return (-learn_rate * update, first_new, second_new)


def swap(values, axis, mask):
    count = lax.axis_size(axis)
    return lax.ppermute(values, axis, [(i, i ^ mask) for i in range(count)])


def pack(first, second, gains, row, deps=()):
    rows = first.shape[1]
    used = first.shape[0] * first.shape[2] + second.shape[0] + 1
    width = -(-used // 128) * 128
    return stream(
        lambda *refs: pack_kernel(row, *refs), [((rows, width), BF)], [first, second, gains], smem=0, deps=deps, vmem=16, near=(0,), far=(0, 1, 2)
    )[0]


def gather_pieces(beside, pack_a, pack_b):
    if lax.axis_size("dp") != 8:
        full_a = lax.all_gather(pack_a(()), "dp", axis=0, tiled=True)
        full_b = lax.all_gather(pack_b(()), "dp", axis=0, tiled=True)
        return [full_a], None, [full_b], None, [], []
    order = (4, 6, 2)
    shard_a, shard_b = pack_a(()), pack_b(())
    far_one, far_two, near = [swap(shard_a, "dp", m) for m in order]
    side = swap(shard_a, "dp", 1)
    sides = [side, swap(gate(side, beside), "dp", 2), swap(far_one, "dp", 1), swap(far_two, "dp", 1)]
    pieces_a = [shard_a, near, far_one, far_two] + sides
    masks_a = [[m] for m in (0, 2, 4, 6, 1, 3, 5, 7)]
    shard_b = gate(shard_b, [far_one, far_two, sides[1]])
    column = [swap(shard_b, "dp", m) for m in order]
    side = swap(shard_b, "dp", 1)
    stacked = stack(column)
    pieces_b = [shard_b, stacked, side, swap(stacked, "dp", 1)]
    return pieces_a, masks_a, pieces_b, [[0], [4, 6, 2], [1], [5, 7, 3]], column + [side], [stacked]


def pair_kernel(where_ref, keep_ref, got_ref, own_ref, *far_refs):
    level = where_ref[0] >> 1
    for m, ref in enumerate((own_ref,) + far_refs):
        at = level ^ m
        ref[...] = (keep_ref[at].astype(F32) + got_ref[at].astype(F32)).astype(BF)


def scatter_start(where, grads, deps=()):
    if len(grads) == 1:
        return [lax.psum_scatter(grads[0].astype(F32), "dp", scatter_dimension=0, tiled=True)], [], []
    keep, send = grads
    got = swap(send, "dp", 1)
    parts = call(pair_kernel, [(keep.shape[1:], BF)] * keep.shape[0], [where, keep, got], deps=deps)
    return [parts[0]] + [swap(parts[m], "dp", 2 * m) for m in range(1, len(parts))], [got], [parts[0]]


def grad_outs(depth, width):
    count = lax.axis_size("dp")
    if count != 8:
        return [((depth, width), BF)]
    return [((count // 2, depth // count, width), BF)] * 2


def emit_grad(where_ref, grad_scr, refs):
    if len(refs) == 1:
        refs[0][...] = grad_scr[...]
        return
    keep_ref, send_ref = refs
    levels, rows, _width = keep_ref.shape
    odd = where_ref[0] & 1
    for level in range(levels):
        at = pl.multiple_of((2 * level + odd) * rows, rows)
        keep_ref[level] = grad_scr[pl.ds(at, rows), :]
        at = pl.multiple_of((2 * level + 1 - odd) * rows, rows)
        send_ref[level] = grad_scr[pl.ds(at, rows), :]


def add_kernel(a_ref, b_ref, out_ref):
    out_ref[...] = (a_ref[...].astype(F32) + b_ref[...].astype(F32)).astype(BF)


def reduce_start(mine, theirs, deps=()):
    got = swap(theirs, "tensor", 1)
    return call(add_kernel, [(mine.shape, BF)], [mine, got], smem=0, deps=deps)[0]


def reduce_finish(chip, deps=()):
    got = swap(chip, "tensor", 2)
    if deps:
        got = gate(got, deps)
    return [chip, got, swap(chip, "tensor", 1), swap(got, "tensor", 1)]


def dot(a, b):
    return jnp.dot(a, b, preferred_element_type=F32)


def dot_nt(a, b):
    return lax.dot_general(a, b, (((1,), (1,)), ((), ())), preferred_element_type=F32)


def dot_tn(a, b):
    return lax.dot_general(a, b, (((0,), (0,)), ((), ())), preferred_element_type=F32)


def head_mask(rows, width, head):
    lane = lax.broadcasted_iota(jnp.int32, (rows, width), 1)
    return (lane >= head * HEAD_DIM) & (lane < (head + 1) * HEAD_DIM)


def only_head(values, head):
    return jnp.where(head_mask(values.shape[0], values.shape[1], head), values, jnp.zeros_like(values))


def spread(table, width):
    count = width // HEAD_DIM
    cosine, sine = table[:, :HEAD_DIM], table[:, HEAD_DIM:]
    return jnp.concatenate([cosine] * count, axis=1), jnp.concatenate([sine] * count, axis=1)


def turn_matrix(width):
    half = HEAD_DIM // 2
    source = lax.broadcasted_iota(jnp.int32, (width, width), 0)
    target = lax.broadcasted_iota(jnp.int32, (width, width), 1)
    low = (target & (HEAD_DIM - 1)) < half
    value = jnp.where(low & (source == target + half), -1.0, 0.0)
    return (value + jnp.where((~low) & (source == target - half), 1.0, 0.0)).astype(BF)


def column_as_row(block, lane):
    pick = (lax.broadcasted_iota(jnp.int32, (16, block.shape[1]), 1) == lane).astype(F32).astype(BF)
    return dot_nt(pick, block)[0:1]


def normalize(values):
    center = values - jnp.mean(values, axis=-1, keepdims=True)
    inverse = lax.rsqrt(jnp.mean(center * center, axis=-1, keepdims=True) + norm_eps)
    return center * inverse, inverse


def norm_back(grad_norm, gain_row, normed, inverse):
    scaled = grad_norm * gain_row
    return (
        scaled
        - jnp.mean(scaled, axis=-1, keepdims=True)
        - normed * jnp.mean(scaled * normed, axis=-1, keepdims=True)
    ) * inverse


def place_pieces(where_ref, pieces, masks, out_ref):
    if masks is None:
        out_ref[...] = pieces[0][...]
        return
    for piece, own in zip(pieces, masks):
        rows = piece.shape[-2]
        for i, mask in enumerate(own):
            at = pl.multiple_of((where_ref[0] ^ mask) * rows, rows)
            out_ref[pl.ds(at, rows), :] = piece[i] if len(piece.shape) == 3 else piece[...]


def call(kernel, outs, operands, scratch=(), smem=1, deps=(), vmem=8):
    count = len(operands)

    def body(*refs):
        kernel(*refs[:count], *refs[count + len(deps) :])

    return pl.pallas_call(
        body,
        out_shape=[jax.ShapeDtypeStruct(s, d) for s, d in outs],
        in_specs=[pl.BlockSpec(memory_space=pltpu.SMEM)] * smem
        + [pl.BlockSpec()] * (count - smem)
        + [pl.BlockSpec(memory_space=pl.ANY)] * len(deps),
        out_specs=[pl.BlockSpec()] * len(outs),
        scratch_shapes=list(scratch),
        compiler_params=pltpu.CompilerParams(vmem_limit_bytes=vmem * 1024 * 1024),
    )(*operands, *deps)


def stream(kernel, outs, operands, scratch=(), smem=1, deps=(), vmem=40, near=(), far=(), here=(), stages=(), cost=None):
    count, total = len(operands), len(outs)
    moved = [i for i in range(smem, count) if i not in here]
    late = len(moved)
    room = [pltpu.VMEM(operands[i].shape, operands[i].dtype) for i in moved]
    room += [pltpu.VMEM(*out) for i, out in enumerate(outs) if i not in near]
    gone = total - len(near)

    def body(*refs):
        given, results = refs[:count], refs[count + len(deps) : count + len(deps) + total]
        own = refs[count + len(deps) + total :]
        flags, own = own[-1], own[:-1]
        own, held, made = own[: -late - gone], own[-late - gone : -gone or None], list(own[len(own) - gone :])
        for i in sorted(near):
            made.insert(i, results[i])
        copies = [pltpu.make_async_copy(given[i], held[n], flags.at[n]) for n, i in enumerate(moved)]
        waiting = {id(ref): copy for ref, copy in zip(held, copies)}
        inputs = list(given[smem:])
        for n, i in enumerate(moved):
            inputs[i - smem] = held[n]
        queue = list(zip(moved, copies))

        def launch():
            first = True
            while queue and (first or queue[0][0] not in stages):
                queue.pop(0)[1].start()
                first = False

        place = {id(ref): i for i, ref in enumerate(made) if i not in near}
        sent = []
        shipped = {}

        def ready(*wanted):
            for ref in wanted:
                copy = waiting.pop(id(ref), None)
                while any(copy is other for _unused, other in queue):
                    launch()
                if copy is not None:
                    copy.wait()
            launch()

        def ship(ref, rows=None):
            i = place.get(id(ref))
            if i is None:
                return
            part = shipped.get(i, 0)
            shipped[i] = part + 1
            source, target = (ref, results[i]) if rows is None else (ref.at[rows], results[i].at[rows])
            copy = pltpu.make_async_copy(source, target, flags.at[late + 2 * i + part])
            copy.start()
            sent.append(copy)

        launch()
        kernel(ready, ship, *refs[:smem], *inputs, *made, *own)
        ready(*held)
        for i, ref in enumerate(made):
            if i not in shipped:
                ship(ref)
        for copy in sent:
            copy.wait()

    anywhere = pl.BlockSpec(memory_space=pl.ANY)
    pinned = [pltpu.with_memory_space_constraint(x, pltpu.HBM) if i in far else x for i, x in enumerate(operands)]
    return pl.pallas_call(
        body,
        out_shape=[jax.ShapeDtypeStruct(*out) if i in near else pltpu.HBM(*out) for i, out in enumerate(outs)],
        in_specs=[pl.BlockSpec(memory_space=pltpu.SMEM)] * smem
        + [pl.BlockSpec() if i in here else anywhere for i in range(smem, count)]
        + [anywhere] * len(deps),
        out_specs=[pl.BlockSpec() if i in near else anywhere for i in range(total)],
        scratch_shapes=list(scratch) + room + [pltpu.SemaphoreType.DMA((late + 2 * total,))],
        compiler_params=pltpu.CompilerParams(vmem_limit_bytes=vmem * 1024 * 1024),
        cost_estimate=None if cost is None else pl.CostEstimate(flops=cost, bytes_accessed=cost, transcendentals=0),
    )(*pinned, *deps)


def gate(value, deps):
    if not deps:
        return value
    return pl.pallas_call(
        lambda *refs: None,
        out_shape=jax.ShapeDtypeStruct(value.shape, value.dtype),
        in_specs=[pl.BlockSpec(memory_space=pl.ANY)] * (1 + len(deps)),
        out_specs=pl.BlockSpec(memory_space=pl.ANY),
        input_output_aliases={0: 0},
        compiler_params=pltpu.CompilerParams(vmem_limit_bytes=1024 * 1024),
    )(value, *deps)


def pack_kernel(row, ready, ship, first_ref, second_ref, gain_ref, out_ref):
    width = out_ref.shape[1]
    ready(first_ref, second_ref, gain_ref)
    gain = jnp.broadcast_to(gain_ref[row : row + 1, :], (8, gain_ref.shape[1])).T
    parts = [first_ref[i] for i in range(first_ref.shape[0])] + [second_ref[...].T, gain[:, 0:1]]
    used = sum(part.shape[1] for part in parts)
    parts.append(jnp.zeros((out_ref.shape[0], width - used), F32))
    out_ref[...] = jnp.concatenate(parts, axis=1).astype(BF)


def stack(pieces):
    def body(*refs):
        flags = refs[-1]
        copies = [pltpu.make_async_copy(ref, refs[-2].at[i], flags.at[i]) for i, ref in enumerate(refs[:-2])]
        for copy in copies:
            copy.start()
        for copy in copies:
            copy.wait()

    anywhere = pl.BlockSpec(memory_space=pl.ANY)
    return pl.pallas_call(
        body,
        out_shape=jax.ShapeDtypeStruct((len(pieces),) + pieces[0].shape, pieces[0].dtype),
        in_specs=[anywhere] * len(pieces),
        out_specs=anywhere,
        scratch_shapes=[pltpu.SemaphoreType.DMA((len(pieces),))],
        compiler_params=pltpu.CompilerParams(vmem_limit_bytes=1024 * 1024),
    )(*pieces)


CHUNK = 256


def halves(core, length):
    half = length // 2
    return ((False, (1 - core) * half), (True, core * half))


def attention_kernel(masks, count, width, ready, ship, where_ref, tok_ref, segc_ref, segr_ref, table_ref, *rest):
    pieces = rest[:count]
    n1_ref, q_ref, k_ref, v_ref, o_ref, ab_ref, gain_ref, mine_ref, theirs_ref, full_ref, w_scr, vm_scr = rest[count:]
    length = tok_ref.shape[0]
    heads = width // HEAD_DIM
    ready(*pieces)
    place_pieces(where_ref, pieces, masks, full_ref)
    ship(full_ref)
    gain = column_as_row(full_ref[:, 4 * width :], 0)
    gain_ref[...] = jnp.broadcast_to(gain, gain_ref.shape)
    turn = turn_matrix(width)
    for s in range(3):
        w_scr[s] = full_ref[:, s * width : (s + 1) * width]
    for s in range(2):
        w_scr[3 + s] = dot(w_scr[s], turn).astype(BF)
    w_scr[5] = full_ref[:, 3 * width : 4 * width]
    ready(tok_ref, table_ref, segc_ref, segr_ref)

    def project(i, _):
        rows = pl.ds(pl.multiple_of(i * CHUNK, CHUNK), CHUNK)
        hat, _unused = normalize(tok_ref[rows, :].astype(F32))
        normed = (hat * gain).astype(BF)
        n1_ref[rows, :] = normed
        cosine, sine = spread(table_ref[rows, :], width)
        q_ref[rows, :] = (dot(normed, w_scr[0]) * cosine + dot(normed, w_scr[3]) * sine).astype(BF)
        k_ref[rows, :] = (dot(normed, w_scr[1]) * cosine + dot(normed, w_scr[4]) * sine).astype(BF)
        v_ref[rows, :] = dot(normed, w_scr[2]).astype(BF)
        return 0

    lax.fori_loop(0, length // CHUNK, project, 0)
    for ref in (n1_ref, q_ref, k_ref, v_ref):
        ship(ref)
    for h in range(heads):
        vm_scr[h] = only_head(v_ref[...], h)
    core = where_ref[1] & 1
    for is_mine, first in halves(core, length):
        def attend(i, _):
            at = pl.multiple_of(i * CHUNK, CHUNK)
            rows = pl.ds(pl.multiple_of(first + at, CHUNK), CHUNK)
            allowed = segc_ref[rows, :] == segr_ref[...]
            query, keys = q_ref[rows, :], k_ref[...]
            total = jnp.zeros((CHUNK, width), F32)
            for h in range(heads):
                logits = dot_nt(only_head(query, h), keys) * HEAD_DIM ** (-0.5)
                logits = jnp.where(allowed, logits, big_negative)
                expd = jnp.exp(logits - jnp.max(logits, axis=-1, keepdims=True))
                probs = (expd / jnp.sum(expd, axis=-1, keepdims=True)).astype(BF)
                ab_ref[h, rows, :] = probs
                total = total + dot(probs, vm_scr[h])
            attended = total.astype(BF)
            o_ref[rows, :] = attended
            part = dot_nt(attended, w_scr[5]).astype(BF)
            if is_mine:
                mine_ref[pl.ds(at, CHUNK), :] = part
            else:
                theirs_ref[pl.ds(at, CHUNK), :] = part
            return 0

        lax.fori_loop(0, length // 2 // CHUNK, attend, 0)
        ship(mine_ref if is_mine else theirs_ref)
        ship(ab_ref, (slice(None), pl.ds(pl.multiple_of(first, length // 2), length // 2)))


def feed_kernel(masks, count, width, ready, ship, where_ref, tok_ref, cot_ref, a_ref, b_ref, c_ref, d_ref, *rest):
    pieces = rest[:count]
    (h_ref, n2_ref, z_ref, du_ref, dv_ref, gain_ref, mine_ref, theirs_ref, wd_ref, full_ref, w_scr) = rest[count:]
    length = tok_ref.shape[0]
    core = where_ref[1] & 1
    ready(*pieces)
    place_pieces(where_ref, pieces, masks, full_ref)
    last = 3 * width // 128 * 128
    gain = column_as_row(full_ref[:, last:], 3 * width - last)
    gain_ref[...] = jnp.broadcast_to(gain, gain_ref.shape)
    for s in range(2):
        w_scr[s] = full_ref[:, s * width : (s + 1) * width]
    wd_ref[...] = full_ref[:, 2 * width : 3 * width]
    ship(wd_ref)
    ready(tok_ref, cot_ref, a_ref, b_ref, c_ref, d_ref)
    for is_mine, first in halves(core, length):
        low, high = (a_ref, b_ref) if is_mine else (c_ref, d_ref)

        def step(i, _):
            at = pl.multiple_of(i * CHUNK, CHUNK)
            rows = pl.ds(pl.multiple_of(first + at, CHUNK), CHUNK)
            here = pl.ds(at, CHUNK)
            middle = tok_ref[rows, :].astype(F32) + (low[here, :].astype(F32) + high[here, :].astype(F32))
            h_ref[rows, :] = middle
            hat, _unused = normalize(middle)
            normed = (hat * gain).astype(BF)
            n2_ref[rows, :] = normed
            up, gate = dot(normed, w_scr[0]), dot(normed, w_scr[1])
            value, slope = gelu_parts(up)
            z_ref[rows, :] = (value * gate).astype(BF)
            back = dot(cot_ref[rows, :], wd_ref[...])
            du, dv = (back * gate * slope).astype(BF), (back * value).astype(BF)
            du_ref[rows, :] = du
            dv_ref[rows, :] = dv
            part = dot_nt(du, w_scr[0]) + dot_nt(dv, w_scr[1])
            part = part.astype(BF)
            if is_mine:
                mine_ref[here, :] = part
            else:
                theirs_ref[here, :] = part
            return 0

        lax.fori_loop(0, length // 2 // CHUNK, step, 0)
        rows = pl.ds(pl.multiple_of(first, length // 2), length // 2)
        for ref in (h_ref, n2_ref, z_ref, du_ref, dv_ref):
            ship(ref, rows)
        ship(mine_ref if is_mine else theirs_ref)


def feed_grad_kernel(width, ready, ship, where_ref, n2_ref, du_ref, dv_ref, cot_ref, z_ref, wd_ref, mine_ref, theirs_ref, *rest):
    grad_ref = rest[-1]
    ready(n2_ref, du_ref)
    grad_ref[:, 0:width] = dot_tn(n2_ref[...], du_ref[...]).astype(BF)
    ready(dv_ref)
    grad_ref[:, width : 2 * width] = dot_tn(n2_ref[...], dv_ref[...]).astype(BF)
    ready(cot_ref, z_ref)
    grad_ref[:, 2 * width : 3 * width] = dot_tn(cot_ref[...], z_ref[...]).astype(BF)
    emit_grad(where_ref, grad_ref, rest[:-1])
    ready(wd_ref)
    length = z_ref.shape[0]
    core = where_ref[1] & 1
    for is_mine, first in halves(core, length):
        rows = pl.ds(pl.multiple_of(first, length // 2), length // 2)
        part = dot_nt(z_ref[rows, :], wd_ref[...]).astype(BF)
        if is_mine:
            mine_ref[...] = part
        else:
            theirs_ref[...] = part


SPAN = 256


def back_kernel(width, ready, ship, where_ref, a_ref, b_ref, c_ref, d_ref, h_ref, cot_ref, gain_ref, full_ref, q_ref, k_ref, v_ref, o_ref, ab_ref,
                n1_ref, table_ref, dh_ref, mine_ref, theirs_ref, *rest):
    grad_ref, low_scr, do_scr, w_scr, km_scr, qm_scr, dk_scr, dv_scr, dp_scr = rest[-9:]
    length = h_ref.shape[0]
    half = length // 2
    heads = width // HEAD_DIM
    core = where_ref[1] & 1
    ready(gain_ref, full_ref, a_ref, b_ref, c_ref, d_ref, h_ref, cot_ref)
    gain = gain_ref[0:1, :]
    for s in range(4):
        w_scr[s] = full_ref[:, s * width : (s + 1) * width]
    for is_mine, first in halves(core, length):
        low, high = (a_ref, b_ref) if is_mine else (c_ref, d_ref)

        def step(i, _):
            at = pl.multiple_of(i * CHUNK, CHUNK)
            rows = pl.ds(pl.multiple_of(first + at, CHUNK), CHUNK)
            here = pl.ds(at, CHUNK)
            grad = low[here, :].astype(F32) + high[here, :].astype(F32)
            hat, inverse = normalize(h_ref[rows, :])
            total = cot_ref[rows, :].astype(F32) + norm_back(grad, gain, hat, inverse)
            dh_ref[rows, :] = total
            narrow = total.astype(BF)
            low_scr[rows, :] = narrow
            do_scr[rows, :] = dot(narrow, w_scr[3]).astype(BF)
            return 0

        lax.fori_loop(0, half // CHUNK, step, 0)
    ship(dh_ref)
    turn = turn_matrix(width)
    ready(q_ref, k_ref, v_ref, o_ref, ab_ref)
    kt = (-dot(k_ref[...], turn)).astype(BF)
    qt = (-dot(q_ref[...], turn)).astype(BF)
    for h in range(heads):
        km_scr[h, :, 0:width] = only_head(k_ref[...], h)
        km_scr[h, :, 256 : 256 + width] = only_head(kt, h)
        qm_scr[h, :, 0:width] = only_head(q_ref[...], h)
        qm_scr[h, :, 256 : 256 + width] = only_head(qt, h)

    ready(table_ref)
    for i in range(length // SPAN):
        rows = pl.ds(i * SPAN, SPAN)
        grad_o = do_scr[rows, :]
        product = grad_o.astype(F32) * o_ref[rows, :].astype(F32)
        dq = None
        dk = None
        dv = None
        for h in range(heads):
            own = only_head(grad_o, h)
            delta = jnp.sum(only_head(product, h), axis=-1, keepdims=True)
            da = dot_nt(own, v_ref[...])
            probs = ab_ref[h, rows, :]
            term = dot_tn(probs, own)
            dv = term if dv is None else dv + term
            ds = (probs.astype(F32) * (da - delta) * HEAD_DIM ** (-0.5)).astype(BF)
            term = dot(ds, km_scr[h])
            dq = term if dq is None else dq + term
            term = dot_tn(ds, qm_scr[h, rows, :])
            dk = term if dk is None else dk + term
        cosine, sine = spread(table_ref[rows, :], width)
        dp_scr[0, rows, :] = (dq[:, :width] * cosine + dq[:, 256 : 256 + width] * sine).astype(BF)
        if i == 0:
            dk_scr[...] = dk
            dv_scr[...] = dv
        else:
            dk_scr[...] += dk
            dv_scr[...] += dv
    cosine, sine = spread(table_ref[...], width)
    dp_scr[1] = (dk_scr[:, :width] * cosine + dk_scr[:, 256 : 256 + width] * sine).astype(BF)
    dp_scr[2] = dv_scr[...].astype(BF)
    ready(n1_ref)
    for s in range(3):
        grad_ref[:, s * width : (s + 1) * width] = dot_tn(n1_ref[...], dp_scr[s]).astype(BF)
    grad_ref[:, 3 * width :] = dot_tn(low_scr[...], o_ref[...]).astype(BF)
    emit_grad(where_ref, grad_ref, rest[:-9])
    for ref in rest[:-9]:
        ship(ref)
    for is_mine, first in halves(core, length):
        out = mine_ref if is_mine else theirs_ref
        rows = pl.ds(pl.multiple_of(first, half), half)
        part = dot_nt(dp_scr[0, rows, :], w_scr[0]) + dot_nt(dp_scr[1, rows, :], w_scr[1]) + dot_nt(dp_scr[2, rows, :], w_scr[2])
        out[...] = part.astype(BF)
        ship(out)


def output_kernel(ready, ship, where_ref, h_ref, a_ref, b_ref, c_ref, d_ref, out_ref, sign_ref):
    sign_ref[...] = jnp.zeros_like(sign_ref)
    half = h_ref.shape[0] // 2
    core = where_ref[1] & 1
    ready(h_ref, a_ref, b_ref, c_ref, d_ref)
    for is_mine, first in halves(core, 2 * half):
        low, high = (a_ref, b_ref) if is_mine else (c_ref, d_ref)
        rows = pl.ds(pl.multiple_of(first, half), half)
        out_ref[rows, :] = h_ref[rows, :] + (low[...].astype(F32) + high[...].astype(F32))
        ship(out_ref, rows)


def input_grad_kernel(ready, ship, where_ref, tok_ref, dh_ref, gain_ref, a_ref, b_ref, c_ref, d_ref, grad_ref, sign_ref):
    sign_ref[...] = jnp.zeros_like(sign_ref)
    half = dh_ref.shape[0] // 2
    core = where_ref[1] & 1
    ready(dh_ref, tok_ref, gain_ref, a_ref, b_ref, c_ref, d_ref)
    gain = gain_ref[0:1, :]
    for is_mine, first in halves(core, 2 * half):
        low, high = (a_ref, b_ref) if is_mine else (c_ref, d_ref)

        def step(i, _):
            at = pl.multiple_of(i * CHUNK, CHUNK)
            rows = pl.ds(pl.multiple_of(first + at, CHUNK), CHUNK)
            here = pl.ds(at, CHUNK)
            grad = low[here, :].astype(F32) + high[here, :].astype(F32)
            hat, inverse = normalize(tok_ref[rows, :].astype(F32))
            grad_ref[rows, :] = dh_ref[rows, :] + norm_back(grad, gain, hat, inverse)
            return 0

        lax.fori_loop(0, half // CHUNK, step, 0)
        ship(grad_ref, pl.ds(pl.multiple_of(first, half), half))


def total_of(refs):
    total = refs[0][...].astype(F32)
    for ref in refs[1:]:
        total = total + ref[...].astype(F32)
    return total


def step_kernel(groups, plan, *refs):
    at = 0
    shards = []
    for count in groups:
        shards.append(total_of(refs[at : at + count]))
        at += count
    outs = refs[at + 3 * len(plan) :]
    for leaf, (transposed, slices) in enumerate(plan):
        w_ref, f_ref, s_ref = refs[at : at + 3]
        at += 3
        g_out, d_out, f_out, s_out = outs[4 * leaf : 4 * leaf + 4]
        for i, (group, first, columns) in enumerate(slices):
            grad = shards[group][:, first : first + columns]
            if transposed:
                grad = grad.T
            where = (i,) if len(w_ref.shape) == 3 else Ellipsis
            delta, first_new, second_new = adamw(w_ref[where], grad, f_ref[where], s_ref[where], decay_rate)
            g_out[where] = grad
            d_out[where] = delta
            f_out[where] = first_new
            s_out[where] = second_new


def gain_kernel(columns, gain_row, w_ref, gains_ref, *refs):
    shard = total_of(refs[:-1])
    total = jnp.zeros((shard.shape[0], 1), F32)
    for i, first in enumerate(columns):
        width = w_ref.shape[2]
        narrow = w_ref[i].astype(BF).astype(F32)
        total = total + jnp.sum(narrow * shard[:, first : first + width], axis=-1, keepdims=True)
    wide = jnp.broadcast_to(total, (shard.shape[0], 128)).T
    gain = gains_ref[gain_row : gain_row + 1, :].astype(BF).astype(F32)
    refs[-1][...] = wide[0:8, :] / gain


def gain_call(columns, gain_row, weight, gains, pieces, deps=()):
    return call(
        lambda *refs: gain_kernel(columns, gain_row, *refs),
        [((8, gains.shape[1]), F32)],
        [weight, gains, *pieces],
        smem=0,
        deps=deps,
    )[0]


def sum_small(values):
    if lax.axis_size("tensor") != 4:
        return lax.psum(values, "tensor")
    return (values + swap(values, "tensor", 1)) + (swap(values, "tensor", 2) + swap(values, "tensor", 3))


def step_call(groups, plan, leaves):
    operands = [piece for group in groups for piece in group]
    for leaf in leaves:
        operands += list(leaf)
    outs = [(leaf[0].shape, F32) for leaf in leaves for _ in range(4)] + [((8, 128), F32)]

    def kernel(*refs):
        step_kernel([len(g) for g in groups], plan, *refs[:-1])
        refs[-1][...] = jnp.zeros_like(refs[-1])

    flat = call(kernel, outs, operands, smem=0)
    return [flat[4 * i : 4 * i + 4] for i in range(len(leaves))], flat[-1]


def local(
    tokens,
    segment_ids,
    cotangent,
    w_qkv,
    w_out,
    w_in,
    w_down,
    gains,
    first_qkv,
    first_out,
    first_in,
    first_down,
    first_gains,
    second_qkv,
    second_out,
    second_in,
    second_down,
    second_gains,
):
    heads = w_qkv.shape[2]
    hidden = w_in.shape[2]
    length, depth = tokens.shape
    half = length // 2
    where = jnp.stack([lax.axis_index("dp"), lax.axis_index("tensor")]).astype(jnp.int32)
    table = rope_tables(length)
    pieces_a, masks_a, pieces_b, masks_b, early, later = gather_pieces(
        [table],
        lambda deps: pack(w_qkv, w_out, gains, 0, deps), lambda deps: pack(w_in, w_down, gains, 1, deps)
    )
    wide_a, wide_b = pieces_a[0].shape[-1], pieces_b[0].shape[-1]
    repeat = heads // HEAD_DIM
    segments = segment_ids.astype(jnp.int32)

    n1, q, k, v, o, ab, gain_one, mine, theirs, full_a = stream(
        lambda *refs: attention_kernel(masks_a, len(pieces_a), heads, *refs),
        [
            ((length, depth), BF),
            ((length, heads), BF),
            ((length, heads), BF),
            ((length, heads), BF),
            ((length, heads), BF),
            ((repeat, length, length), BF),
            ((8, depth), F32),
            ((half, depth), BF),
            ((half, depth), BF),
            ((depth, wide_a), BF),
        ],
        [where, tokens, segments.reshape(length, 1), segments, table, *pieces_a],
        [pltpu.VMEM((6, depth, heads), BF), pltpu.VMEM((repeat, length, heads), BF)],
        near=(7, 8),
        far=(1,),
        here=range(5, 5 + len(pieces_a)),
    )
    terms = reduce_finish(reduce_start(mine, gate(theirs, early) if early else theirs, later))
    middle, n2, z, du, dv2, gain_two, mine, theirs, wd = stream(
        lambda *refs: feed_kernel(masks_b, len(pieces_b), hidden, *refs),
        [
            ((length, depth), F32),
            ((length, depth), BF),
            ((length, hidden), BF),
            ((length, hidden), BF),
            ((length, hidden), BF),
            ((8, depth), F32),
            ((half, depth), BF),
            ((half, depth), BF),
            ((depth, hidden), BF),
        ],
        [where, tokens, cotangent, *terms, *pieces_b],
        [pltpu.VMEM((depth, wide_b), BF), pltpu.VMEM((2, depth, hidden), BF)],
        near=(6, 7),
        far=(1, 2),
        here=range(3, 7 + len(pieces_b)),
    )
    chip = reduce_start(mine, theirs)
    feed_outs = grad_outs(depth, 3 * hidden)
    out_mine, out_theirs, *grad_feed = stream(
        lambda *refs: feed_grad_kernel(hidden, *refs),
        [((half, depth), BF), ((half, depth), BF)] + feed_outs,
        [where, n2, du, dv2, cotangent, z, wd],
        [pltpu.VMEM((depth, 3 * hidden), BF)],
        deps=[chip],
        near=range(2 + len(feed_outs)),
        far=range(1, 7),
    )
    terms = reduce_finish(chip, [out_mine])
    feed_pieces, feed_got, _unused = scatter_start(where, grad_feed)
    out_chip = reduce_start(out_mine, out_theirs, terms[1:2])
    out_got = swap(out_chip, "tensor", 2)
    small = ((8, 128), F32)
    whole = ((length, depth), F32)
    width = 4 * heads
    attn_outs = grad_outs(depth, width)
    dh, mine, theirs, *grad_attn = stream(
        lambda *refs: back_kernel(heads, *refs),
        [((length, depth), F32), ((half, depth), BF), ((half, depth), BF)] + attn_outs,
        [where, *terms, middle, cotangent, gain_two, full_a, q, k, v, o, ab, n1, table],
        [
            pltpu.VMEM((depth, width), BF),
            pltpu.VMEM((length, depth), BF),
            pltpu.VMEM((length, heads), BF),
            pltpu.VMEM((4, depth, heads), BF),
            pltpu.VMEM((repeat, length, 512), BF),
            pltpu.VMEM((repeat, length, 512), BF),
            pltpu.VMEM((length, 512), F32),
            pltpu.VMEM((length, heads), F32),
            pltpu.VMEM((3, length, heads), BF),
        ],
        near=range(1, 3 + len(attn_outs)),
        here=range(1, 16),
        vmem=28,
        cost=1,
    )
    chip = reduce_start(mine, gate(theirs, feed_got), [out_got])
    attn_pieces, _unused, attn_pair = scatter_start(where, grad_attn, feed_pieces[1:])
    out_chip, out_got = gate(out_chip, attn_pair), gate(out_got, attn_pair)
    out_terms = [out_chip, out_got, swap(out_chip, "tensor", 1), swap(out_got, "tensor", 1)]
    output, sign = stream(
        output_kernel, [whole, small], [where, middle, *out_terms], near=(1,), far=(1,), here=range(2, 6), vmem=10, deps=attn_pair
    )
    signs = [sign]
    terms = reduce_finish(chip, feed_pieces[1:])
    grad_tokens, sign = stream(
        input_grad_kernel, [whole, small], [where, tokens, dh, gain_one, *terms], near=(1,), far=(1, 2), here=range(4, 8), vmem=10
    )
    signs.append(sign)

    gain_sum_two = gain_call([0, hidden], 1, w_in, gains, feed_pieces)
    (leaf_in, leaf_down), sign = step_call(
        [feed_pieces],
        [(False, [(0, 0, hidden), (0, hidden, hidden)]), (True, [(0, 2 * hidden, hidden)])],
        [(w_in, first_in, second_in), (w_down, first_down, second_down)],
    )
    gain_sum_one = gain_call([0, heads, 2 * heads], 0, w_qkv, gains, attn_pieces, signs + [sign])
    share_gains = sum_small(jnp.concatenate([gain_sum_one[0:1], gain_sum_two[0:1]], axis=0))
    (leaf_qkv, leaf_out), _unused = step_call(
        [attn_pieces],
        [(False, [(0, 0, heads), (0, heads, heads), (0, 2 * heads, heads)]), (True, [(0, 3 * heads, heads)])],
        [(w_qkv, first_qkv, second_qkv), (w_out, first_out, second_out)],
    )
    n_gains, m_gains, s_gains = adamw(gains, share_gains, first_gains, second_gains, 0.0)
    by_kind = list(zip(leaf_qkv, leaf_out, leaf_in, leaf_down, (share_gains, n_gains, m_gains, s_gains)))
    return (output, grad_tokens, *by_kind[0], *by_kind[1], *by_kind[2], *by_kind[3])


def solution(mesh):
    placed = (
        P("dp", None),
        P("dp", None),
        P("dp", None),
        P(None, "dp", "tensor"),
        P("tensor", "dp"),
        P(None, "dp", "tensor"),
        P("tensor", "dp"),
        P(None, "dp"),
        P(None, "dp", "tensor"),
        P("tensor", "dp"),
        P(None, "dp", "tensor"),
        P("tensor", "dp"),
        P(None, "dp"),
        P(None, "dp", "tensor"),
        P("tensor", "dp"),
        P(None, "dp", "tensor"),
        P("tensor", "dp"),
        P(None, "dp"),
    )
    return jax.shard_map(
        local,
        mesh=mesh,
        in_specs=placed,
        out_specs=(
            P("dp", None),
            P("dp", None),
            P(None, "dp", "tensor"),
            P("tensor", "dp"),
            P(None, "dp", "tensor"),
            P("tensor", "dp"),
            P(None, "dp"),
            P(None, "dp", "tensor"),
            P("tensor", "dp"),
            P(None, "dp", "tensor"),
            P("tensor", "dp"),
            P(None, "dp"),
            P(None, "dp", "tensor"),
            P("tensor", "dp"),
            P(None, "dp", "tensor"),
            P("tensor", "dp"),
            P(None, "dp"),
            P(None, "dp", "tensor"),
            P("tensor", "dp"),
            P(None, "dp", "tensor"),
            P("tensor", "dp"),
            P(None, "dp"),
        ),
        check_vma=False,
    )
```

```python
import jax
import jax.numpy as jnp
from jax import lax
from jax.experimental import pallas as pl
from jax.experimental.pallas import tpu as pltpu
from jax.sharding import PartitionSpec as P

HEAD_DIM = 64
STEP = 3


norm_eps = 1e-05
rope_base = 160000.0
learn_rate = 0.01
beta_one = 0.9
beta_two = 0.98
adam_eps = 1e-08
decay_rate = 0.01
big_negative = -1e30

BF = jnp.bfloat16
F32 = jnp.float32


def rope_tables(count):
    half_dim = HEAD_DIM // 2
    lane = jnp.arange(2 * HEAD_DIM)
    frequency = rope_base ** (-((lane % half_dim).astype(jnp.float32) * 2.0 / HEAD_DIM))
    angles = jnp.arange(count, dtype=jnp.float32)[:, None] * frequency[None, :]
    return jnp.where(lane[None, :] < HEAD_DIM, jnp.cos(angles), jnp.sin(angles))


def gelu_parts(inputs):
    normal_cdf = 0.5 * (1.0 + lax.erf(inputs * 0.7071067811865476))
    density = jnp.exp(-0.5 * inputs * inputs) * 0.3989422804014327
    return (inputs * normal_cdf, normal_cdf + inputs * density)


def adamw(weight, gradient, first_mom, second, decay_now):
    first_new = beta_one * first_mom + (1.0 - beta_one) * gradient
    second_new = beta_two * second + (1.0 - beta_two) * gradient * gradient
    corr_one = 1.0 - beta_one**STEP
    corr_two = 1.0 - beta_two**STEP
    update = (
        first_new / corr_one / (jnp.sqrt(second_new / corr_two) + adam_eps) + decay_now * weight
    )
    return (-learn_rate * update, first_new, second_new)


def swap(values, axis, mask):
    count = lax.axis_size(axis)
    return lax.ppermute(values, axis, [(i, i ^ mask) for i in range(count)])


def pack(first, second, gains, row, deps=()):
    rows = first.shape[1]
    used = first.shape[0] * first.shape[2] + second.shape[0] + 1
    width = -(-used // 128) * 128
    return stream(
        lambda *refs: pack_kernel(row, *refs), [((rows, width), BF)], [first, second, gains], smem=0, deps=deps, vmem=16, near=(0,), far=(0, 1, 2)
    )[0]


def gather_pieces(beside, pack_a, pack_b):
    if lax.axis_size("dp") != 8:
        full_a = lax.all_gather(pack_a(()), "dp", axis=0, tiled=True)
        full_b = lax.all_gather(pack_b(()), "dp", axis=0, tiled=True)
        return [full_a], None, [full_b], None, [], []
    order = (4, 6, 2)
    shard_a, shard_b = pack_a(()), pack_b(())
    far_one, far_two, near = [swap(shard_a, "dp", m) for m in order]
    side = swap(shard_a, "dp", 1)
    sides = [side, swap(gate(side, beside), "dp", 2), swap(far_one, "dp", 1), swap(far_two, "dp", 1)]
    pieces_a = [shard_a, near, far_one, far_two] + sides
    masks_a = [[m] for m in (0, 2, 4, 6, 1, 3, 5, 7)]
    shard_b = gate(shard_b, [far_one, far_two, sides[1]])
    column = [swap(shard_b, "dp", m) for m in order]
    side = swap(shard_b, "dp", 1)
    stacked = stack(column)
    pieces_b = [shard_b, stacked, side, swap(stacked, "dp", 1)]
    return pieces_a, masks_a, pieces_b, [[0], [4, 6, 2], [1], [5, 7, 3]], column + [side], [stacked]


def pair_kernel(where_ref, keep_ref, got_ref, own_ref, *far_refs):
    level = where_ref[0] >> 1
    for m, ref in enumerate((own_ref,) + far_refs):
        at = level ^ m
        ref[...] = (keep_ref[at].astype(F32) + got_ref[at].astype(F32)).astype(BF)


def scatter_start(where, grads, deps=()):
    if len(grads) == 1:
        return [lax.psum_scatter(grads[0].astype(F32), "dp", scatter_dimension=0, tiled=True)], [], []
    keep, send = grads
    got = swap(send, "dp", 1)
    parts = call(pair_kernel, [(keep.shape[1:], BF)] * keep.shape[0], [where, keep, got], deps=deps)
    came = [swap(parts[m], "dp", 2 * m) for m in reversed(range(1, len(parts)))]
    return [parts[0]] + came, [got], [parts[0]]


def grad_outs(depth, width):
    count = lax.axis_size("dp")
    if count != 8:
        return [((depth, width), BF)]
    return [((count // 2, depth // count, width), BF)] * 2


def emit_grad(where_ref, grad_scr, refs):
    if len(refs) == 1:
        refs[0][...] = grad_scr[...]
        return
    keep_ref, send_ref = refs
    levels, rows, _width = keep_ref.shape
    odd = where_ref[0] & 1
    for level in range(levels):
        at = pl.multiple_of((2 * level + odd) * rows, rows)
        keep_ref[level] = grad_scr[pl.ds(at, rows), :]
        at = pl.multiple_of((2 * level + 1 - odd) * rows, rows)
        send_ref[level] = grad_scr[pl.ds(at, rows), :]


def add_kernel(a_ref, b_ref, out_ref):
    out_ref[...] = (a_ref[...].astype(F32) + b_ref[...].astype(F32)).astype(BF)


def reduce_start(mine, theirs, deps=()):
    got = swap(theirs, "tensor", 1)
    return call(add_kernel, [(mine.shape, BF)], [mine, got], smem=0, deps=deps)[0]


def reduce_finish(chip, deps=()):
    got = swap(chip, "tensor", 2)
    if deps:
        got = gate(got, deps)
    return [chip, got, swap(chip, "tensor", 1), swap(got, "tensor", 1)]


def dot(a, b):
    return jnp.dot(a, b, preferred_element_type=F32)


def dot_nt(a, b):
    return lax.dot_general(a, b, (((1,), (1,)), ((), ())), preferred_element_type=F32)


def dot_tn(a, b):
    return lax.dot_general(a, b, (((0,), (0,)), ((), ())), preferred_element_type=F32)


def head_mask(rows, width, head):
    lane = lax.broadcasted_iota(jnp.int32, (rows, width), 1)
    return (lane >= head * HEAD_DIM) & (lane < (head + 1) * HEAD_DIM)


def only_head(values, head):
    return jnp.where(head_mask(values.shape[0], values.shape[1], head), values, jnp.zeros_like(values))


def spread(table, width):
    count = width // HEAD_DIM
    cosine, sine = table[:, :HEAD_DIM], table[:, HEAD_DIM:]
    return jnp.concatenate([cosine] * count, axis=1), jnp.concatenate([sine] * count, axis=1)


def turn_matrix(width):
    half = HEAD_DIM // 2
    source = lax.broadcasted_iota(jnp.int32, (width, width), 0)
    target = lax.broadcasted_iota(jnp.int32, (width, width), 1)
    low = (target & (HEAD_DIM - 1)) < half
    value = jnp.where(low & (source == target + half), -1.0, 0.0)
    return (value + jnp.where((~low) & (source == target - half), 1.0, 0.0)).astype(BF)


def column_as_row(block, lane):
    pick = (lax.broadcasted_iota(jnp.int32, (16, block.shape[1]), 1) == lane).astype(F32).astype(BF)
    return dot_nt(pick, block)[0:1]


def normalize(values):
    center = values - jnp.mean(values, axis=-1, keepdims=True)
    inverse = lax.rsqrt(jnp.mean(center * center, axis=-1, keepdims=True) + norm_eps)
    return center * inverse, inverse


def norm_back(grad_norm, gain_row, normed, inverse):
    scaled = grad_norm * gain_row
    return (
        scaled
        - jnp.mean(scaled, axis=-1, keepdims=True)
        - normed * jnp.mean(scaled * normed, axis=-1, keepdims=True)
    ) * inverse


def place_pieces(where_ref, pieces, masks, out_ref):
    if masks is None:
        out_ref[...] = pieces[0][...]
        return
    for piece, own in zip(pieces, masks):
        rows = piece.shape[-2]
        for i, mask in enumerate(own):
            at = pl.multiple_of((where_ref[0] ^ mask) * rows, rows)
            out_ref[pl.ds(at, rows), :] = piece[i] if len(piece.shape) == 3 else piece[...]


def call(kernel, outs, operands, scratch=(), smem=1, deps=(), vmem=8):
    count = len(operands)

    def body(*refs):
        kernel(*refs[:count], *refs[count + len(deps) :])

    return pl.pallas_call(
        body,
        out_shape=[jax.ShapeDtypeStruct(s, d) for s, d in outs],
        in_specs=[pl.BlockSpec(memory_space=pltpu.SMEM)] * smem
        + [pl.BlockSpec()] * (count - smem)
        + [pl.BlockSpec(memory_space=pl.ANY)] * len(deps),
        out_specs=[pl.BlockSpec()] * len(outs),
        scratch_shapes=list(scratch),
        compiler_params=pltpu.CompilerParams(vmem_limit_bytes=vmem * 1024 * 1024),
    )(*operands, *deps)


def stream(kernel, outs, operands, scratch=(), smem=1, deps=(), vmem=40, near=(), far=(), here=(), stages=(), cost=None):
    count, total = len(operands), len(outs)
    moved = [i for i in range(smem, count) if i not in here]
    late = len(moved)
    room = [pltpu.VMEM(operands[i].shape, operands[i].dtype) for i in moved]
    room += [pltpu.VMEM(*out) for i, out in enumerate(outs) if i not in near]
    gone = total - len(near)

    def body(*refs):
        given, results = refs[:count], refs[count + len(deps) : count + len(deps) + total]
        own = refs[count + len(deps) + total :]
        flags, own = own[-1], own[:-1]
        own, held, made = own[: -late - gone], own[-late - gone : -gone or None], list(own[len(own) - gone :])
        for i in sorted(near):
            made.insert(i, results[i])
        copies = [pltpu.make_async_copy(given[i], held[n], flags.at[n]) for n, i in enumerate(moved)]
        waiting = {id(ref): copy for ref, copy in zip(held, copies)}
        inputs = list(given[smem:])
        for n, i in enumerate(moved):
            inputs[i - smem] = held[n]
        queue = list(zip(moved, copies))

        def launch():
            first = True
            while queue and (first or queue[0][0] not in stages):
                queue.pop(0)[1].start()
                first = False

        place = {id(ref): i for i, ref in enumerate(made) if i not in near}
        sent = []
        shipped = {}

        def ready(*wanted):
            for ref in wanted:
                copy = waiting.pop(id(ref), None)
                while any(copy is other for _unused, other in queue):
                    launch()
                if copy is not None:
                    copy.wait()
            launch()

        def ship(ref, rows=None):
            i = place.get(id(ref))
            if i is None:
                return
            part = shipped.get(i, 0)
            shipped[i] = part + 1
            source, target = (ref, results[i]) if rows is None else (ref.at[rows], results[i].at[rows])
            copy = pltpu.make_async_copy(source, target, flags.at[late + 2 * i + part])
            copy.start()
            sent.append(copy)

        launch()
        kernel(ready, ship, *refs[:smem], *inputs, *made, *own)
        ready(*held)
        for i, ref in enumerate(made):
            if i not in shipped:
                ship(ref)
        for copy in sent:
            copy.wait()

    anywhere = pl.BlockSpec(memory_space=pl.ANY)
    pinned = [pltpu.with_memory_space_constraint(x, pltpu.HBM) if i in far else x for i, x in enumerate(operands)]
    return pl.pallas_call(
        body,
        out_shape=[jax.ShapeDtypeStruct(*out) if i in near else pltpu.HBM(*out) for i, out in enumerate(outs)],
        in_specs=[pl.BlockSpec(memory_space=pltpu.SMEM)] * smem
        + [pl.BlockSpec() if i in here else anywhere for i in range(smem, count)]
        + [anywhere] * len(deps),
        out_specs=[pl.BlockSpec() if i in near else anywhere for i in range(total)],
        scratch_shapes=list(scratch) + room + [pltpu.SemaphoreType.DMA((late + 2 * total,))],
        compiler_params=pltpu.CompilerParams(vmem_limit_bytes=vmem * 1024 * 1024),
        cost_estimate=None if cost is None else pl.CostEstimate(flops=cost, bytes_accessed=cost, transcendentals=0),
    )(*pinned, *deps)


def gate(value, deps):
    if not deps:
        return value
    return pl.pallas_call(
        lambda *refs: None,
        out_shape=jax.ShapeDtypeStruct(value.shape, value.dtype),
        in_specs=[pl.BlockSpec(memory_space=pl.ANY)] * (1 + len(deps)),
        out_specs=pl.BlockSpec(memory_space=pl.ANY),
        input_output_aliases={0: 0},
        compiler_params=pltpu.CompilerParams(vmem_limit_bytes=1024 * 1024),
    )(value, *deps)


def pack_kernel(row, ready, ship, first_ref, second_ref, gain_ref, out_ref):
    width = out_ref.shape[1]
    ready(first_ref, second_ref, gain_ref)
    gain = jnp.broadcast_to(gain_ref[row : row + 1, :], (8, gain_ref.shape[1])).T
    parts = [first_ref[i] for i in range(first_ref.shape[0])] + [second_ref[...].T, gain[:, 0:1]]
    used = sum(part.shape[1] for part in parts)
    parts.append(jnp.zeros((out_ref.shape[0], width - used), F32))
    out_ref[...] = jnp.concatenate(parts, axis=1).astype(BF)


def stack(pieces):
    def body(*refs):
        flags = refs[-1]
        copies = [pltpu.make_async_copy(ref, refs[-2].at[i], flags.at[i]) for i, ref in enumerate(refs[:-2])]
        for copy in copies:
            copy.start()
        for copy in copies:
            copy.wait()

    anywhere = pl.BlockSpec(memory_space=pl.ANY)
    return pl.pallas_call(
        body,
        out_shape=jax.ShapeDtypeStruct((len(pieces),) + pieces[0].shape, pieces[0].dtype),
        in_specs=[anywhere] * len(pieces),
        out_specs=anywhere,
        scratch_shapes=[pltpu.SemaphoreType.DMA((len(pieces),))],
        compiler_params=pltpu.CompilerParams(vmem_limit_bytes=1024 * 1024),
    )(*pieces)


CHUNK = 256


def halves(core, length):
    half = length // 2
    return ((False, (1 - core) * half), (True, core * half))


def attention_kernel(masks, count, width, ready, ship, where_ref, tok_ref, segc_ref, segr_ref, table_ref, *rest):
    pieces = rest[:count]
    n1_ref, q_ref, k_ref, v_ref, o_ref, ab_ref, gain_ref, mine_ref, theirs_ref, full_ref, w_scr, vm_scr = rest[count:]
    length = tok_ref.shape[0]
    heads = width // HEAD_DIM
    ready(*pieces)
    place_pieces(where_ref, pieces, masks, full_ref)
    ship(full_ref)
    gain = column_as_row(full_ref[:, 4 * width :], 0)
    gain_ref[...] = jnp.broadcast_to(gain, gain_ref.shape)
    turn = turn_matrix(width)
    for s in range(3):
        w_scr[s] = full_ref[:, s * width : (s + 1) * width]
    for s in range(2):
        w_scr[3 + s] = dot(w_scr[s], turn).astype(BF)
    w_scr[5] = full_ref[:, 3 * width : 4 * width]
    ready(tok_ref, table_ref, segc_ref, segr_ref)

    def project(i, _):
        rows = pl.ds(pl.multiple_of(i * CHUNK, CHUNK), CHUNK)
        hat, _unused = normalize(tok_ref[rows, :].astype(F32))
        normed = (hat * gain).astype(BF)
        n1_ref[rows, :] = normed
        cosine, sine = spread(table_ref[rows, :], width)
        q_ref[rows, :] = (dot(normed, w_scr[0]) * cosine + dot(normed, w_scr[3]) * sine).astype(BF)
        k_ref[rows, :] = (dot(normed, w_scr[1]) * cosine + dot(normed, w_scr[4]) * sine).astype(BF)
        v_ref[rows, :] = dot(normed, w_scr[2]).astype(BF)
        return 0

    lax.fori_loop(0, length // CHUNK, project, 0)
    for ref in (n1_ref, q_ref, k_ref, v_ref):
        ship(ref)
    for h in range(heads):
        vm_scr[h] = only_head(v_ref[...], h)
    core = where_ref[1] & 1
    for is_mine, first in halves(core, length):
        def attend(i, _):
            at = pl.multiple_of(i * CHUNK, CHUNK)
            rows = pl.ds(pl.multiple_of(first + at, CHUNK), CHUNK)
            allowed = segc_ref[rows, :] == segr_ref[...]
            query, keys = q_ref[rows, :], k_ref[...]
            total = jnp.zeros((CHUNK, width), F32)
            for h in range(heads):
                logits = dot_nt(only_head(query, h), keys) * HEAD_DIM ** (-0.5)
                logits = jnp.where(allowed, logits, big_negative)
                expd = jnp.exp(logits - jnp.max(logits, axis=-1, keepdims=True))
                probs = (expd / jnp.sum(expd, axis=-1, keepdims=True)).astype(BF)
                ab_ref[h, rows, :] = probs
                total = total + dot(probs, vm_scr[h])
            attended = total.astype(BF)
            o_ref[rows, :] = attended
            part = dot_nt(attended, w_scr[5]).astype(BF)
            if is_mine:
                mine_ref[pl.ds(at, CHUNK), :] = part
            else:
                theirs_ref[pl.ds(at, CHUNK), :] = part
            return 0

        lax.fori_loop(0, length // 2 // CHUNK, attend, 0)
        ship(mine_ref if is_mine else theirs_ref)
        ship(ab_ref, (slice(None), pl.ds(pl.multiple_of(first, length // 2), length // 2)))


def feed_kernel(masks, count, width, ready, ship, where_ref, tok_ref, cot_ref, a_ref, b_ref, c_ref, d_ref, *rest):
    pieces = rest[:count]
    (h_ref, n2_ref, z_ref, du_ref, dv_ref, gain_ref, mine_ref, theirs_ref, wd_ref, full_ref, w_scr) = rest[count:]
    length = tok_ref.shape[0]
    core = where_ref[1] & 1
    ready(*pieces)
    place_pieces(where_ref, pieces, masks, full_ref)
    last = 3 * width // 128 * 128
    gain = column_as_row(full_ref[:, last:], 3 * width - last)
    gain_ref[...] = jnp.broadcast_to(gain, gain_ref.shape)
    for s in range(2):
        w_scr[s] = full_ref[:, s * width : (s + 1) * width]
    wd_ref[...] = full_ref[:, 2 * width : 3 * width]
    ship(wd_ref)
    ready(tok_ref, cot_ref, a_ref, b_ref, c_ref, d_ref)
    for is_mine, first in halves(core, length):
        low, high = (a_ref, b_ref) if is_mine else (c_ref, d_ref)

        def step(i, _):
            at = pl.multiple_of(i * CHUNK, CHUNK)
            rows = pl.ds(pl.multiple_of(first + at, CHUNK), CHUNK)
            here = pl.ds(at, CHUNK)
            middle = tok_ref[rows, :].astype(F32) + (low[here, :].astype(F32) + high[here, :].astype(F32))
            h_ref[rows, :] = middle
            hat, _unused = normalize(middle)
            normed = (hat * gain).astype(BF)
            n2_ref[rows, :] = normed
            up, gate = dot(normed, w_scr[0]), dot(normed, w_scr[1])
            value, slope = gelu_parts(up)
            z_ref[rows, :] = (value * gate).astype(BF)
            back = dot(cot_ref[rows, :], wd_ref[...])
            du, dv = (back * gate * slope).astype(BF), (back * value).astype(BF)
            du_ref[rows, :] = du
            dv_ref[rows, :] = dv
            part = dot_nt(du, w_scr[0]) + dot_nt(dv, w_scr[1])
            part = part.astype(BF)
            if is_mine:
                mine_ref[here, :] = part
            else:
                theirs_ref[here, :] = part
            return 0

        lax.fori_loop(0, length // 2 // CHUNK, step, 0)
        rows = pl.ds(pl.multiple_of(first, length // 2), length // 2)
        for ref in (h_ref, n2_ref, z_ref, du_ref, dv_ref):
            ship(ref, rows)
        ship(mine_ref if is_mine else theirs_ref)


def feed_grad_kernel(width, ready, ship, where_ref, n2_ref, du_ref, dv_ref, cot_ref, z_ref, wd_ref, mine_ref, theirs_ref, *rest):
    grad_ref = rest[-1]
    ready(n2_ref, du_ref)
    grad_ref[:, 0:width] = dot_tn(n2_ref[...], du_ref[...]).astype(BF)
    ready(dv_ref)
    grad_ref[:, width : 2 * width] = dot_tn(n2_ref[...], dv_ref[...]).astype(BF)
    ready(cot_ref, z_ref)
    grad_ref[:, 2 * width : 3 * width] = dot_tn(cot_ref[...], z_ref[...]).astype(BF)
    emit_grad(where_ref, grad_ref, rest[:-1])
    ready(wd_ref)
    length = z_ref.shape[0]
    core = where_ref[1] & 1
    for is_mine, first in halves(core, length):
        rows = pl.ds(pl.multiple_of(first, length // 2), length // 2)
        part = dot_nt(z_ref[rows, :], wd_ref[...]).astype(BF)
        if is_mine:
            mine_ref[...] = part
        else:
            theirs_ref[...] = part


SPAN = 256


def ahead_kernel(width, ready, ship, where_ref, full_ref, q_ref, k_ref, w_ref, km_ref, qm_ref):
    ready(q_ref, k_ref)
    turn = turn_matrix(width)
    for given, out_ref in ((k_ref, km_ref), (q_ref, qm_ref)):
        turned = (-dot(given[...], turn)).astype(BF)
        for h in range(width // HEAD_DIM):
            out_ref[h, :, 0:width] = only_head(given[...], h)
            out_ref[h, :, 256 : 256 + width] = only_head(turned, h)
    ready(full_ref)
    for s in range(4):
        w_ref[s] = full_ref[:, s * width : (s + 1) * width]


def back_kernel(width, ready, ship, where_ref, a_ref, b_ref, c_ref, d_ref, h_ref, cot_ref, gain_ref, w_scr, km_scr, qm_scr, v_ref, o_ref, ab_ref,
                n1_ref, table_ref, dh_ref, mine_ref, theirs_ref, *rest):
    grad_ref, low_scr, do_scr, dk_scr, dv_scr, dp_scr = rest[-6:]
    length = h_ref.shape[0]
    half = length // 2
    heads = width // HEAD_DIM
    core = where_ref[1] & 1
    ready(gain_ref, w_scr, a_ref, b_ref, c_ref, d_ref, h_ref, cot_ref)
    gain = gain_ref[0:1, :]
    for is_mine, first in halves(core, length):
        low, high = (a_ref, b_ref) if is_mine else (c_ref, d_ref)

        def step(i, _):
            at = pl.multiple_of(i * CHUNK, CHUNK)
            rows = pl.ds(pl.multiple_of(first + at, CHUNK), CHUNK)
            here = pl.ds(at, CHUNK)
            grad = low[here, :].astype(F32) + high[here, :].astype(F32)
            hat, inverse = normalize(h_ref[rows, :])
            total = cot_ref[rows, :].astype(F32) + norm_back(grad, gain, hat, inverse)
            dh_ref[rows, :] = total
            narrow = total.astype(BF)
            low_scr[rows, :] = narrow
            do_scr[rows, :] = dot(narrow, w_scr[3]).astype(BF)
            return 0

        lax.fori_loop(0, half // CHUNK, step, 0)
    ship(dh_ref)
    ready(km_scr, qm_scr, v_ref, o_ref, ab_ref)
    ready(table_ref)
    for i in range(length // SPAN):
        rows = pl.ds(i * SPAN, SPAN)
        grad_o = do_scr[rows, :]
        product = grad_o.astype(F32) * o_ref[rows, :].astype(F32)
        dq = None
        dk = None
        dv = None
        for h in range(heads):
            own = only_head(grad_o, h)
            delta = jnp.sum(only_head(product, h), axis=-1, keepdims=True)
            da = dot_nt(own, v_ref[...])
            probs = ab_ref[h, rows, :]
            term = dot_tn(probs, own)
            dv = term if dv is None else dv + term
            ds = (probs.astype(F32) * (da - delta) * HEAD_DIM ** (-0.5)).astype(BF)
            term = dot(ds, km_scr[h])
            dq = term if dq is None else dq + term
            term = dot_tn(ds, qm_scr[h, rows, :])
            dk = term if dk is None else dk + term
        cosine, sine = spread(table_ref[rows, :], width)
        dp_scr[0, rows, :] = (dq[:, :width] * cosine + dq[:, 256 : 256 + width] * sine).astype(BF)
        if i == 0:
            dk_scr[...] = dk
            dv_scr[...] = dv
        else:
            dk_scr[...] += dk
            dv_scr[...] += dv
    cosine, sine = spread(table_ref[...], width)
    dp_scr[1] = (dk_scr[:, :width] * cosine + dk_scr[:, 256 : 256 + width] * sine).astype(BF)
    dp_scr[2] = dv_scr[...].astype(BF)
    ready(n1_ref)
    for s in range(3):
        grad_ref[:, s * width : (s + 1) * width] = dot_tn(n1_ref[...], dp_scr[s]).astype(BF)
    grad_ref[:, 3 * width :] = dot_tn(low_scr[...], o_ref[...]).astype(BF)
    emit_grad(where_ref, grad_ref, rest[:-6])
    for ref in rest[:-6]:
        ship(ref)
    for is_mine, first in halves(core, length):
        out = mine_ref if is_mine else theirs_ref
        rows = pl.ds(pl.multiple_of(first, half), half)
        part = dot_nt(dp_scr[0, rows, :], w_scr[0]) + dot_nt(dp_scr[1, rows, :], w_scr[1]) + dot_nt(dp_scr[2, rows, :], w_scr[2])
        out[...] = part.astype(BF)
        ship(out)


def output_kernel(ready, ship, where_ref, h_ref, a_ref, b_ref, c_ref, d_ref, out_ref, sign_ref):
    sign_ref[...] = jnp.zeros_like(sign_ref)
    half = h_ref.shape[0] // 2
    core = where_ref[1] & 1
    ready(h_ref, a_ref, b_ref, c_ref, d_ref)
    for is_mine, first in halves(core, 2 * half):
        low, high = (a_ref, b_ref) if is_mine else (c_ref, d_ref)
        rows = pl.ds(pl.multiple_of(first, half), half)
        out_ref[rows, :] = h_ref[rows, :] + (low[...].astype(F32) + high[...].astype(F32))
        ship(out_ref, rows)


def input_grad_kernel(ready, ship, where_ref, tok_ref, dh_ref, gain_ref, a_ref, b_ref, c_ref, d_ref, grad_ref, sign_ref):
    sign_ref[...] = jnp.zeros_like(sign_ref)
    half = dh_ref.shape[0] // 2
    core = where_ref[1] & 1
    ready(dh_ref, tok_ref, gain_ref, a_ref, b_ref, c_ref, d_ref)
    gain = gain_ref[0:1, :]
    for is_mine, first in halves(core, 2 * half):
        low, high = (a_ref, b_ref) if is_mine else (c_ref, d_ref)

        def step(i, _):
            at = pl.multiple_of(i * CHUNK, CHUNK)
            rows = pl.ds(pl.multiple_of(first + at, CHUNK), CHUNK)
            here = pl.ds(at, CHUNK)
            grad = low[here, :].astype(F32) + high[here, :].astype(F32)
            hat, inverse = normalize(tok_ref[rows, :].astype(F32))
            grad_ref[rows, :] = dh_ref[rows, :] + norm_back(grad, gain, hat, inverse)
            return 0

        lax.fori_loop(0, half // CHUNK, step, 0)
        ship(grad_ref, pl.ds(pl.multiple_of(first, half), half))


def total_of(refs):
    total = refs[0][...].astype(F32)
    for ref in refs[1:]:
        total = total + ref[...].astype(F32)
    return total


def step_kernel(groups, plan, *refs):
    at = 0
    shards = []
    for count in groups:
        shards.append(total_of(refs[at : at + count]))
        at += count
    outs = refs[at + 3 * len(plan) :]
    for leaf, (transposed, slices) in enumerate(plan):
        w_ref, f_ref, s_ref = refs[at : at + 3]
        at += 3
        g_out, d_out, f_out, s_out = outs[4 * leaf : 4 * leaf + 4]
        for i, (group, first, columns) in enumerate(slices):
            grad = shards[group][:, first : first + columns]
            if transposed:
                grad = grad.T
            where = (i,) if len(w_ref.shape) == 3 else Ellipsis
            delta, first_new, second_new = adamw(w_ref[where], grad, f_ref[where], s_ref[where], decay_rate)
            g_out[where] = grad
            d_out[where] = delta
            f_out[where] = first_new
            s_out[where] = second_new


def gain_kernel(columns, gain_row, w_ref, gains_ref, *refs):
    shard = total_of(refs[:-1])
    total = jnp.zeros((shard.shape[0], 1), F32)
    for i, first in enumerate(columns):
        width = w_ref.shape[2]
        narrow = w_ref[i].astype(BF).astype(F32)
        total = total + jnp.sum(narrow * shard[:, first : first + width], axis=-1, keepdims=True)
    wide = jnp.broadcast_to(total, (shard.shape[0], 128)).T
    gain = gains_ref[gain_row : gain_row + 1, :].astype(BF).astype(F32)
    refs[-1][...] = wide[0:8, :] / gain


def gain_call(columns, gain_row, weight, gains, pieces, deps=()):
    return call(
        lambda *refs: gain_kernel(columns, gain_row, *refs),
        [((8, gains.shape[1]), F32)],
        [weight, gains, *pieces],
        smem=0,
        deps=deps,
    )[0]


def sum_small(values):
    if lax.axis_size("tensor") != 4:
        return lax.psum(values, "tensor")
    return (values + swap(values, "tensor", 1)) + (swap(values, "tensor", 2) + swap(values, "tensor", 3))


def step_call(groups, plan, leaves):
    operands = [piece for group in groups for piece in group]
    for leaf in leaves:
        operands += list(leaf)
    outs = [(leaf[0].shape, F32) for leaf in leaves for _ in range(4)] + [((8, 128), F32)]

    def kernel(*refs):
        step_kernel([len(g) for g in groups], plan, *refs[:-1])
        refs[-1][...] = jnp.zeros_like(refs[-1])

    flat = call(kernel, outs, operands, smem=0)
    return [flat[4 * i : 4 * i + 4] for i in range(len(leaves))], flat[-1]


def local(
    tokens,
    segment_ids,
    cotangent,
    w_qkv,
    w_out,
    w_in,
    w_down,
    gains,
    first_qkv,
    first_out,
    first_in,
    first_down,
    first_gains,
    second_qkv,
    second_out,
    second_in,
    second_down,
    second_gains,
):
    heads = w_qkv.shape[2]
    hidden = w_in.shape[2]
    length, depth = tokens.shape
    half = length // 2
    where = jnp.stack([lax.axis_index("dp"), lax.axis_index("tensor")]).astype(jnp.int32)
    table = rope_tables(length)
    pieces_a, masks_a, pieces_b, masks_b, early, later = gather_pieces(
        [table],
        lambda deps: pack(w_qkv, w_out, gains, 0, deps), lambda deps: pack(w_in, w_down, gains, 1, deps)
    )
    wide_a, wide_b = pieces_a[0].shape[-1], pieces_b[0].shape[-1]
    repeat = heads // HEAD_DIM
    segments = segment_ids.astype(jnp.int32)

    n1, q, k, v, o, ab, gain_one, mine, theirs, full_a = stream(
        lambda *refs: attention_kernel(masks_a, len(pieces_a), heads, *refs),
        [
            ((length, depth), BF),
            ((length, heads), BF),
            ((length, heads), BF),
            ((length, heads), BF),
            ((length, heads), BF),
            ((repeat, length, length), BF),
            ((8, depth), F32),
            ((half, depth), BF),
            ((half, depth), BF),
            ((depth, wide_a), BF),
        ],
        [where, tokens, segments.reshape(length, 1), segments, table, *pieces_a],
        [pltpu.VMEM((6, depth, heads), BF), pltpu.VMEM((repeat, length, heads), BF)],
        near=(7, 8),
        far=(1,),
        here=range(5, 5 + len(pieces_a)),
    )
    terms = reduce_finish(reduce_start(mine, gate(theirs, early) if early else theirs, later))
    middle, n2, z, du, dv2, gain_two, mine, theirs, wd = stream(
        lambda *refs: feed_kernel(masks_b, len(pieces_b), hidden, *refs),
        [
            ((length, depth), F32),
            ((length, depth), BF),
            ((length, hidden), BF),
            ((length, hidden), BF),
            ((length, hidden), BF),
            ((8, depth), F32),
            ((half, depth), BF),
            ((half, depth), BF),
            ((depth, hidden), BF),
        ],
        [where, tokens, cotangent, *terms, *pieces_b],
        [pltpu.VMEM((depth, wide_b), BF), pltpu.VMEM((2, depth, hidden), BF)],
        near=(1, 2, 3, 4, 6, 7, 8),
        far=(1, 2),
        here=range(3, 7 + len(pieces_b)),
    )
    chip = reduce_start(mine, theirs)
    feed_outs = grad_outs(depth, 3 * hidden)
    out_mine, out_theirs, *grad_feed = stream(
        lambda *refs: feed_grad_kernel(hidden, *refs),
        [((half, depth), BF), ((half, depth), BF)] + feed_outs,
        [where, n2, du, dv2, cotangent, z, wd],
        [pltpu.VMEM((depth, 3 * hidden), BF)],
        deps=[chip],
        near=range(2 + len(feed_outs)),
        far=(4,),
        here=(1, 2, 3, 5, 6),
    )
    weights, keys, queries = stream(
        lambda *refs: ahead_kernel(heads, *refs),
        [((4, depth, heads), BF), ((repeat, length, 512), BF), ((repeat, length, 512), BF)],
        [where, full_a, q, k],
        deps=[chip, out_mine],
        near=(0, 1, 2),
        far=(1, 2, 3),
        vmem=16,
    )
    terms = reduce_finish(chip, [out_mine, keys])
    feed_pieces, feed_got, _unused = scatter_start(where, grad_feed)
    out_chip = reduce_start(out_mine, out_theirs, terms[1:2])
    out_got = swap(out_chip, "tensor", 2)
    small = ((8, 128), F32)
    whole = ((length, depth), F32)
    width = 4 * heads
    attn_outs = grad_outs(depth, width)
    dh, mine, theirs, *grad_attn = stream(
        lambda *refs: back_kernel(heads, *refs),
        [((length, depth), F32), ((half, depth), BF), ((half, depth), BF)] + attn_outs,
        [where, *terms, middle, cotangent, gain_two, weights, keys, queries, v, o, ab, n1, table],
        [
            pltpu.VMEM((depth, width), BF),
            pltpu.VMEM((length, depth), BF),
            pltpu.VMEM((length, heads), BF),
            pltpu.VMEM((length, 512), F32),
            pltpu.VMEM((length, heads), F32),
            pltpu.VMEM((3, length, heads), BF),
        ],
        near=range(1, 3 + len(attn_outs)),
        here=range(1, 16),
        vmem=28,
        cost=1,
    )
    chip = reduce_start(mine, gate(theirs, feed_got), [out_got])
    attn_pieces, _unused, _unused = scatter_start(where, grad_attn, feed_pieces[1:])
    out_chip, out_got = gate(out_chip, feed_pieces[-1:]), gate(out_got, feed_pieces[-1:])
    out_terms = [out_chip, out_got, swap(out_chip, "tensor", 1), swap(out_got, "tensor", 1)]
    output, sign = stream(
        output_kernel, [whole, small], [where, middle, *out_terms], near=(1,), far=(1,), here=range(2, 6), vmem=10
    )
    signs = [sign]
    terms = reduce_finish(chip, feed_pieces[1:])
    grad_tokens, sign = stream(
        input_grad_kernel, [whole, small], [where, tokens, dh, gain_one, *terms], near=(1,), far=(1, 2), here=range(4, 8), vmem=10
    )
    signs.append(sign)

    gain_sum_two = gain_call([0, hidden], 1, w_in, gains, feed_pieces)
    (leaf_in, leaf_down), sign = step_call(
        [feed_pieces],
        [(False, [(0, 0, hidden), (0, hidden, hidden)]), (True, [(0, 2 * hidden, hidden)])],
        [(w_in, first_in, second_in), (w_down, first_down, second_down)],
    )
    gain_sum_one = gain_call([0, heads, 2 * heads], 0, w_qkv, gains, attn_pieces, signs + [sign])
    share_gains = sum_small(jnp.concatenate([gain_sum_one[0:1], gain_sum_two[0:1]], axis=0))
    (leaf_qkv, leaf_out), _unused = step_call(
        [attn_pieces],
        [(False, [(0, 0, heads), (0, heads, heads), (0, 2 * heads, heads)]), (True, [(0, 3 * heads, heads)])],
        [(w_qkv, first_qkv, second_qkv), (w_out, first_out, second_out)],
    )
    n_gains, m_gains, s_gains = adamw(gains, share_gains, first_gains, second_gains, 0.0)
    by_kind = list(zip(leaf_qkv, leaf_out, leaf_in, leaf_down, (share_gains, n_gains, m_gains, s_gains)))
    return (output, grad_tokens, *by_kind[0], *by_kind[1], *by_kind[2], *by_kind[3])


def solution(mesh):
    placed = (
        P("dp", None),
        P("dp", None),
        P("dp", None),
        P(None, "dp", "tensor"),
        P("tensor", "dp"),
        P(None, "dp", "tensor"),
        P("tensor", "dp"),
        P(None, "dp"),
        P(None, "dp", "tensor"),
        P("tensor", "dp"),
        P(None, "dp", "tensor"),
        P("tensor", "dp"),
        P(None, "dp"),
        P(None, "dp", "tensor"),
        P("tensor", "dp"),
        P(None, "dp", "tensor"),
        P("tensor", "dp"),
        P(None, "dp"),
    )
    return jax.shard_map(
        local,
        mesh=mesh,
        in_specs=placed,
        out_specs=(
            P("dp", None),
            P("dp", None),
            P(None, "dp", "tensor"),
            P("tensor", "dp"),
            P(None, "dp", "tensor"),
            P("tensor", "dp"),
            P(None, "dp"),
            P(None, "dp", "tensor"),
            P("tensor", "dp"),
            P(None, "dp", "tensor"),
            P("tensor", "dp"),
            P(None, "dp"),
            P(None, "dp", "tensor"),
            P("tensor", "dp"),
            P(None, "dp", "tensor"),
            P("tensor", "dp"),
            P(None, "dp"),
            P(None, "dp", "tensor"),
            P("tensor", "dp"),
            P(None, "dp", "tensor"),
            P("tensor", "dp"),
            P(None, "dp"),
        ),
        check_vma=False,
    )
```

```python
import jax
import jax.numpy as jnp
from jax import lax
from jax.experimental import pallas as pl
from jax.experimental.pallas import tpu as pltpu
from jax.sharding import PartitionSpec as P

HEAD_DIM = 64
STEP = 3


norm_eps = 1e-05
rope_base = 160000.0
learn_rate = 0.01
beta_one = 0.9
beta_two = 0.98
adam_eps = 1e-08
decay_rate = 0.01
big_negative = -1e30

BF = jnp.bfloat16
F32 = jnp.float32


def rope_tables(count):
    half_dim = HEAD_DIM // 2
    lane = jnp.arange(2 * HEAD_DIM)
    frequency = rope_base ** (-((lane % half_dim).astype(jnp.float32) * 2.0 / HEAD_DIM))
    angles = jnp.arange(count, dtype=jnp.float32)[:, None] * frequency[None, :]
    return jnp.where(lane[None, :] < HEAD_DIM, jnp.cos(angles), jnp.sin(angles))


def gelu_parts(inputs):
    normal_cdf = 0.5 * (1.0 + lax.erf(inputs * 0.7071067811865476))
    density = jnp.exp(-0.5 * inputs * inputs) * 0.3989422804014327
    return (inputs * normal_cdf, normal_cdf + inputs * density)


def adamw(weight, gradient, first_mom, second, decay_now):
    first_new = beta_one * first_mom + (1.0 - beta_one) * gradient
    second_new = beta_two * second + (1.0 - beta_two) * gradient * gradient
    corr_one = 1.0 - beta_one**STEP
    corr_two = 1.0 - beta_two**STEP
    update = (
        first_new / corr_one / (jnp.sqrt(second_new / corr_two) + adam_eps) + decay_now * weight
    )
    return (-learn_rate * update, first_new, second_new)


def swap(values, axis, mask):
    count = lax.axis_size(axis)
    return lax.ppermute(values, axis, [(i, i ^ mask) for i in range(count)])


def pack(first, second, gains, row, deps=()):
    rows = first.shape[1]
    used = first.shape[0] * first.shape[2] + second.shape[0] + 1
    width = -(-used // 128) * 128
    return stream(
        lambda *refs: pack_kernel(row, *refs), [((rows, width), BF)], [first, second, gains], smem=0, deps=deps, vmem=16, near=(0,), far=(0, 1, 2)
    )[0]


def gather_pieces(beside, pack_a, pack_b):
    if lax.axis_size("dp") != 8:
        full_a = lax.all_gather(pack_a(()), "dp", axis=0, tiled=True)
        full_b = lax.all_gather(pack_b(()), "dp", axis=0, tiled=True)
        return [full_a], None, [full_b], None, [], []
    order = (4, 6, 2)
    shard_a, shard_b = pack_a(()), pack_b(())
    far_one, far_two, near = [swap(shard_a, "dp", m) for m in order]
    side = swap(shard_a, "dp", 1)
    sides = [side, swap(gate(side, beside), "dp", 2), swap(far_one, "dp", 1), swap(far_two, "dp", 1)]
    pieces_a = [shard_a, near, far_one, far_two] + sides
    masks_a = [[m] for m in (0, 2, 4, 6, 1, 3, 5, 7)]
    shard_b = gate(shard_b, [far_one, far_two, sides[1]])
    column = [swap(shard_b, "dp", m) for m in order]
    side = swap(shard_b, "dp", 1)
    stacked = stack(column)
    pieces_b = [shard_b, stacked, side, swap(stacked, "dp", 1)]
    return pieces_a, masks_a, pieces_b, [[0], [4, 6, 2], [1], [5, 7, 3]], column + [side], [stacked]


def pair_kernel(where_ref, keep_ref, got_ref, own_ref, *far_refs):
    level = where_ref[0] >> 1
    for m, ref in enumerate((own_ref,) + far_refs):
        at = level ^ m
        ref[...] = (keep_ref[at].astype(F32) + got_ref[at].astype(F32)).astype(BF)


def scatter_start(where, grads, deps=()):
    if len(grads) == 1:
        return [lax.psum_scatter(grads[0].astype(F32), "dp", scatter_dimension=0, tiled=True)], [], []
    keep, send = grads
    got = swap(send, "dp", 1)
    parts = call(pair_kernel, [(keep.shape[1:], BF)] * keep.shape[0], [where, keep, got], deps=deps)
    came = [swap(parts[m], "dp", 2 * m) for m in reversed(range(1, len(parts)))]
    return [parts[0]] + came, [got], [parts[0]]


def grad_outs(depth, width):
    count = lax.axis_size("dp")
    if count != 8:
        return [((depth, width), BF)]
    return [((count // 2, depth // count, width), BF)] * 2


def emit_grad(where_ref, grad_scr, refs):
    if len(refs) == 1:
        refs[0][...] = grad_scr[...]
        return
    keep_ref, send_ref = refs
    levels, rows, _width = keep_ref.shape
    odd = where_ref[0] & 1
    for level in range(levels):
        at = pl.multiple_of((2 * level + odd) * rows, rows)
        keep_ref[level] = grad_scr[pl.ds(at, rows), :]
        at = pl.multiple_of((2 * level + 1 - odd) * rows, rows)
        send_ref[level] = grad_scr[pl.ds(at, rows), :]


def add_kernel(a_ref, b_ref, out_ref):
    out_ref[...] = (a_ref[...].astype(F32) + b_ref[...].astype(F32)).astype(BF)


def reduce_start(mine, theirs, deps=()):
    got = swap(theirs, "tensor", 1)
    return call(add_kernel, [(mine.shape, BF)], [mine, got], smem=0, deps=deps)[0]


def reduce_finish(chip, deps=()):
    got = swap(chip, "tensor", 2)
    if deps:
        got = gate(got, deps)
    return [chip, got, swap(chip, "tensor", 1), swap(got, "tensor", 1)]


def dot(a, b):
    return jnp.dot(a, b, preferred_element_type=F32)


def dot_nt(a, b):
    return lax.dot_general(a, b, (((1,), (1,)), ((), ())), preferred_element_type=F32)


def dot_tn(a, b):
    return lax.dot_general(a, b, (((0,), (0,)), ((), ())), preferred_element_type=F32)


def head_mask(rows, width, head):
    lane = lax.broadcasted_iota(jnp.int32, (rows, width), 1)
    return (lane >= head * HEAD_DIM) & (lane < (head + 1) * HEAD_DIM)


def only_head(values, head):
    return jnp.where(head_mask(values.shape[0], values.shape[1], head), values, jnp.zeros_like(values))


def spread(table, width):
    count = width // HEAD_DIM
    cosine, sine = table[:, :HEAD_DIM], table[:, HEAD_DIM:]
    return jnp.concatenate([cosine] * count, axis=1), jnp.concatenate([sine] * count, axis=1)


def turn_matrix(width):
    half = HEAD_DIM // 2
    source = lax.broadcasted_iota(jnp.int32, (width, width), 0)
    target = lax.broadcasted_iota(jnp.int32, (width, width), 1)
    low = (target & (HEAD_DIM - 1)) < half
    value = jnp.where(low & (source == target + half), -1.0, 0.0)
    return (value + jnp.where((~low) & (source == target - half), 1.0, 0.0)).astype(BF)


def column_as_row(block, lane):
    pick = (lax.broadcasted_iota(jnp.int32, (16, block.shape[1]), 1) == lane).astype(F32).astype(BF)
    return dot_nt(pick, block)[0:1]


def normalize(values):
    center = values - jnp.mean(values, axis=-1, keepdims=True)
    inverse = lax.rsqrt(jnp.mean(center * center, axis=-1, keepdims=True) + norm_eps)
    return center * inverse, inverse


def norm_back(grad_norm, gain_row, normed, inverse):
    scaled = grad_norm * gain_row
    return (
        scaled
        - jnp.mean(scaled, axis=-1, keepdims=True)
        - normed * jnp.mean(scaled * normed, axis=-1, keepdims=True)
    ) * inverse


def place_pieces(where_ref, pieces, masks, out_ref):
    if masks is None:
        out_ref[...] = pieces[0][...]
        return
    for piece, own in zip(pieces, masks):
        rows = piece.shape[-2]
        for i, mask in enumerate(own):
            at = pl.multiple_of((where_ref[0] ^ mask) * rows, rows)
            out_ref[pl.ds(at, rows), :] = piece[i] if len(piece.shape) == 3 else piece[...]


def call(kernel, outs, operands, scratch=(), smem=1, deps=(), vmem=8):
    count = len(operands)

    def body(*refs):
        kernel(*refs[:count], *refs[count + len(deps) :])

    return pl.pallas_call(
        body,
        out_shape=[jax.ShapeDtypeStruct(s, d) for s, d in outs],
        in_specs=[pl.BlockSpec(memory_space=pltpu.SMEM)] * smem
        + [pl.BlockSpec()] * (count - smem)
        + [pl.BlockSpec(memory_space=pl.ANY)] * len(deps),
        out_specs=[pl.BlockSpec()] * len(outs),
        scratch_shapes=list(scratch),
        compiler_params=pltpu.CompilerParams(vmem_limit_bytes=vmem * 1024 * 1024),
    )(*operands, *deps)


def stream(kernel, outs, operands, scratch=(), smem=1, deps=(), vmem=40, near=(), far=(), here=(), stages=(), cost=None):
    count, total = len(operands), len(outs)
    moved = [i for i in range(smem, count) if i not in here]
    late = len(moved)
    room = [pltpu.VMEM(operands[i].shape, operands[i].dtype) for i in moved]
    room += [pltpu.VMEM(*out) for i, out in enumerate(outs) if i not in near]
    gone = total - len(near)

    def body(*refs):
        given, results = refs[:count], refs[count + len(deps) : count + len(deps) + total]
        own = refs[count + len(deps) + total :]
        flags, own = own[-1], own[:-1]
        own, held, made = own[: -late - gone], own[-late - gone : -gone or None], list(own[len(own) - gone :])
        for i in sorted(near):
            made.insert(i, results[i])
        copies = [pltpu.make_async_copy(given[i], held[n], flags.at[n]) for n, i in enumerate(moved)]
        waiting = {id(ref): copy for ref, copy in zip(held, copies)}
        inputs = list(given[smem:])
        for n, i in enumerate(moved):
            inputs[i - smem] = held[n]
        queue = list(zip(moved, copies))

        def launch():
            first = True
            while queue and (first or queue[0][0] not in stages):
                queue.pop(0)[1].start()
                first = False

        place = {id(ref): i for i, ref in enumerate(made) if i not in near}
        sent = []
        shipped = {}

        def ready(*wanted):
            for ref in wanted:
                copy = waiting.pop(id(ref), None)
                while any(copy is other for _unused, other in queue):
                    launch()
                if copy is not None:
                    copy.wait()
            launch()

        def ship(ref, rows=None):
            i = place.get(id(ref))
            if i is None:
                return
            part = shipped.get(i, 0)
            shipped[i] = part + 1
            source, target = (ref, results[i]) if rows is None else (ref.at[rows], results[i].at[rows])
            copy = pltpu.make_async_copy(source, target, flags.at[late + 2 * i + part])
            copy.start()
            sent.append(copy)

        launch()
        kernel(ready, ship, *refs[:smem], *inputs, *made, *own)
        ready(*held)
        for i, ref in enumerate(made):
            if i not in shipped:
                ship(ref)
        for copy in sent:
            copy.wait()

    anywhere = pl.BlockSpec(memory_space=pl.ANY)
    pinned = [pltpu.with_memory_space_constraint(x, pltpu.HBM) if i in far else x for i, x in enumerate(operands)]
    return pl.pallas_call(
        body,
        out_shape=[jax.ShapeDtypeStruct(*out) if i in near else pltpu.HBM(*out) for i, out in enumerate(outs)],
        in_specs=[pl.BlockSpec(memory_space=pltpu.SMEM)] * smem
        + [pl.BlockSpec() if i in here else anywhere for i in range(smem, count)]
        + [anywhere] * len(deps),
        out_specs=[pl.BlockSpec() if i in near else anywhere for i in range(total)],
        scratch_shapes=list(scratch) + room + [pltpu.SemaphoreType.DMA((late + 2 * total,))],
        compiler_params=pltpu.CompilerParams(vmem_limit_bytes=vmem * 1024 * 1024),
        cost_estimate=None if cost is None else pl.CostEstimate(flops=cost, bytes_accessed=cost, transcendentals=0),
    )(*pinned, *deps)


def gate(value, deps):
    if not deps:
        return value
    return pl.pallas_call(
        lambda *refs: None,
        out_shape=jax.ShapeDtypeStruct(value.shape, value.dtype),
        in_specs=[pl.BlockSpec(memory_space=pl.ANY)] * (1 + len(deps)),
        out_specs=pl.BlockSpec(memory_space=pl.ANY),
        input_output_aliases={0: 0},
        compiler_params=pltpu.CompilerParams(vmem_limit_bytes=1024 * 1024),
    )(value, *deps)


def pack_kernel(row, ready, ship, first_ref, second_ref, gain_ref, out_ref):
    width = out_ref.shape[1]
    ready(first_ref, second_ref, gain_ref)
    gain = jnp.broadcast_to(gain_ref[row : row + 1, :], (8, gain_ref.shape[1])).T
    parts = [first_ref[i] for i in range(first_ref.shape[0])] + [second_ref[...].T, gain[:, 0:1]]
    used = sum(part.shape[1] for part in parts)
    parts.append(jnp.zeros((out_ref.shape[0], width - used), F32))
    out_ref[...] = jnp.concatenate(parts, axis=1).astype(BF)


def stack(pieces):
    def body(*refs):
        flags = refs[-1]
        copies = [pltpu.make_async_copy(ref, refs[-2].at[i], flags.at[i]) for i, ref in enumerate(refs[:-2])]
        for copy in copies:
            copy.start()
        for copy in copies:
            copy.wait()

    anywhere = pl.BlockSpec(memory_space=pl.ANY)
    return pl.pallas_call(
        body,
        out_shape=jax.ShapeDtypeStruct((len(pieces),) + pieces[0].shape, pieces[0].dtype),
        in_specs=[anywhere] * len(pieces),
        out_specs=anywhere,
        scratch_shapes=[pltpu.SemaphoreType.DMA((len(pieces),))],
        compiler_params=pltpu.CompilerParams(vmem_limit_bytes=1024 * 1024),
    )(*pieces)


CHUNK = 256


def halves(core, length):
    half = length // 2
    return ((False, (1 - core) * half), (True, core * half))


def attention_kernel(masks, count, width, ready, ship, where_ref, tok_ref, segc_ref, segr_ref, table_ref, *rest):
    pieces = rest[:count]
    n1_ref, q_ref, k_ref, v_ref, o_ref, ab_ref, gain_ref, mine_ref, theirs_ref, full_ref, w_scr, vm_scr = rest[count:]
    length = tok_ref.shape[0]
    heads = width // HEAD_DIM
    ready(*pieces)
    place_pieces(where_ref, pieces, masks, full_ref)
    ship(full_ref)
    gain = column_as_row(full_ref[:, 4 * width :], 0)
    gain_ref[...] = jnp.broadcast_to(gain, gain_ref.shape)
    turn = turn_matrix(width)
    for s in range(3):
        w_scr[s] = full_ref[:, s * width : (s + 1) * width]
    for s in range(2):
        w_scr[3 + s] = dot(w_scr[s], turn).astype(BF)
    w_scr[5] = full_ref[:, 3 * width : 4 * width]
    ready(tok_ref, table_ref, segc_ref, segr_ref)

    def project(i, _):
        rows = pl.ds(pl.multiple_of(i * CHUNK, CHUNK), CHUNK)
        hat, _unused = normalize(tok_ref[rows, :].astype(F32))
        normed = (hat * gain).astype(BF)
        n1_ref[rows, :] = normed
        cosine, sine = spread(table_ref[rows, :], width)
        q_ref[rows, :] = (dot(normed, w_scr[0]) * cosine + dot(normed, w_scr[3]) * sine).astype(BF)
        k_ref[rows, :] = (dot(normed, w_scr[1]) * cosine + dot(normed, w_scr[4]) * sine).astype(BF)
        v_ref[rows, :] = dot(normed, w_scr[2]).astype(BF)
        return 0

    lax.fori_loop(0, length // CHUNK, project, 0)
    for ref in (n1_ref, q_ref, k_ref, v_ref):
        ship(ref)
    for h in range(heads):
        vm_scr[h] = only_head(v_ref[...], h)
    core = where_ref[1] & 1
    for is_mine, first in halves(core, length):
        def attend(i, _):
            at = pl.multiple_of(i * CHUNK, CHUNK)
            rows = pl.ds(pl.multiple_of(first + at, CHUNK), CHUNK)
            allowed = segc_ref[rows, :] == segr_ref[...]
            query, keys = q_ref[rows, :], k_ref[...]
            total = jnp.zeros((CHUNK, width), F32)
            for h in range(heads):
                logits = dot_nt(only_head(query, h), keys) * HEAD_DIM ** (-0.5)
                logits = jnp.where(allowed, logits, big_negative)
                expd = jnp.exp(logits - jnp.max(logits, axis=-1, keepdims=True))
                probs = (expd / jnp.sum(expd, axis=-1, keepdims=True)).astype(BF)
                ab_ref[h, rows, :] = probs
                total = total + dot(probs, vm_scr[h])
            attended = total.astype(BF)
            o_ref[rows, :] = attended
            part = dot_nt(attended, w_scr[5]).astype(BF)
            if is_mine:
                mine_ref[pl.ds(at, CHUNK), :] = part
            else:
                theirs_ref[pl.ds(at, CHUNK), :] = part
            return 0

        lax.fori_loop(0, length // 2 // CHUNK, attend, 0)
        ship(mine_ref if is_mine else theirs_ref)
        ship(ab_ref, (slice(None), pl.ds(pl.multiple_of(first, length // 2), length // 2)))


def feed_kernel(masks, count, width, ready, ship, where_ref, tok_ref, cot_ref, a_ref, b_ref, c_ref, d_ref, *rest):
    pieces = rest[:count]
    (h_ref, n2_ref, z_ref, du_ref, dv_ref, gain_ref, mine_ref, theirs_ref, wd_ref, full_ref, w_scr) = rest[count:]
    length = tok_ref.shape[0]
    core = where_ref[1] & 1
    ready(*pieces)
    place_pieces(where_ref, pieces, masks, full_ref)
    last = 3 * width // 128 * 128
    gain = column_as_row(full_ref[:, last:], 3 * width - last)
    gain_ref[...] = jnp.broadcast_to(gain, gain_ref.shape)
    for s in range(2):
        w_scr[s] = full_ref[:, s * width : (s + 1) * width]
    wd_ref[...] = full_ref[:, 2 * width : 3 * width]
    ship(wd_ref)
    ready(tok_ref, cot_ref, a_ref, b_ref, c_ref, d_ref)
    for is_mine, first in halves(core, length):
        low, high = (a_ref, b_ref) if is_mine else (c_ref, d_ref)

        def step(i, _):
            at = pl.multiple_of(i * CHUNK, CHUNK)
            rows = pl.ds(pl.multiple_of(first + at, CHUNK), CHUNK)
            here = pl.ds(at, CHUNK)
            middle = tok_ref[rows, :].astype(F32) + (low[here, :].astype(F32) + high[here, :].astype(F32))
            h_ref[rows, :] = middle
            hat, _unused = normalize(middle)
            normed = (hat * gain).astype(BF)
            n2_ref[rows, :] = normed
            up, gate = dot(normed, w_scr[0]), dot(normed, w_scr[1])
            value, slope = gelu_parts(up)
            z_ref[rows, :] = (value * gate).astype(BF)
            back = dot(cot_ref[rows, :], wd_ref[...])
            du, dv = (back * gate * slope).astype(BF), (back * value).astype(BF)
            du_ref[rows, :] = du
            dv_ref[rows, :] = dv
            part = dot_nt(du, w_scr[0]) + dot_nt(dv, w_scr[1])
            part = part.astype(BF)
            if is_mine:
                mine_ref[here, :] = part
            else:
                theirs_ref[here, :] = part
            return 0

        lax.fori_loop(0, length // 2 // CHUNK, step, 0)
        rows = pl.ds(pl.multiple_of(first, length // 2), length // 2)
        for ref in (h_ref, n2_ref, z_ref, du_ref, dv_ref):
            ship(ref, rows)
        ship(mine_ref if is_mine else theirs_ref)


def feed_grad_kernel(width, ready, ship, where_ref, n2_ref, du_ref, dv_ref, cot_ref, z_ref, wd_ref, mine_ref, theirs_ref, *rest):
    grad_ref = rest[-1]
    ready(n2_ref, du_ref)
    grad_ref[:, 0:width] = dot_tn(n2_ref[...], du_ref[...]).astype(BF)
    ready(dv_ref)
    grad_ref[:, width : 2 * width] = dot_tn(n2_ref[...], dv_ref[...]).astype(BF)
    ready(cot_ref, z_ref)
    grad_ref[:, 2 * width : 3 * width] = dot_tn(cot_ref[...], z_ref[...]).astype(BF)
    emit_grad(where_ref, grad_ref, rest[:-1])
    ready(wd_ref)
    length = z_ref.shape[0]
    core = where_ref[1] & 1
    for is_mine, first in halves(core, length):
        rows = pl.ds(pl.multiple_of(first, length // 2), length // 2)
        part = dot_nt(z_ref[rows, :], wd_ref[...]).astype(BF)
        if is_mine:
            mine_ref[...] = part
        else:
            theirs_ref[...] = part


SPAN = 256


def ahead_kernel(width, ready, ship, where_ref, full_ref, q_ref, k_ref, w_ref, km_ref, qm_ref):
    ready(q_ref, k_ref)
    turn = turn_matrix(width)
    for given, out_ref in ((k_ref, km_ref), (q_ref, qm_ref)):
        turned = (-dot(given[...], turn)).astype(BF)
        for h in range(width // HEAD_DIM):
            out_ref[h, :, 0:width] = only_head(given[...], h)
            out_ref[h, :, 256 : 256 + width] = only_head(turned, h)
    ready(full_ref)
    for s in range(4):
        w_ref[s] = full_ref[:, s * width : (s + 1) * width]


def back_kernel(width, ready, ship, where_ref, a_ref, b_ref, c_ref, d_ref, h_ref, cot_ref, gain_ref, w_scr, km_scr, qm_scr, v_ref, o_ref, ab_ref,
                n1_ref, table_ref, dh_ref, mine_ref, theirs_ref, *rest):
    grad_ref, low_scr, do_scr, dk_scr, dv_scr, dp_scr = rest[-6:]
    length = h_ref.shape[0]
    half = length // 2
    heads = width // HEAD_DIM
    core = where_ref[1] & 1
    ready(gain_ref, w_scr, a_ref, b_ref, c_ref, d_ref, h_ref, cot_ref)
    gain = gain_ref[0:1, :]
    for is_mine, first in halves(core, length):
        low, high = (a_ref, b_ref) if is_mine else (c_ref, d_ref)

        def step(i, _):
            at = pl.multiple_of(i * CHUNK, CHUNK)
            rows = pl.ds(pl.multiple_of(first + at, CHUNK), CHUNK)
            here = pl.ds(at, CHUNK)
            grad = low[here, :].astype(F32) + high[here, :].astype(F32)
            hat, inverse = normalize(h_ref[rows, :])
            total = cot_ref[rows, :].astype(F32) + norm_back(grad, gain, hat, inverse)
            dh_ref[rows, :] = total
            narrow = total.astype(BF)
            low_scr[rows, :] = narrow
            do_scr[rows, :] = dot(narrow, w_scr[3]).astype(BF)
            return 0

        lax.fori_loop(0, half // CHUNK, step, 0)
    ship(dh_ref)
    ready(km_scr, qm_scr, v_ref, o_ref, ab_ref)
    ready(table_ref)
    for i in range(length // SPAN):
        rows = pl.ds(i * SPAN, SPAN)
        grad_o = do_scr[rows, :]
        product = grad_o.astype(F32) * o_ref[rows, :].astype(F32)
        dq = None
        dk = None
        dv = None
        for h in range(heads):
            own = only_head(grad_o, h)
            delta = jnp.sum(only_head(product, h), axis=-1, keepdims=True)
            da = dot_nt(own, v_ref[...])
            probs = ab_ref[h, rows, :]
            term = dot_tn(probs, own)
            dv = term if dv is None else dv + term
            ds = (probs.astype(F32) * (da - delta) * HEAD_DIM ** (-0.5)).astype(BF)
            term = dot(ds, km_scr[h])
            dq = term if dq is None else dq + term
            term = dot_tn(ds, qm_scr[h, rows, :])
            dk = term if dk is None else dk + term
        cosine, sine = spread(table_ref[rows, :], width)
        dp_scr[0, rows, :] = (dq[:, :width] * cosine + dq[:, 256 : 256 + width] * sine).astype(BF)
        if i == 0:
            dk_scr[...] = dk
            dv_scr[...] = dv
        else:
            dk_scr[...] += dk
            dv_scr[...] += dv
    cosine, sine = spread(table_ref[...], width)
    dp_scr[1] = (dk_scr[:, :width] * cosine + dk_scr[:, 256 : 256 + width] * sine).astype(BF)
    dp_scr[2] = dv_scr[...].astype(BF)
    ready(n1_ref)
    for s in range(3):
        grad_ref[:, s * width : (s + 1) * width] = dot_tn(n1_ref[...], dp_scr[s]).astype(BF)
    grad_ref[:, 3 * width :] = dot_tn(low_scr[...], o_ref[...]).astype(BF)
    emit_grad(where_ref, grad_ref, rest[:-6])
    for ref in rest[:-6]:
        ship(ref)
    for is_mine, first in halves(core, length):
        out = mine_ref if is_mine else theirs_ref
        rows = pl.ds(pl.multiple_of(first, half), half)
        part = dot_nt(dp_scr[0, rows, :], w_scr[0]) + dot_nt(dp_scr[1, rows, :], w_scr[1]) + dot_nt(dp_scr[2, rows, :], w_scr[2])
        out[...] = part.astype(BF)
        ship(out)


def output_kernel(ready, ship, where_ref, h_ref, a_ref, b_ref, c_ref, d_ref, out_ref, sign_ref):
    sign_ref[...] = jnp.zeros_like(sign_ref)
    half = h_ref.shape[0] // 2
    core = where_ref[1] & 1
    ready(h_ref, a_ref, b_ref, c_ref, d_ref)
    for is_mine, first in halves(core, 2 * half):
        low, high = (a_ref, b_ref) if is_mine else (c_ref, d_ref)
        rows = pl.ds(pl.multiple_of(first, half), half)
        out_ref[rows, :] = h_ref[rows, :] + (low[...].astype(F32) + high[...].astype(F32))
        ship(out_ref, rows)


def input_grad_kernel(ready, ship, where_ref, tok_ref, dh_ref, gain_ref, a_ref, b_ref, c_ref, d_ref, grad_ref, sign_ref):
    sign_ref[...] = jnp.zeros_like(sign_ref)
    half = dh_ref.shape[0] // 2
    core = where_ref[1] & 1
    ready(dh_ref, tok_ref, gain_ref, a_ref, b_ref, c_ref, d_ref)
    gain = gain_ref[0:1, :]
    for is_mine, first in halves(core, 2 * half):
        low, high = (a_ref, b_ref) if is_mine else (c_ref, d_ref)

        def step(i, _):
            at = pl.multiple_of(i * CHUNK, CHUNK)
            rows = pl.ds(pl.multiple_of(first + at, CHUNK), CHUNK)
            here = pl.ds(at, CHUNK)
            grad = low[here, :].astype(F32) + high[here, :].astype(F32)
            hat, inverse = normalize(tok_ref[rows, :].astype(F32))
            grad_ref[rows, :] = dh_ref[rows, :] + norm_back(grad, gain, hat, inverse)
            return 0

        lax.fori_loop(0, half // CHUNK, step, 0)
        ship(grad_ref, pl.ds(pl.multiple_of(first, half), half))


def total_of(refs):
    total = refs[0][...].astype(F32)
    for ref in refs[1:]:
        total = total + ref[...].astype(F32)
    return total


def step_kernel(groups, plan, *refs):
    at = 0
    shards = []
    for count in groups:
        shards.append(total_of(refs[at : at + count]))
        at += count
    outs = refs[at + 3 * len(plan) :]
    for leaf, (transposed, slices) in enumerate(plan):
        w_ref, f_ref, s_ref = refs[at : at + 3]
        at += 3
        g_out, d_out, f_out, s_out = outs[4 * leaf : 4 * leaf + 4]
        for i, (group, first, columns) in enumerate(slices):
            grad = shards[group][:, first : first + columns]
            if transposed:
                grad = grad.T
            where = (i,) if len(w_ref.shape) == 3 else Ellipsis
            delta, first_new, second_new = adamw(w_ref[where], grad, f_ref[where], s_ref[where], decay_rate)
            g_out[where] = grad
            d_out[where] = delta
            f_out[where] = first_new
            s_out[where] = second_new


def gain_kernel(columns, gain_row, w_ref, gains_ref, *refs):
    shard = total_of(refs[:-1])
    total = jnp.zeros((shard.shape[0], 1), F32)
    for i, first in enumerate(columns):
        width = w_ref.shape[2]
        narrow = w_ref[i].astype(BF).astype(F32)
        total = total + jnp.sum(narrow * shard[:, first : first + width], axis=-1, keepdims=True)
    wide = jnp.broadcast_to(total, (shard.shape[0], 128)).T
    gain = gains_ref[gain_row : gain_row + 1, :].astype(BF).astype(F32)
    refs[-1][...] = wide[0:8, :] / gain


def gain_call(columns, gain_row, weight, gains, pieces, deps=()):
    return call(
        lambda *refs: gain_kernel(columns, gain_row, *refs),
        [((8, gains.shape[1]), F32)],
        [weight, gains, *pieces],
        smem=0,
        deps=deps,
    )[0]


def sum_small(values):
    if lax.axis_size("tensor") != 4:
        return lax.psum(values, "tensor")
    return (values + swap(values, "tensor", 1)) + (swap(values, "tensor", 2) + swap(values, "tensor", 3))


def step_call(groups, plan, leaves):
    operands = [piece for group in groups for piece in group]
    for leaf in leaves:
        operands += list(leaf)
    outs = [(leaf[0].shape, F32) for leaf in leaves for _ in range(4)] + [((8, 128), F32)]

    def kernel(*refs):
        step_kernel([len(g) for g in groups], plan, *refs[:-1])
        refs[-1][...] = jnp.zeros_like(refs[-1])

    flat = call(kernel, outs, operands, smem=0)
    return [flat[4 * i : 4 * i + 4] for i in range(len(leaves))], flat[-1]


def local(
    tokens,
    segment_ids,
    cotangent,
    w_qkv,
    w_out,
    w_in,
    w_down,
    gains,
    first_qkv,
    first_out,
    first_in,
    first_down,
    first_gains,
    second_qkv,
    second_out,
    second_in,
    second_down,
    second_gains,
):
    heads = w_qkv.shape[2]
    hidden = w_in.shape[2]
    length, depth = tokens.shape
    half = length // 2
    where = jnp.stack([lax.axis_index("dp"), lax.axis_index("tensor")]).astype(jnp.int32)
    table = rope_tables(length)
    pieces_a, masks_a, pieces_b, masks_b, early, later = gather_pieces(
        [table],
        lambda deps: pack(w_qkv, w_out, gains, 0, deps), lambda deps: pack(w_in, w_down, gains, 1, deps)
    )
    wide_a, wide_b = pieces_a[0].shape[-1], pieces_b[0].shape[-1]
    repeat = heads // HEAD_DIM
    segments = segment_ids.astype(jnp.int32)

    n1, q, k, v, o, ab, gain_one, mine, theirs, full_a = stream(
        lambda *refs: attention_kernel(masks_a, len(pieces_a), heads, *refs),
        [
            ((length, depth), BF),
            ((length, heads), BF),
            ((length, heads), BF),
            ((length, heads), BF),
            ((length, heads), BF),
            ((repeat, length, length), BF),
            ((8, depth), F32),
            ((half, depth), BF),
            ((half, depth), BF),
            ((depth, wide_a), BF),
        ],
        [where, tokens, segments.reshape(length, 1), segments, table, *pieces_a],
        [pltpu.VMEM((6, depth, heads), BF), pltpu.VMEM((repeat, length, heads), BF)],
        near=(7, 8),
        here=range(1, 5 + len(pieces_a)),
    )
    terms = reduce_finish(reduce_start(mine, gate(theirs, early) if early else theirs, later))
    middle, n2, z, du, dv2, gain_two, mine, theirs, wd = stream(
        lambda *refs: feed_kernel(masks_b, len(pieces_b), hidden, *refs),
        [
            ((length, depth), F32),
            ((length, depth), BF),
            ((length, hidden), BF),
            ((length, hidden), BF),
            ((length, hidden), BF),
            ((8, depth), F32),
            ((half, depth), BF),
            ((half, depth), BF),
            ((depth, hidden), BF),
        ],
        [where, tokens, cotangent, *terms, *pieces_b],
        [pltpu.VMEM((depth, wide_b), BF), pltpu.VMEM((2, depth, hidden), BF)],
        near=(1, 2, 3, 4, 6, 7, 8),
        here=range(1, 7 + len(pieces_b)),
    )
    chip = reduce_start(mine, theirs)
    feed_outs = grad_outs(depth, 3 * hidden)
    out_mine, out_theirs, *grad_feed = stream(
        lambda *refs: feed_grad_kernel(hidden, *refs),
        [((half, depth), BF), ((half, depth), BF)] + feed_outs,
        [where, n2, du, dv2, cotangent, z, wd],
        [pltpu.VMEM((depth, 3 * hidden), BF)],
        deps=[chip],
        near=range(2 + len(feed_outs)),
        far=(4,),
        here=(1, 2, 3, 5, 6),
    )
    weights, keys, queries = stream(
        lambda *refs: ahead_kernel(heads, *refs),
        [((4, depth, heads), BF), ((repeat, length, 512), BF), ((repeat, length, 512), BF)],
        [where, full_a, q, k],
        deps=[chip, out_mine],
        near=(0, 1, 2),
        far=(1, 2, 3),
        vmem=16,
    )
    terms = reduce_finish(chip, [out_mine, keys])
    feed_pieces, feed_got, _unused = scatter_start(where, grad_feed)
    out_chip = reduce_start(out_mine, out_theirs, terms[1:2])
    out_got = swap(out_chip, "tensor", 2)
    small = ((8, 128), F32)
    whole = ((length, depth), F32)
    width = 4 * heads
    attn_outs = grad_outs(depth, width)
    dh, mine, theirs, *grad_attn = stream(
        lambda *refs: back_kernel(heads, *refs),
        [((length, depth), F32), ((half, depth), BF), ((half, depth), BF)] + attn_outs,
        [where, *terms, middle, cotangent, gain_two, weights, keys, queries, v, o, ab, n1, table],
        [
            pltpu.VMEM((depth, width), BF),
            pltpu.VMEM((length, depth), BF),
            pltpu.VMEM((length, heads), BF),
            pltpu.VMEM((length, 512), F32),
            pltpu.VMEM((length, heads), F32),
            pltpu.VMEM((3, length, heads), BF),
        ],
        near=range(1, 3 + len(attn_outs)),
        here=range(1, 16),
        vmem=28,
        cost=1,
    )
    chip = reduce_start(mine, gate(theirs, feed_got), [out_got])
    attn_pieces, _unused, _unused = scatter_start(where, grad_attn, feed_pieces[1:])
    out_chip, out_got = gate(out_chip, feed_pieces[-1:]), gate(out_got, feed_pieces[-1:])
    out_terms = [out_chip, out_got, swap(out_chip, "tensor", 1), swap(out_got, "tensor", 1)]
    output, sign = stream(
        output_kernel, [whole, small], [where, middle, *out_terms], near=(1,), here=range(1, 6), vmem=10
    )
    signs = [sign]
    terms = reduce_finish(chip, feed_pieces[1:])
    grad_tokens, sign = stream(
        input_grad_kernel, [whole, small], [where, tokens, dh, gain_one, *terms], near=(1,), here=range(1, 8), vmem=10
    )
    signs.append(sign)

    gain_sum_two = gain_call([0, hidden], 1, w_in, gains, feed_pieces)
    (leaf_in, leaf_down), sign = step_call(
        [feed_pieces],
        [(False, [(0, 0, hidden), (0, hidden, hidden)]), (True, [(0, 2 * hidden, hidden)])],
        [(w_in, first_in, second_in), (w_down, first_down, second_down)],
    )
    gain_sum_one = gain_call([0, heads, 2 * heads], 0, w_qkv, gains, attn_pieces, signs + [sign])
    share_gains = sum_small(jnp.concatenate([gain_sum_one[0:1], gain_sum_two[0:1]], axis=0))
    (leaf_qkv, leaf_out), _unused = step_call(
        [attn_pieces],
        [(False, [(0, 0, heads), (0, heads, heads), (0, 2 * heads, heads)]), (True, [(0, 3 * heads, heads)])],
        [(w_qkv, first_qkv, second_qkv), (w_out, first_out, second_out)],
    )
    n_gains, m_gains, s_gains = adamw(gains, share_gains, first_gains, second_gains, 0.0)
    by_kind = list(zip(leaf_qkv, leaf_out, leaf_in, leaf_down, (share_gains, n_gains, m_gains, s_gains)))
    return (output, grad_tokens, *by_kind[0], *by_kind[1], *by_kind[2], *by_kind[3])


def solution(mesh):
    placed = (
        P("dp", None),
        P("dp", None),
        P("dp", None),
        P(None, "dp", "tensor"),
        P("tensor", "dp"),
        P(None, "dp", "tensor"),
        P("tensor", "dp"),
        P(None, "dp"),
        P(None, "dp", "tensor"),
        P("tensor", "dp"),
        P(None, "dp", "tensor"),
        P("tensor", "dp"),
        P(None, "dp"),
        P(None, "dp", "tensor"),
        P("tensor", "dp"),
        P(None, "dp", "tensor"),
        P("tensor", "dp"),
        P(None, "dp"),
    )
    return jax.shard_map(
        local,
        mesh=mesh,
        in_specs=placed,
        out_specs=(
            P("dp", None),
            P("dp", None),
            P(None, "dp", "tensor"),
            P("tensor", "dp"),
            P(None, "dp", "tensor"),
            P("tensor", "dp"),
            P(None, "dp"),
            P(None, "dp", "tensor"),
            P("tensor", "dp"),
            P(None, "dp", "tensor"),
            P("tensor", "dp"),
            P(None, "dp"),
            P(None, "dp", "tensor"),
            P("tensor", "dp"),
            P(None, "dp", "tensor"),
            P("tensor", "dp"),
            P(None, "dp"),
            P(None, "dp", "tensor"),
            P("tensor", "dp"),
            P(None, "dp", "tensor"),
            P("tensor", "dp"),
            P(None, "dp"),
        ),
        check_vma=False,
    )
```
